32 devices in a mesh: ctx: 16 (over z, y, x), fsdp: 2 (over core).
Axes of the slice: x: 2, y: 2, z: 4, core: 2. Of those that a mesh axis runs over, the one named last changes fastest.
Arguments:
- block_input: bfloat16 [2, 16, 2, 64, 1024], P('fsdp', 'ctx'), may hold values from -6 to 6
- w_qkv: bfloat16 [1024, 3072], P('fsdp'), may hold values from -0.1875 to 0.1875
- w_out: bfloat16 [1024, 1024], P('fsdp'), may hold values from -3 to 3
- w_fc: bfloat16 [1024, 4096], P('fsdp'), may hold values from -0.1875 to 0.1875
- w_proj: bfloat16 [4096, 1024], P('fsdp'), may hold values from -0.09375 to 0.09375
- ln1_gain: bfloat16 [1024], P('fsdp'), may hold values from 0.099609375 to 1.8984375
- ln1_bias: bfloat16 [1024], P('fsdp'), may hold values from -4 to 4
- ln2_gain: bfloat16 [1024], P('fsdp'), may hold values from 0.099609375 to 1.8984375
- ln2_bias: bfloat16 [1024], P('fsdp'), may hold values from -4 to 4
- bias_q: bfloat16 [1024], P('fsdp'), may hold values from -4 to 4
- bias_v: bfloat16 [1024], P('fsdp'), may hold values from -0.75 to 0.75
- bias_out: bfloat16 [1024], P('fsdp'), may hold values from -4 to 4
- bias_fc: bfloat16 [4096], P('fsdp'), may hold values from -4 to 4
- bias_proj: bfloat16 [1024], P('fsdp'), may hold values from -4 to 4
- cotangent: bfloat16 [2, 16, 2, 64, 1024], P('fsdp', 'ctx'), may hold values from -6 to 6
Outputs:
- block_output: bfloat16 [2, 16, 2, 64, 1024], P('fsdp', 'ctx')
- grad_input: float32 [2, 16, 2, 64, 1024], P('fsdp', 'ctx')
- grad_w_qkv: float32 [1024, 3072], P(('ctx', 'fsdp'))
- grad_w_out: float32 [1024, 1024], P(('ctx', 'fsdp'))
- grad_w_fc: float32 [1024, 4096], P(('ctx', 'fsdp'))
- grad_w_proj: float32 [4096, 1024], P(('ctx', 'fsdp'))
- grad_ln1_gain: float32 [1024], P(('ctx', 'fsdp'))
- grad_ln1_bias: float32 [1024], P(('ctx', 'fsdp'))
- grad_ln2_gain: float32 [1024], P(('ctx', 'fsdp'))
- grad_ln2_bias: float32 [1024], P(('ctx', 'fsdp'))
- grad_bias_q: float32 [1024], P(('ctx', 'fsdp'))
- grad_bias_v: float32 [1024], P(('ctx', 'fsdp'))
- grad_bias_out: float32 [1024], P(('ctx', 'fsdp'))
- grad_bias_fc: float32 [4096], P(('ctx', 'fsdp'))
- grad_bias_proj: float32 [1024], P(('ctx', 'fsdp'))
The draws below stay inside these ranges and needn't reach their ends.
All inputs are finite; a program needn't handle non-finite values.
Results may differ from the reference program's by a relative error of at most 0.012.
The reference program's roundings to bfloat16 on the way count: a program that leaves them out, or rounds other values in their place, can miss the bound.
Values may be sent and summed in bfloat16 or wider, within the bound.
A program may use at most 384 MiB of HBM per device.

```python
import jax
import jax.numpy as jnp
from jax import lax

D = 1024
HEADS = 16
HEAD = 64
FF = 4096
BLK = 64
SEQS = 2
N_CTX = 16


def with_spikes(entries, key, source, target, blocks, factor):
    def block_of(position):
        return (jnp.arange(entries.shape[position]) // (entries.shape[position] // blocks)).reshape((-1,) + (1,) * (entries.ndim - 1 - position))

    near = jax.random.permutation(key, blocks)[block_of(target)]
    other_side = (block_of(target) + blocks // 2) % blocks
    return jnp.where((block_of(source) == near) | (block_of(source) == other_side), factor * entries, entries)


def steps_of(rng, extent, shards, smallest, largest):
    level, own = 1.0, jax.random.fold_in(rng, 6)
    for axis_at, blocks in shards:
        steps = jnp.exp(jax.random.uniform(jax.random.fold_in(own, axis_at), (blocks,), jnp.float32, smallest / len(shards), largest / len(shards)))
        level = level * jnp.repeat(steps, extent[axis_at] // blocks).reshape([-1 if axis == axis_at else 1 for axis in range(len(extent))])
    return level


def normal_values(rng, shape, scale, reach, cuts=(), dtype=jnp.bfloat16):
    factor_of = steps_of(rng, shape, cuts, -0.22, 0.18) if cuts else 1.0
    array = jax.random.normal(rng, shape, jnp.float32) * scale * factor_of
    return jnp.minimum(jnp.maximum(array, -reach), reach).astype(dtype)


def gaussian_with(own_key, dims, scale, bound, shards, heavy, held_as=jnp.bfloat16):
    entries = scale * jax.random.normal(own_key, dims, jnp.float32)
    if shards:
        entries = entries * steps_of(own_key, dims, shards, -0.22, 0.18)
    return jnp.clip(with_spikes(entries, jax.random.fold_in(own_key, 3), *heavy), -bound, bound).astype(held_as)


def setup_inputs(seed: int = 0) -> dict:
    key_list = jax.random.split(jax.random.key(seed), 16)
    block_input = normal_values(key_list[0], (SEQS, N_CTX, 2, BLK, D), 1.0, 6.0, ((0, 2), (1, 16)))
    w_qkv = normal_values(key_list[1], (D, 3 * D), D ** -0.5, 0.1875, ((0, 2),))
    w_out = normal_values(key_list[2], (D, D), (max(D // 256, 2)) ** -0.5, 3.0, ((0, 2),))
    w_fc = normal_values(key_list[3], (D, FF), D ** -0.5, 0.1875, ((0, 2),))
    w_proj = normal_values(key_list[4], (FF, D), FF ** -0.5, 0.09375, ((0, 2),))
    ln1_gain = jnp.clip(1.0 + 0.18 * jax.random.normal(key_list[5], (D,), jnp.float32), 0.099609375, 1.8984375).astype(jnp.bfloat16)
    ln1_bias = normal_values(key_list[6], (D,), 0.3, 4.0, ((0, 2),))
    ln2_gain = jnp.clip(1.0 + 0.18 * jax.random.normal(key_list[7], (D,), jnp.float32), 0.099609375, 1.8984375).astype(jnp.bfloat16)
    ln2_bias = normal_values(key_list[8], (D,), 0.3, 4.0, ((0, 2),))
    bias_q = normal_values(key_list[9], (D,), 0.3, 4.0, ((0, 2),))
    bias_v = normal_values(key_list[10], (D,), 0.05, 0.75, ((0, 2),))
    bias_out = normal_values(key_list[11], (D,), 0.3, 4.0, ((0, 2),))
    bias_fc = normal_values(key_list[12], (FF,), 0.3, 4.0, ((0, 2),))
    bias_proj = normal_values(key_list[13], (D,), 0.3, 4.0, ((0, 2),))
    cotangent = gaussian_with(key_list[14], (SEQS, N_CTX, 2, BLK, D), 1.0, 6.0, ((0, 2), (1, 16)), (1, 4, 16, 2.0))
    return dict(block_input=block_input, w_qkv=w_qkv, w_out=w_out, w_fc=w_fc, w_proj=w_proj, ln1_gain=ln1_gain, ln1_bias=ln1_bias, ln2_gain=ln2_gain, ln2_bias=ln2_bias, bias_q=bias_q, bias_v=bias_v, bias_out=bias_out, bias_fc=bias_fc, bias_proj=bias_proj, cotangent=cotangent)


@jax.custom_vjp
def low(v):
    return lax.optimization_barrier(v.astype(jnp.bfloat16)).astype(jnp.float32)

@jax.custom_vjp
def low_back(v):
    return v

def low_keep(v):
    return (low(v), None)

def low_pass(kept, grad):
    return (grad,)

def back_keep(v):
    return (v, None)

def back_low(kept, grad):
    return (low(grad),)
low.defvjp(low_keep, low_pass)
low_back.defvjp(back_keep, back_low)

def product(left, right):
    return jnp.dot(left, right, preferred_element_type=jnp.float32, precision=lax.Precision.HIGHEST)

def layer_norm(values, gain, shift):
    average = lax.optimization_barrier(jnp.mean(values, -1, keepdims=True))
    centered = values - average
    variance = lax.optimization_barrier(jnp.mean(centered * centered, -1, keepdims=True))
    return centered * lax.rsqrt(variance + 1e-05) * gain + shift

def natural_order(dealt):
    early_part = dealt[:, :, 0]
    late_part = dealt[:, ::-1, 1]
    joined = jnp.concatenate([early_part, late_part], axis=1)
    return joined.reshape(joined.shape[0], -1, joined.shape[-1])

def dealt_order(natural):
    blocks = natural.reshape(natural.shape[0], 2 * N_CTX, BLK, natural.shape[-1])
    early_part = blocks[:, :N_CTX]
    late_part = blocks[:, N_CTX:][:, ::-1]
    return jnp.stack([early_part, late_part], axis=2)

def attend(triple):
    queries, keys, values = triple
    seq_length = queries.shape[0]
    scores = low_back(jnp.einsum('qhd,khd->hqk', queries, keys, precision=lax.Precision.HIGHEST) * HEAD ** (-0.5))
    positions = jnp.arange(seq_length)
    causal = positions[None, :] <= positions[:, None]
    scores = jnp.where(causal[None], scores, -1e+30)
    probs = low(jax.nn.softmax(scores, axis=-1))
    mixed = jnp.einsum('hqk,khd->qhd', probs, values, precision=lax.Precision.HIGHEST)
    return mixed.reshape(seq_length, -1)

def forward(inputs, w_qkv, w_out, w_fc, w_proj, ln1_gain, ln1_bias, ln2_gain, ln2_bias, bias_q, bias_v, bias_out, bias_fc, bias_proj):
    seq_total, seq_length, width = inputs.shape
    rows = inputs.reshape(-1, width)
    normed_one = low(layer_norm(rows, ln1_gain, ln1_bias))
    bias_all = jnp.concatenate([bias_q, jnp.zeros_like(bias_q), bias_v])
    projected = low(low_back(product(normed_one, w_qkv) + bias_all))
    split = projected.reshape(seq_total, seq_length, 3, HEADS, HEAD)
    attended = lax.map(jax.checkpoint(attend), (split[:, :, 0], split[:, :, 1], split[:, :, 2]))
    attended = low(low_back(attended.reshape(-1, width)))
    residual = rows + low_back(product(attended, w_out) + bias_out)
    normed_two = low(layer_norm(residual, ln2_gain, ln2_bias))
    hidden = low_back(product(normed_two, w_fc) + bias_fc)
    activated = low(jax.nn.gelu(hidden, approximate=True))
    result = residual + low_back(product(activated, w_proj) + bias_proj)
    return result.reshape(seq_total, seq_length, width)

def reference(block_input, w_qkv, w_out, w_fc, w_proj, ln1_gain, ln1_bias, ln2_gain, ln2_bias, bias_q, bias_v, bias_out, bias_fc, bias_proj, cotangent):
    params = [weight.astype(jnp.float32) for weight in (w_qkv, w_out, w_fc, w_proj, ln1_gain, ln1_bias, ln2_gain, ln2_bias, bias_q, bias_v, bias_out, bias_fc, bias_proj)]
    inputs = natural_order(block_input.astype(jnp.float32))
    result, pullback = jax.vjp(forward, inputs, *params)
    grads = pullback(natural_order(cotangent.astype(jnp.float32)))
    return (dealt_order(result).astype(jnp.bfloat16), dealt_order(grads[0]), grads[1], grads[2], grads[3], grads[4], grads[5], grads[6], grads[7], grads[8], grads[9], grads[10], grads[11], grads[12], grads[13])
```

```python
from functools import partial

import jax
import jax.numpy as jnp
from jax import lax
from jax.sharding import PartitionSpec as P

HEADS = 16


def norm_parts(values):
    average = jnp.mean(values, -1, keepdims=True)
    centered = values - average
    variance = jnp.mean(centered * centered, -1, keepdims=True)
    inverse = lax.rsqrt(variance + 1e-05)
    return (centered * inverse, inverse)


def norm_grads(upstream, normalized, inverse, gain):
    scaled = upstream * gain
    inner_part = (
        scaled
        - jnp.mean(scaled, -1, keepdims=True)
        - normalized * jnp.mean(scaled * normalized, -1, keepdims=True)
    )
    return (inverse * inner_part, jnp.sum(upstream * normalized, 0), jnp.sum(upstream, 0))


def rows_product(left, right):
    return lax.dot_general(
        left, right, (((0,), (0,)), ((), ())), preferred_element_type=jnp.float32
    )


def right_transposed(left, weight):
    return lax.dot_general(
        left, weight, (((1,), (1,)), ((), ())), preferred_element_type=jnp.float32
    )


def split_heads(matrix):
    return matrix.reshape(matrix.shape[0], HEADS, -1)


def head_scores(queries, keys, allowed, scaling):
    scores = (
        jnp.einsum(
            "qhd,khd->hqk",
            split_heads(queries),
            split_heads(keys),
            preferred_element_type=jnp.float32,
        )
        * scaling
    )
    return jnp.where(allowed[None], scores, -1e30)


def general_layer(
    block_input,
    w_qkv,
    w_out,
    w_fc,
    w_proj,
    ln1_gain,
    ln1_bias,
    ln2_gain,
    ln2_bias,
    bias_q,
    bias_v,
    bias_out,
    bias_fc,
    bias_proj,
    cotangent,
):
    seq_count = block_input.shape[0]
    blk_rows = block_input.shape[3]
    width = block_input.shape[4]
    seq_rows = 2 * blk_rows
    row_count = seq_count * seq_rows
    groups = lax.axis_size("ctx")
    member = lax.axis_index("ctx")
    head_size = width // HEADS
    scaling = head_size ** (-0.5)
    full_rows = groups * seq_rows
    gathered = (
        lax.all_gather(w_qkv, "fsdp", axis=0, tiled=True),
        lax.all_gather(w_out, "fsdp", axis=0, tiled=True),
        lax.all_gather(w_fc, "fsdp", axis=0, tiled=True),
        lax.all_gather(w_proj, "fsdp", axis=0, tiled=True),
        lax.all_gather(ln1_gain, "fsdp", axis=0, tiled=True),
        lax.all_gather(ln1_bias, "fsdp", axis=0, tiled=True),
        lax.all_gather(ln2_gain, "fsdp", axis=0, tiled=True),
        lax.all_gather(ln2_bias, "fsdp", axis=0, tiled=True),
        lax.all_gather(bias_q, "fsdp", axis=0, tiled=True),
        lax.all_gather(bias_v, "fsdp", axis=0, tiled=True),
        lax.all_gather(bias_out, "fsdp", axis=0, tiled=True),
        lax.all_gather(bias_fc, "fsdp", axis=0, tiled=True),
        lax.all_gather(bias_proj, "fsdp", axis=0, tiled=True),
    )
    weight_qkv, weight_out, weight_fc, weight_proj = (
        gathered[0],
        gathered[1],
        gathered[2],
        gathered[3],
    )
    vectors = [piece.astype(jnp.float32) for piece in gathered[4:]]
    (
        gain_one,
        shift_one,
        gain_two,
        shift_two,
        query_bias,
        value_bias,
        out_bias,
        fc_bias,
        proj_bias,
    ) = vectors
    local_index = jnp.arange(seq_rows)
    own_block = jnp.where(local_index // blk_rows == 0, member, 2 * groups - 1 - member)
    own_pos = own_block * blk_rows + local_index % blk_rows
    every_index = jnp.arange(full_rows)
    every_owner = every_index // seq_rows
    every_block = jnp.where(
        every_index // blk_rows % 2 == 0, every_owner, 2 * groups - 1 - every_owner
    )
    every_pos = every_block * blk_rows + every_index % blk_rows
    allowed = every_pos[None, :] <= own_pos[:, None]
    inputs = block_input.reshape(row_count, width).astype(jnp.float32)
    normal_one, inverse_one = norm_parts(inputs)
    normed_one = (normal_one * gain_one + shift_one).astype(jnp.bfloat16)
    bias_all = jnp.concatenate([query_bias, jnp.zeros_like(query_bias), value_bias])
    projected = (
        jnp.dot(normed_one, weight_qkv, preferred_element_type=jnp.float32) + bias_all
    ).astype(jnp.bfloat16)
    queries = projected[:, :width]
    keys = projected[:, width : 2 * width]
    values = projected[:, 2 * width :]
    key_all = lax.all_gather(keys, "ctx", axis=0, tiled=True)
    value_all = lax.all_gather(values, "ctx", axis=0, tiled=True)
    scores = head_scores(queries, key_all, allowed, scaling)
    row_top = jnp.max(scores, -1, keepdims=True)
    log_sum = row_top + jnp.log(jnp.sum(jnp.exp(scores - row_top), -1, keepdims=True))
    probs_low = jnp.exp(scores - log_sum).astype(jnp.bfloat16)
    mixed = jnp.einsum(
        "hqk,khd->qhd", probs_low, split_heads(value_all), preferred_element_type=jnp.float32
    )
    mixed_rows = mixed.reshape(seq_rows, width)
    attended = mixed_rows.astype(jnp.bfloat16)
    residual = inputs + jnp.dot(attended, weight_out, preferred_element_type=jnp.float32) + out_bias
    normal_two, inverse_two = norm_parts(residual)
    normed_two = (normal_two * gain_two + shift_two).astype(jnp.bfloat16)
    hidden = jnp.dot(normed_two, weight_fc, preferred_element_type=jnp.float32) + fc_bias
    activated, gelu_pullback = jax.vjp(partial(jax.nn.gelu, approximate=True), hidden)
    activated_low = activated.astype(jnp.bfloat16)
    result = (
        residual
        + jnp.dot(activated_low, weight_proj, preferred_element_type=jnp.float32)
        + proj_bias
    )
    block_output = result.astype(jnp.bfloat16).reshape(block_input.shape)
    weight_qkv, weight_out, weight_fc, weight_proj, gain_low_one, gain_low_two = (
        lax.all_gather(w_qkv, "fsdp", axis=0, tiled=True),
        lax.all_gather(w_out, "fsdp", axis=0, tiled=True),
        lax.all_gather(w_fc, "fsdp", axis=0, tiled=True),
        lax.all_gather(w_proj, "fsdp", axis=0, tiled=True),
        lax.all_gather(ln1_gain, "fsdp", axis=0, tiled=True),
        lax.all_gather(ln2_gain, "fsdp", axis=0, tiled=True),
    )
    gain_one = gain_low_one.astype(jnp.float32)
    gain_two = gain_low_two.astype(jnp.float32)
    out_grad_low = cotangent.reshape(row_count, width)
    upstream = out_grad_low.astype(jnp.float32)
    grad_proj = rows_product(activated_low, out_grad_low)
    grad_proj_bias = jnp.sum(upstream, 0)
    hidden_grad = gelu_pullback(right_transposed(out_grad_low, weight_proj))[0].astype(jnp.bfloat16)
    grad_fc = rows_product(normed_two, hidden_grad)
    grad_fc_bias = jnp.sum(hidden_grad.astype(jnp.float32), 0)
    residual_part, grad_gain_two, grad_shift_two = norm_grads(
        right_transposed(hidden_grad, weight_fc), normal_two, inverse_two, gain_two
    )
    residual_grad = upstream + residual_part
    branch_grad = residual_grad.astype(jnp.bfloat16)
    grad_out = rows_product(attended, branch_grad)
    grad_out_bias = jnp.sum(branch_grad.astype(jnp.float32), 0)
    attended_grad = right_transposed(branch_grad, weight_out).astype(jnp.bfloat16)
    key_all = lax.all_gather(keys, "ctx", axis=0, tiled=True)
    value_all = lax.all_gather(values, "ctx", axis=0, tiled=True)
    scores = head_scores(queries, key_all, allowed, scaling)
    probs = jnp.exp(scores - log_sum)
    prob_grad = jnp.einsum(
        "qhd,khd->hqk",
        split_heads(attended_grad),
        split_heads(value_all),
        preferred_element_type=jnp.float32,
    )
    inner_sum = jnp.sum(probs * prob_grad, -1, keepdims=True)
    score_grad = (probs * (prob_grad - inner_sum)).astype(jnp.bfloat16)
    query_part = (
        jnp.einsum(
            "hqk,khd->qhd", score_grad, split_heads(key_all), preferred_element_type=jnp.float32
        )
        * scaling
    )
    query_grads = query_part.reshape(seq_rows, width)
    probs_low = probs.astype(jnp.bfloat16)
    query_heads = split_heads(queries)
    grad_heads = split_heads(attended_grad)

    def key_terms(
        start,
        count,
        score_grad=score_grad,
        probs_low=probs_low,
        query_heads=query_heads,
        grad_heads=grad_heads,
    ):
        key_part = (
            jnp.einsum("hqk,qhd->khd", score_grad, query_heads, preferred_element_type=jnp.float32)
            * scaling
        )
        value_part = jnp.einsum(
            "hqk,qhd->khd", probs_low, grad_heads, preferred_element_type=jnp.float32
        )
        return jnp.concatenate(
            [key_part.reshape(count, width), value_part.reshape(count, width)], 1
        )

    own_terms = lax.psum_scatter(
        key_terms(jnp.int32(0), lax.axis_size("ctx") * seq_rows),
        "ctx",
        scatter_dimension=0,
        tiled=True,
    )
    key_grads = own_terms[:, :width]
    value_grads = own_terms[:, width:]
    qkv_grad = jnp.concatenate([query_grads, key_grads, value_grads], 1).astype(jnp.bfloat16)
    grad_qkv = rows_product(normed_one, qkv_grad)
    qkv_sums = jnp.sum(qkv_grad.astype(jnp.float32), 0)
    grad_query_bias = qkv_sums[:width]
    grad_value_bias = qkv_sums[2 * width :]
    input_part, grad_gain_one, grad_shift_one = norm_grads(
        right_transposed(qkv_grad, weight_qkv), normal_one, inverse_one, gain_one
    )
    input_grad = (residual_grad + input_part).reshape(block_input.shape)
    sharded = (
        lax.psum_scatter(grad_qkv, ("ctx", "fsdp"), scatter_dimension=0, tiled=True),
        lax.psum_scatter(grad_out, ("ctx", "fsdp"), scatter_dimension=0, tiled=True),
        lax.psum_scatter(grad_fc, ("ctx", "fsdp"), scatter_dimension=0, tiled=True),
        lax.psum_scatter(grad_proj, ("ctx", "fsdp"), scatter_dimension=0, tiled=True),
        lax.psum_scatter(grad_gain_one, ("ctx", "fsdp"), scatter_dimension=0, tiled=True),
        lax.psum_scatter(grad_shift_one, ("ctx", "fsdp"), scatter_dimension=0, tiled=True),
        lax.psum_scatter(grad_gain_two, ("ctx", "fsdp"), scatter_dimension=0, tiled=True),
        lax.psum_scatter(grad_shift_two, ("ctx", "fsdp"), scatter_dimension=0, tiled=True),
        lax.psum_scatter(grad_query_bias, ("ctx", "fsdp"), scatter_dimension=0, tiled=True),
        lax.psum_scatter(grad_value_bias, ("ctx", "fsdp"), scatter_dimension=0, tiled=True),
        lax.psum_scatter(grad_out_bias, ("ctx", "fsdp"), scatter_dimension=0, tiled=True),
        lax.psum_scatter(grad_fc_bias, ("ctx", "fsdp"), scatter_dimension=0, tiled=True),
        lax.psum_scatter(grad_proj_bias, ("ctx", "fsdp"), scatter_dimension=0, tiled=True),
    )
    return (
        block_output,
        input_grad,
        sharded[0],
        sharded[1],
        sharded[2],
        sharded[3],
        sharded[4],
        sharded[5],
        sharded[6],
        sharded[7],
        sharded[8],
        sharded[9],
        sharded[10],
        sharded[11],
        sharded[12],
    )


def headwise_layer(
    block_input,
    w_qkv,
    w_out,
    w_fc,
    w_proj,
    ln1_gain,
    ln1_bias,
    ln2_gain,
    ln2_bias,
    bias_q,
    bias_v,
    bias_out,
    bias_fc,
    bias_proj,
    cotangent,
):
    blk_rows = block_input.shape[3]
    width = block_input.shape[4]
    seq_rows = 2 * blk_rows
    groups = lax.axis_size("ctx")
    shards = groups * lax.axis_size("fsdp")
    head_size = width // HEADS
    scaling = head_size ** (-0.5)
    full_rows = groups * seq_rows
    weight_qkv, weight_out, weight_fc, weight_proj = (
        lax.all_gather(w, "fsdp", axis=0, tiled=True) for w in (w_qkv, w_out, w_fc, w_proj)
    )
    small = (ln1_gain, ln1_bias, ln2_gain, ln2_bias, bias_q, bias_v, bias_out, bias_fc, bias_proj)
    joined = lax.all_gather(jnp.concatenate(small), "fsdp", axis=0).astype(jnp.float32)
    vectors, at = [], 0
    for piece in small:
        vectors.append(joined[:, at : at + piece.shape[0]].reshape(-1))
        at += piece.shape[0]
    (
        gain_one,
        shift_one,
        gain_two,
        shift_two,
        query_bias,
        value_bias,
        out_bias,
        fc_bias,
        proj_bias,
    ) = vectors
    every_index = jnp.arange(full_rows)
    every_owner = every_index // seq_rows
    every_block = jnp.where(
        every_index // blk_rows % 2 == 0, every_owner, 2 * groups - 1 - every_owner
    )
    every_pos = every_block * blk_rows + every_index % blk_rows
    allowed = every_pos[None, :] <= every_pos[:, None]

    def to_heads(rows):
        parts = rows.reshape(seq_rows, -1, HEADS, head_size)
        moved = lax.all_to_all(parts, "ctx", split_axis=2, concat_axis=0, tiled=True)
        return moved[:, :, 0]

    def to_tokens(rows):
        parts = rows.reshape(full_rows, -1, 1, head_size)
        moved = lax.all_to_all(parts, "ctx", split_axis=0, concat_axis=2, tiled=True)
        return moved.reshape(seq_rows, -1)

    inputs = block_input.reshape(seq_rows, width).astype(jnp.float32)
    normal_one, inverse_one = norm_parts(inputs)
    normed_one = (normal_one * gain_one + shift_one).astype(jnp.bfloat16)
    bias_all = jnp.concatenate([query_bias, jnp.zeros_like(query_bias), value_bias])
    projected = (
        jnp.dot(normed_one, weight_qkv, preferred_element_type=jnp.float32) + bias_all
    ).astype(jnp.bfloat16)
    triple = to_heads(projected)
    queries, keys, values = triple[:, 0], triple[:, 1], triple[:, 2]
    scores = jnp.where(allowed, right_transposed(queries, keys) * scaling, -1e30)
    row_top = jnp.max(scores, -1, keepdims=True)
    log_sum = row_top + jnp.log(jnp.sum(jnp.exp(scores - row_top), -1, keepdims=True))
    probs = jnp.exp(scores - log_sum)
    probs_low = probs.astype(jnp.bfloat16)
    mixed = jnp.dot(probs_low, values, preferred_element_type=jnp.float32)
    attended = to_tokens(mixed.astype(jnp.bfloat16))
    residual = inputs + jnp.dot(attended, weight_out, preferred_element_type=jnp.float32) + out_bias
    normal_two, inverse_two = norm_parts(residual)
    normed_two = (normal_two * gain_two + shift_two).astype(jnp.bfloat16)
    hidden = jnp.dot(normed_two, weight_fc, preferred_element_type=jnp.float32) + fc_bias
    activated, gelu_pullback = jax.vjp(partial(jax.nn.gelu, approximate=True), hidden)
    activated_low = activated.astype(jnp.bfloat16)
    result = (
        residual
        + jnp.dot(activated_low, weight_proj, preferred_element_type=jnp.float32)
        + proj_bias
    )
    block_output = result.astype(jnp.bfloat16).reshape(block_input.shape)
    out_grad_low = cotangent.reshape(seq_rows, width)
    upstream = out_grad_low.astype(jnp.float32)
    grad_proj = rows_product(activated_low, out_grad_low)
    grad_proj_bias = jnp.sum(upstream, 0)
    hidden_grad = gelu_pullback(right_transposed(out_grad_low, weight_proj))[0].astype(jnp.bfloat16)
    grad_fc = rows_product(normed_two, hidden_grad)
    grad_fc_bias = jnp.sum(hidden_grad.astype(jnp.float32), 0)
    residual_part, grad_gain_two, grad_shift_two = norm_grads(
        right_transposed(hidden_grad, weight_fc), normal_two, inverse_two, gain_two
    )
    residual_grad = upstream + residual_part
    branch_grad = residual_grad.astype(jnp.bfloat16)
    grad_out = rows_product(attended, branch_grad)
    grad_out_bias = jnp.sum(branch_grad.astype(jnp.float32), 0)
    attended_grad = to_heads(right_transposed(branch_grad, weight_out).astype(jnp.bfloat16))[:, 0]
    prob_grad = right_transposed(attended_grad, values)
    inner_sum = jnp.sum(probs * prob_grad, -1, keepdims=True)
    score_grad = (probs * (prob_grad - inner_sum)).astype(jnp.bfloat16)
    query_part = jnp.dot(score_grad, keys, preferred_element_type=jnp.float32) * scaling
    key_part = rows_product(score_grad, queries) * scaling
    value_part = rows_product(probs_low, attended_grad)
    qkv_grad = to_tokens(
        jnp.stack([query_part, key_part, value_part], 1).astype(jnp.bfloat16)
    )
    grad_qkv = rows_product(normed_one, qkv_grad)
    qkv_sums = jnp.sum(qkv_grad.astype(jnp.float32), 0)
    grad_query_bias = qkv_sums[:width]
    grad_value_bias = qkv_sums[2 * width :]
    input_part, grad_gain_one, grad_shift_one = norm_grads(
        right_transposed(qkv_grad, weight_qkv), normal_one, inverse_one, gain_one
    )
    input_grad = (residual_grad + input_part).reshape(block_input.shape)
    big = tuple(
        lax.psum_scatter(
            part.astype(jnp.bfloat16), ("ctx", "fsdp"), scatter_dimension=0, tiled=True
        ).astype(jnp.float32)
        for part in (grad_qkv, grad_out, grad_fc, grad_proj)
    )
    sums = (
        grad_gain_one,
        grad_shift_one,
        grad_gain_two,
        grad_shift_two,
        grad_query_bias,
        grad_value_bias,
        grad_out_bias,
        grad_fc_bias,
        grad_proj_bias,
    )
    packed = lax.psum_scatter(
        jnp.concatenate([part.reshape(shards, -1) for part in sums], 1),
        ("ctx", "fsdp"),
        scatter_dimension=0,
        tiled=True,
    )[0]
    lows, at = [], 0
    for part in sums:
        count = part.shape[0] // shards
        lows.append(packed[at : at + count])
        at += count
    return (block_output, input_grad, *big, *lows)


def on_device(*arrays):
    if lax.axis_size("ctx") == HEADS and arrays[0].shape[0] == 1:
        return headwise_layer(*arrays)
    return general_layer(*arrays)


def solution(mesh):
    placed = (
        P("fsdp", "ctx", None, None, None),
        P("fsdp", None),
        P("fsdp", None),
        P("fsdp", None),
        P("fsdp", None),
        P("fsdp"),
        P("fsdp"),
        P("fsdp"),
        P("fsdp"),
        P("fsdp"),
        P("fsdp"),
        P("fsdp"),
        P("fsdp"),
        P("fsdp"),
        P("fsdp", "ctx", None, None, None),
    )
    return jax.shard_map(
        on_device,
        mesh=mesh,
        in_specs=placed,
        out_specs=(
            P("fsdp", "ctx", None, None, None),
            P("fsdp", "ctx", None, None, None),
            P(("ctx", "fsdp"), None),
            P(("ctx", "fsdp"), None),
            P(("ctx", "fsdp"), None),
            P(("ctx", "fsdp"), None),
            P(("ctx", "fsdp")),
            P(("ctx", "fsdp")),
            P(("ctx", "fsdp")),
            P(("ctx", "fsdp")),
            P(("ctx", "fsdp")),
            P(("ctx", "fsdp")),
            P(("ctx", "fsdp")),
            P(("ctx", "fsdp")),
            P(("ctx", "fsdp")),
        ),
        check_vma=False,
    )
```

```python
from functools import partial
from types import SimpleNamespace

import jax
import jax.numpy as jnp
from jax import lax
from jax.experimental import pallas as pl
from jax.experimental.pallas import tpu as pltpu
from jax.sharding import PartitionSpec as P

HEADS = 16
VMEM_BYTES = 62 * 2**20


def norm_parts(values):
    average = jnp.mean(values, -1, keepdims=True)
    centered = values - average
    variance = jnp.mean(centered * centered, -1, keepdims=True)
    inverse = lax.rsqrt(variance + 1e-05)
    return (centered * inverse, inverse)


def norm_grads(upstream, normalized, inverse, gain):
    scaled = upstream * gain
    inner_part = (
        scaled
        - jnp.mean(scaled, -1, keepdims=True)
        - normalized * jnp.mean(scaled * normalized, -1, keepdims=True)
    )
    return (inverse * inner_part, jnp.sum(upstream * normalized, 0), jnp.sum(upstream, 0))


def rows_product(left, right):
    return lax.dot_general(
        left, right, (((0,), (0,)), ((), ())), preferred_element_type=jnp.float32
    )


def right_transposed(left, weight):
    return lax.dot_general(
        left, weight, (((1,), (1,)), ((), ())), preferred_element_type=jnp.float32
    )


def split_heads(matrix):
    return matrix.reshape(matrix.shape[0], HEADS, -1)


def head_scores(queries, keys, allowed, scaling):
    scores = (
        jnp.einsum(
            "qhd,khd->hqk",
            split_heads(queries),
            split_heads(keys),
            preferred_element_type=jnp.float32,
        )
        * scaling
    )
    return jnp.where(allowed[None], scores, -1e30)


def general_layer(
    block_input,
    w_qkv,
    w_out,
    w_fc,
    w_proj,
    ln1_gain,
    ln1_bias,
    ln2_gain,
    ln2_bias,
    bias_q,
    bias_v,
    bias_out,
    bias_fc,
    bias_proj,
    cotangent,
):
    seq_count = block_input.shape[0]
    blk_rows = block_input.shape[3]
    width = block_input.shape[4]
    seq_rows = 2 * blk_rows
    row_count = seq_count * seq_rows
    groups = lax.axis_size("ctx")
    member = lax.axis_index("ctx")
    head_size = width // HEADS
    scaling = head_size ** (-0.5)
    full_rows = groups * seq_rows
    gathered = (
        lax.all_gather(w_qkv, "fsdp", axis=0, tiled=True),
        lax.all_gather(w_out, "fsdp", axis=0, tiled=True),
        lax.all_gather(w_fc, "fsdp", axis=0, tiled=True),
        lax.all_gather(w_proj, "fsdp", axis=0, tiled=True),
        lax.all_gather(ln1_gain, "fsdp", axis=0, tiled=True),
        lax.all_gather(ln1_bias, "fsdp", axis=0, tiled=True),
        lax.all_gather(ln2_gain, "fsdp", axis=0, tiled=True),
        lax.all_gather(ln2_bias, "fsdp", axis=0, tiled=True),
        lax.all_gather(bias_q, "fsdp", axis=0, tiled=True),
        lax.all_gather(bias_v, "fsdp", axis=0, tiled=True),
        lax.all_gather(bias_out, "fsdp", axis=0, tiled=True),
        lax.all_gather(bias_fc, "fsdp", axis=0, tiled=True),
        lax.all_gather(bias_proj, "fsdp", axis=0, tiled=True),
    )
    weight_qkv, weight_out, weight_fc, weight_proj = (
        gathered[0],
        gathered[1],
        gathered[2],
        gathered[3],
    )
    vectors = [piece.astype(jnp.float32) for piece in gathered[4:]]
    (
        gain_one,
        shift_one,
        gain_two,
        shift_two,
        query_bias,
        value_bias,
        out_bias,
        fc_bias,
        proj_bias,
    ) = vectors
    local_index = jnp.arange(seq_rows)
    own_block = jnp.where(local_index // blk_rows == 0, member, 2 * groups - 1 - member)
    own_pos = own_block * blk_rows + local_index % blk_rows
    every_index = jnp.arange(full_rows)
    every_owner = every_index // seq_rows
    every_block = jnp.where(
        every_index // blk_rows % 2 == 0, every_owner, 2 * groups - 1 - every_owner
    )
    every_pos = every_block * blk_rows + every_index % blk_rows
    allowed = every_pos[None, :] <= own_pos[:, None]
    inputs = block_input.reshape(row_count, width).astype(jnp.float32)
    normal_one, inverse_one = norm_parts(inputs)
    normed_one = (normal_one * gain_one + shift_one).astype(jnp.bfloat16)
    bias_all = jnp.concatenate([query_bias, jnp.zeros_like(query_bias), value_bias])
    projected = (
        jnp.dot(normed_one, weight_qkv, preferred_element_type=jnp.float32) + bias_all
    ).astype(jnp.bfloat16)
    queries = projected[:, :width]
    keys = projected[:, width : 2 * width]
    values = projected[:, 2 * width :]
    key_all = lax.all_gather(keys, "ctx", axis=0, tiled=True)
    value_all = lax.all_gather(values, "ctx", axis=0, tiled=True)
    scores = head_scores(queries, key_all, allowed, scaling)
    row_top = jnp.max(scores, -1, keepdims=True)
    log_sum = row_top + jnp.log(jnp.sum(jnp.exp(scores - row_top), -1, keepdims=True))
    probs_low = jnp.exp(scores - log_sum).astype(jnp.bfloat16)
    mixed = jnp.einsum(
        "hqk,khd->qhd", probs_low, split_heads(value_all), preferred_element_type=jnp.float32
    )
    mixed_rows = mixed.reshape(seq_rows, width)
    attended = mixed_rows.astype(jnp.bfloat16)
    residual = inputs + jnp.dot(attended, weight_out, preferred_element_type=jnp.float32) + out_bias
    normal_two, inverse_two = norm_parts(residual)
    normed_two = (normal_two * gain_two + shift_two).astype(jnp.bfloat16)
    hidden = jnp.dot(normed_two, weight_fc, preferred_element_type=jnp.float32) + fc_bias
    activated, gelu_pullback = jax.vjp(partial(jax.nn.gelu, approximate=True), hidden)
    activated_low = activated.astype(jnp.bfloat16)
    result = (
        residual
        + jnp.dot(activated_low, weight_proj, preferred_element_type=jnp.float32)
        + proj_bias
    )
    block_output = result.astype(jnp.bfloat16).reshape(block_input.shape)
    weight_qkv, weight_out, weight_fc, weight_proj, gain_low_one, gain_low_two = (
        lax.all_gather(w_qkv, "fsdp", axis=0, tiled=True),
        lax.all_gather(w_out, "fsdp", axis=0, tiled=True),
        lax.all_gather(w_fc, "fsdp", axis=0, tiled=True),
        lax.all_gather(w_proj, "fsdp", axis=0, tiled=True),
        lax.all_gather(ln1_gain, "fsdp", axis=0, tiled=True),
        lax.all_gather(ln2_gain, "fsdp", axis=0, tiled=True),
    )
    gain_one = gain_low_one.astype(jnp.float32)
    gain_two = gain_low_two.astype(jnp.float32)
    out_grad_low = cotangent.reshape(row_count, width)
    upstream = out_grad_low.astype(jnp.float32)
    grad_proj = rows_product(activated_low, out_grad_low)
    grad_proj_bias = jnp.sum(upstream, 0)
    hidden_grad = gelu_pullback(right_transposed(out_grad_low, weight_proj))[0].astype(jnp.bfloat16)
    grad_fc = rows_product(normed_two, hidden_grad)
    grad_fc_bias = jnp.sum(hidden_grad.astype(jnp.float32), 0)
    residual_part, grad_gain_two, grad_shift_two = norm_grads(
        right_transposed(hidden_grad, weight_fc), normal_two, inverse_two, gain_two
    )
    residual_grad = upstream + residual_part
    branch_grad = residual_grad.astype(jnp.bfloat16)
    grad_out = rows_product(attended, branch_grad)
    grad_out_bias = jnp.sum(branch_grad.astype(jnp.float32), 0)
    attended_grad = right_transposed(branch_grad, weight_out).astype(jnp.bfloat16)
    key_all = lax.all_gather(keys, "ctx", axis=0, tiled=True)
    value_all = lax.all_gather(values, "ctx", axis=0, tiled=True)
    scores = head_scores(queries, key_all, allowed, scaling)
    probs = jnp.exp(scores - log_sum)
    prob_grad = jnp.einsum(
        "qhd,khd->hqk",
        split_heads(attended_grad),
        split_heads(value_all),
        preferred_element_type=jnp.float32,
    )
    inner_sum = jnp.sum(probs * prob_grad, -1, keepdims=True)
    score_grad = (probs * (prob_grad - inner_sum)).astype(jnp.bfloat16)
    query_part = (
        jnp.einsum(
            "hqk,khd->qhd", score_grad, split_heads(key_all), preferred_element_type=jnp.float32
        )
        * scaling
    )
    query_grads = query_part.reshape(seq_rows, width)
    probs_low = probs.astype(jnp.bfloat16)
    query_heads = split_heads(queries)
    grad_heads = split_heads(attended_grad)

    def key_terms(
        start,
        count,
        score_grad=score_grad,
        probs_low=probs_low,
        query_heads=query_heads,
        grad_heads=grad_heads,
    ):
        key_part = (
            jnp.einsum("hqk,qhd->khd", score_grad, query_heads, preferred_element_type=jnp.float32)
            * scaling
        )
        value_part = jnp.einsum(
            "hqk,qhd->khd", probs_low, grad_heads, preferred_element_type=jnp.float32
        )
        return jnp.concatenate(
            [key_part.reshape(count, width), value_part.reshape(count, width)], 1
        )

    own_terms = lax.psum_scatter(
        key_terms(jnp.int32(0), lax.axis_size("ctx") * seq_rows),
        "ctx",
        scatter_dimension=0,
        tiled=True,
    )
    key_grads = own_terms[:, :width]
    value_grads = own_terms[:, width:]
    qkv_grad = jnp.concatenate([query_grads, key_grads, value_grads], 1).astype(jnp.bfloat16)
    grad_qkv = rows_product(normed_one, qkv_grad)
    qkv_sums = jnp.sum(qkv_grad.astype(jnp.float32), 0)
    grad_query_bias = qkv_sums[:width]
    grad_value_bias = qkv_sums[2 * width :]
    input_part, grad_gain_one, grad_shift_one = norm_grads(
        right_transposed(qkv_grad, weight_qkv), normal_one, inverse_one, gain_one
    )
    input_grad = (residual_grad + input_part).reshape(block_input.shape)
    sharded = (
        lax.psum_scatter(grad_qkv, ("ctx", "fsdp"), scatter_dimension=0, tiled=True),
        lax.psum_scatter(grad_out, ("ctx", "fsdp"), scatter_dimension=0, tiled=True),
        lax.psum_scatter(grad_fc, ("ctx", "fsdp"), scatter_dimension=0, tiled=True),
        lax.psum_scatter(grad_proj, ("ctx", "fsdp"), scatter_dimension=0, tiled=True),
        lax.psum_scatter(grad_gain_one, ("ctx", "fsdp"), scatter_dimension=0, tiled=True),
        lax.psum_scatter(grad_shift_one, ("ctx", "fsdp"), scatter_dimension=0, tiled=True),
        lax.psum_scatter(grad_gain_two, ("ctx", "fsdp"), scatter_dimension=0, tiled=True),
        lax.psum_scatter(grad_shift_two, ("ctx", "fsdp"), scatter_dimension=0, tiled=True),
        lax.psum_scatter(grad_query_bias, ("ctx", "fsdp"), scatter_dimension=0, tiled=True),
        lax.psum_scatter(grad_value_bias, ("ctx", "fsdp"), scatter_dimension=0, tiled=True),
        lax.psum_scatter(grad_out_bias, ("ctx", "fsdp"), scatter_dimension=0, tiled=True),
        lax.psum_scatter(grad_fc_bias, ("ctx", "fsdp"), scatter_dimension=0, tiled=True),
        lax.psum_scatter(grad_proj_bias, ("ctx", "fsdp"), scatter_dimension=0, tiled=True),
    )
    return (
        block_output,
        input_grad,
        sharded[0],
        sharded[1],
        sharded[2],
        sharded[3],
        sharded[4],
        sharded[5],
        sharded[6],
        sharded[7],
        sharded[8],
        sharded[9],
        sharded[10],
        sharded[11],
        sharded[12],
    )


MESH = pl.DeviceIdType.MESH
BF16, F32 = jnp.bfloat16, jnp.float32
PLANE = 4
NEG = -1e30


def remote(src, dst, sent, received, device):
    return pltpu.make_async_remote_copy(
        src_ref=src,
        dst_ref=dst,
        send_sem=sent,
        recv_sem=received,
        device_id=device,
        device_id_type=MESH,
    )


def dot(left, right):
    return jnp.dot(left, right, preferred_element_type=F32)


def low_lanes(rows):
    return lax.broadcasted_iota(jnp.int32, (rows, 128), 1) < 64


def swap(block):
    return pltpu.roll(block, 64, 1)


def pack_pair(pair):
    half = pair.shape[0] // 2
    low = low_lanes(half)
    top, bottom = pair[:half], pair[half:]
    return jnp.where(low, top, swap(bottom)), jnp.where(low, swap(top), bottom)


def unpack_pair(even, odd):
    low = low_lanes(even.shape[0])
    return jnp.concatenate(
        [jnp.where(low, even, swap(odd)), jnp.where(low, swap(even), odd)], 0
    )


def part(index, size):
    return pl.ds(pl.multiple_of(index * size, size), size)


def layer_shapes(rows, width, ff, groups):
    members = 2 * PLANE
    layers = groups // PLANE
    tokens = members * rows
    half = rows // 2
    keys = groups * half
    share = width // members
    return dict(
        w_qkv=((width, 3 * width), BF16),
        w_out=((width, width), BF16),
        w_fc=((width, ff), BF16),
        w_proj=((ff, width), BF16),
        vec=((2, 16, width // 2), F32),
        row=((8, width), F32),
        cot_all=((members, rows, width), BF16),
        n1=((rows, width), BF16),
        n1_t=((width, tokens), BF16),
        stage=((groups, 3, half, 128), BF16),
        qkv=((3, keys, 128), BF16),
        kv_roll=((2, keys, 128), BF16),
        q_low=((2, keys, 128), BF16),
        g_low=((2, keys, 128), BF16),
        q_t=((128, keys), BF16),
        g_t=((128, keys), BF16),
        stat=((2, keys, 128), F32),
        mixed=((keys, 128), F32),
        o_out=((groups, half, 128), BF16),
        o_in=((groups, half, 128), BF16),
        att=((rows, width), BF16),
        att_t=((layers, members, width // members // layers, rows), BF16),
        att_all=((layers, width // members // layers, tokens), BF16),
        res=((rows, width), F32),
        n2=((rows, width), BF16),
        n2_t=((width, tokens), BF16),
        act_t=((ff, rows), BF16),
        act_all=((layers, ff // members // layers, tokens), BF16),
        hg_out=((members, rows, ff // members), BF16),
        hg_all=((members, rows, ff // members), BF16),
        acc_o=((rows, width), F32),
        acc_d=((rows, width), F32),
        res_grad=((rows, width), F32),
        bg_all=((members, rows, width), BF16),
        g_out=((groups, half, 128), BF16),
        g_in=((keys, 128), BF16),
        dk_t=((128, keys), F32),
        dv_t=((128, keys), F32),
        back=((groups, 3, half, 128), BF16),
        qg=((rows, 3 * width), BF16),
        qg_out=((members, rows, 3 * share), BF16),
        qg_all=((members, rows, 3 * share), BF16),
        fc_own=((width // layers, ff // members), F32),
        qkv_own=((width // layers, 3 * share), F32),
        fc_x=((members, width // layers // members, ff // members), BF16),
        fc_y=((members, width // layers // members, ff // members), BF16),
        qkv_x=((members, width // layers // members, 3 * share), BF16),
        qkv_y=((members, width // layers // members, 3 * share), BF16),
        sums=((16, width), F32),
        sums_in=((7, 16, width), F32),
    )


SEMAPHORES = dict(
    local=4,
    w_sent=15,
    w_got=15,
    v_sent=1,
    v_got=1,
    qkv_sent=16,
    qkv_got=16,
    o_sent=16,
    o_got=16,
    g_sent=16,
    g_got=16,
    back_sent=16,
    back_got=16,
    cot_sent=8,
    cot_got=8,
    n1_sent=8,
    n1_got=8,
    n2_sent=8,
    n2_got=8,
    bg_sent=8,
    bg_got=8,
    act_sent=8,
    act_got=8,
    hg_sent=8,
    hg_got=8,
    att_sent=8,
    att_got=8,
    qg_sent=8,
    qg_got=8,
    rp_sent=4,
    rp_got=4,
    rf_sent=4,
    rf_got=4,
    ro_sent=4,
    ro_got=4,
    rq_sent=4,
    rq_got=4,
    fx_sent=8,
    fx_got=8,
    qx_sent=8,
    qx_got=8,
    s_sent=8,
    s_got=8,
)


def layer_kernel(names, *refs):
    x_ref, cot_ref, vec_ref, wq_hbm, wo_hbm, wf_hbm, wp_hbm = refs[:7]
    y_ref, gx_ref, gqkv_ref, gout_ref, gfc_ref, gproj_ref, gvec_ref = refs[7:14]
    s = SimpleNamespace(**dict(zip(names, refs[14:])))
    rows, width = x_ref.shape
    ff = s.w_fc.shape[1]
    half = rows // 2
    groups = s.stage.shape[0]
    members = 2 * PLANE
    layers = groups // PLANE
    tokens = members * rows
    keys = groups * half
    chunk = ff // members
    share = width // members
    scaling = float(width // HEADS) ** (-0.5)
    factor = scaling * 1.4426950408889634
    me = lax.axis_index("ctx")
    core = lax.axis_index("fsdp")
    other = 1 - core
    layer, place = me // PLANE, me % PLANE
    member = place * 2 + core
    twin = (me, other)

    barrier = pltpu.get_barrier_semaphore()
    for step in range(1, groups):
        pl.semaphore_signal(
            barrier, inc=1, device_id=((me + step) % groups, core), device_id_type=MESH
        )
    for step in range(PLANE):
        pl.semaphore_signal(
            barrier,
            inc=1,
            device_id=(layer * PLANE + (place + step) % PLANE, other),
            device_id_type=MESH,
        )
    pl.semaphore_wait(barrier, groups - 1 + PLANE)

    def at_member(index):
        return (layer * PLANE + index // 2, index % 2)

    def top_rows(ref, source):
        count = source.shape[0]
        return ref.at[pl.ds(pl.multiple_of(core * count, count), count)]

    def peer_rows(ref, source):
        count = source.shape[0]
        return ref.at[pl.ds(pl.multiple_of(other * count, count), count)]

    first = 2 * (1 - layer // 2)

    def order(step):
        return (step + first) % 4

    pltpu.make_async_copy(wq_hbm, top_rows(s.w_qkv, wq_hbm), s.local.at[0]).start()

    def qkv_piece(step, third):
        columns = part(third * 4 + order(step), 256)
        index = step * 3 + third
        return remote(
            wq_hbm.at[:, columns],
            top_rows(s.w_qkv, wq_hbm).at[:, columns],
            s.w_sent.at[index],
            s.w_got.at[index],
            twin,
        )

    vec_copy = remote(vec_ref, s.vec.at[core], s.v_sent.at[0], s.v_got.at[0], twin)
    vec_copy.start()
    for step in range(4):
        for third in range(3):
            qkv_piece(step, third).start()
    big = ((wo_hbm, s.w_out), (wf_hbm, s.w_fc), (wp_hbm, s.w_proj))

    def big_piece(index):
        source, target = big[index]
        return remote(
            source, top_rows(target, source), s.w_sent.at[12 + index], s.w_got.at[12 + index], twin
        )

    def big_local(index):
        source, target = big[index]
        return pltpu.make_async_copy(source, top_rows(target, source), s.local.at[1 + index])

    for index in range(3):
        big_piece(index).start()
        big_local(index).start()

    def gather_copy(where, sent, got, index, slot, device):
        return remote(where(slot), where(slot), sent.at[index], got.at[slot], device)

    def gather_start(where, sent, got):
        for step in range(1, PLANE):
            peer = layer * PLANE + (place + step) % PLANE
            gather_copy(where, sent, got, step, member, (peer, core)).start()
        gather_copy(where, sent, got, 0, member, twin).start()

    def gather_forward(where, sent, got):
        for step in range(1, PLANE):
            slot = ((place + step) % PLANE) * 2 + core
            gather_copy(where, sent, got, 0, slot, twin).wait_recv()
            gather_copy(where, sent, got, PLANE - 1 + step, slot, twin).start()

    def gather_finish(where, sent, got):
        for step in range(PLANE):
            slot = ((place + step) % PLANE) * 2 + other
            gather_copy(where, sent, got, 0, slot, twin).wait_recv()

    def gather_drain(where, sent, got):
        for index in range(2 * PLANE - 1):
            gather_copy(where, sent, got, index, member, twin).wait_send()

    def cot_at(slot):
        return s.cot_all.at[slot]

    def bg_at(slot):
        return s.bg_all.at[slot]

    def n1_at(slot):
        return s.n1_t.at[:, part(slot, rows)]

    def n2_at(slot):
        return s.n2_t.at[:, part(slot, rows)]

    def deal_copy(source, target, sent, got, index, slot):
        return remote(source(index), target(slot), sent.at[index], got.at[slot], at_member(index))

    def deal_one(source, target, sent, got, index):
        @pl.when(index == member)
        def _():
            pltpu.make_async_copy(source(index), target(member), got.at[member]).start()

        @pl.when(index != member)
        def _():
            deal_copy(source, target, sent, got, index, member).start()

    def deal_start(source, target, sent, got):
        for step in range(members):
            if step == 0:
                pltpu.make_async_copy(source(member), target(member), got.at[member]).start()
            else:
                deal_copy(source, target, sent, got, (member + step) % members, member).start()

    def deal_wait(source, target, sent, got):
        for slot in range(members):
            pltpu.make_async_copy(source(0), target(slot), got.at[slot]).wait()

    def deal_drain(source, target, sent, got):
        for step in range(1, members):
            deal_copy(source, target, sent, got, (member + step) % members, member).wait_send()

    def swap_one(source, target, sent, got, index):
        @pl.when(index == me)
        def _():
            pltpu.make_async_copy(source(index), target(me), got.at[me]).start()

        @pl.when(index != me)
        def _():
            remote(source(index), target(me), sent.at[index], got.at[me], (index, core)).start()

    def swap_wait(source, target, sent, got):
        for slot in range(groups):
            pltpu.make_async_copy(source(0), target(slot), got.at[slot]).wait()

    def swap_drain(source, target, sent, got):
        for step in range(1, groups):
            peer = (me + step) % groups
            remote(source(peer), target(me), sent.at[peer], got.at[me], (peer, core)).wait_send()

    qkv_move = (
        lambda h: s.stage.at[h],
        lambda i: s.qkv.at[:, part(i, half)],
        s.qkv_sent,
        s.qkv_got,
    )
    o_move = (lambda h: s.o_out.at[h], lambda h: s.o_in.at[h], s.o_sent, s.o_got)
    g_move = (lambda h: s.g_out.at[h], lambda i: s.g_in.at[part(i, half)], s.g_sent, s.g_got)
    back_move = (lambda h: s.stage.at[h], lambda h: s.back.at[h], s.back_sent, s.back_got)

    def vec_row(index):
        return jnp.concatenate([s.vec[0, index : index + 1, :], s.vec[1, index : index + 1, :]], 1)

    s.cot_all[member] = cot_ref[...]
    gather_start(cot_at, s.cot_sent, s.cot_got)
    s.vec[core] = vec_ref[...]
    remote(vec_ref, s.vec.at[other], s.v_sent.at[0], s.v_got.at[0], twin).wait_recv()
    s.row[0:1, :] = vec_row(4)
    s.row[1:2, :] = vec_row(5)
    inputs = x_ref[...].astype(F32)
    normal, _ = norm_parts(inputs)
    normed = (normal * vec_row(0) + vec_row(1)).astype(BF16)
    s.n1[...] = normed
    s.n1_t[:, part(member, rows)] = normed.astype(F32).T.astype(BF16)
    gather_start(n1_at, s.n1_sent, s.n1_got)
    pltpu.make_async_copy(wq_hbm, top_rows(s.w_qkv, wq_hbm), s.local.at[0]).wait()

    for step in range(4):
        four = order(step)
        for third in range(3):
            index = step * 3 + third
            columns = part(third * 4 + four, 256)
            remote(
                wq_hbm.at[:, columns],
                peer_rows(s.w_qkv, wq_hbm).at[:, columns],
                s.w_sent.at[index],
                s.w_got.at[index],
                twin,
            ).wait_recv()
            product = dot(s.n1[...], s.w_qkv[:, columns])
            if third == 0:
                product = product + s.row[0:1, part(four, 256)]
            if third == 2:
                product = product + s.row[1:2, part(four, 256)]
            for pair in range(2):
                even, odd = pack_pair(product[:, pair * 128 : pair * 128 + 128])
                s.stage[four * 4 + 2 * pair, third] = even.astype(BF16)
                s.stage[four * 4 + 2 * pair + 1, third] = odd.astype(BF16)
        for head in range(4):
            swap_one(*qkv_move, four * 4 + head)

    swap_wait(*qkv_move)
    low_all = low_lanes(keys)
    query = s.qkv[0].astype(F32)
    s.q_low[0] = jnp.where(low_all, query, 0.0).astype(BF16)
    s.q_low[1] = jnp.where(low_all, swap(query), 0.0).astype(BF16)
    s.q_t[...] = query.T.astype(BF16)
    s.kv_roll[0] = swap(s.qkv[1].astype(F32)).astype(BF16)
    s.kv_roll[1] = swap(s.qkv[2].astype(F32)).astype(BF16)

    tile = 256
    per_tile = tile // half
    low_tile = low_lanes(tile)
    row_at = lax.broadcasted_iota(jnp.int32, (tile, tile), 0)
    col_at = lax.broadcasted_iota(jnp.int32, (tile, tile), 1)

    def late(index):
        return index + (per_tile - 1 - 2 * (index // half)) * half

    masks = (col_at <= row_at, late(col_at) <= late(row_at))

    def key_block(region, at):
        return s.qkv[1, at, :] if region == 0 else s.kv_roll[0, at, :]

    def value_block(region, at):
        return s.qkv[2, at, :] if region == 0 else s.kv_roll[1, at, :]

    def first_tile(queries, region, at):
        scores = jnp.where(
            masks[region], right_transposed(queries, key_block(region, at)), NEG
        )
        top = jnp.max(scores, 1, keepdims=True)
        probs = jnp.exp2((scores - top) * factor)
        total = jnp.sum(probs, 1, keepdims=True)
        return top, total, dot(probs.astype(BF16), value_block(region, at))

    def next_tile(queries, region, at, carry):
        top, total, mix = carry
        scores = right_transposed(queries, key_block(region, at))
        higher = jnp.maximum(top, jnp.max(scores, 1, keepdims=True))
        probs = jnp.exp2((scores - higher) * factor)
        shrink = jnp.exp2((top - higher) * factor)
        total = total * shrink + jnp.sum(probs, 1, keepdims=True)
        return higher, total, mix * shrink + dot(probs.astype(BF16), value_block(region, at))

    n_tiles = keys // tile

    def attend(index, _):
        at = part(index, tile)
        early_q, late_q = s.q_low[0, at, :], s.q_low[1, at, :]
        one = lax.fori_loop(
            0,
            index,
            lambda k, carry: next_tile(early_q, 0, part(k, tile), carry),
            first_tile(early_q, 0, at),
        )
        two = lax.fori_loop(
            index + 1,
            n_tiles,
            lambda k, carry: next_tile(late_q, 1, part(k, tile), carry),
            first_tile(late_q, 1, at),
        )
        two = lax.fori_loop(
            0, n_tiles // 2, lambda k, carry: next_tile(late_q, 0, part(k, 2 * tile), carry), two
        )
        s.stat[0, at, 0:1] = one[0] * factor + jnp.log2(one[1])
        s.stat[1, at, 0:1] = two[0] * factor + jnp.log2(two[1])
        out = jnp.where(low_tile, one[2] / one[1], swap(two[2] / two[1]))
        s.mixed[at, :] = out
        s.o_out[part(index, per_tile)] = out.astype(BF16).reshape(per_tile, half, 128)
        for block in range(per_tile):
            swap_one(*o_move, index * per_tile + block)
        return 0

    lax.fori_loop(0, n_tiles, attend, 0)

    gather_forward(cot_at, s.cot_sent, s.cot_got)
    gather_forward(n1_at, s.n1_sent, s.n1_got)
    for index in range(3):
        source, target = big[index]
        remote(
            source,
            peer_rows(target, source),
            s.w_sent.at[12 + index],
            s.w_got.at[12 + index],
            twin,
        ).wait_recv()
        big_local(index).wait()
    swap_wait(*o_move)
    for pair in range(HEADS // 2):
        columns = slice(pair * 128, pair * 128 + 128)
        s.att[:, columns] = unpack_pair(
            s.o_in[2 * pair].astype(F32), s.o_in[2 * pair + 1].astype(F32)
        ).astype(BF16)
    turned = s.att[...].astype(F32).T.astype(BF16)
    s.att_t[...] = turned.reshape(s.att_t.shape)
    att_move = (
        lambda g: s.att_t.at[:, g],
        lambda g: s.att_all.at[:, :, part(g, rows)],
        s.att_sent,
        s.att_got,
    )
    deal_start(*att_move)

    def project(index, _):
        at = part(index, 256)
        s.acc_d[:, at] = dot(s.att[...], s.w_out[:, at])
        return 0

    lax.fori_loop(0, width // 256, project, 0)
    s.res[...] = x_ref[...].astype(F32) + s.acc_d[...] + vec_row(6)
    normal, _ = norm_parts(s.res[...])
    normed = (normal * vec_row(2) + vec_row(3)).astype(BF16)
    s.n2[...] = normed
    s.n2_t[:, part(member, rows)] = normed.astype(F32).T.astype(BF16)
    gather_start(n2_at, s.n2_sent, s.n2_got)

    s.acc_o[...] = jnp.zeros_like(s.acc_o)
    s.acc_d[...] = jnp.zeros_like(s.acc_d)
    s.sums[...] = jnp.zeros_like(s.sums)
    hg_move = (lambda g: s.hg_out.at[g], lambda g: s.hg_all.at[g], s.hg_sent, s.hg_got)
    curve = 0.7978845608028654

    def feed(index, _):
        at = part(index, chunk)
        bias = s.vec.at[index // 4][pl.ds(8 + index % 4, 1), :]
        hidden = dot(s.n2[...], s.w_fc[:, at]) + bias
        upstream = right_transposed(cot_ref[...], s.w_proj[at, :])
        square = hidden * hidden
        bend = jnp.tanh(curve * hidden * (1.0 + 0.044715 * square))
        rise = 0.5 * (1.0 + bend)
        active = (hidden * rise).astype(BF16)
        slope = rise + 0.5 * hidden * (1.0 - bend * bend) * (
            curve * (1.0 + 3.0 * 0.044715 * square)
        )
        grad = (upstream * slope).astype(BF16)
        s.act_t[at, :] = active.astype(F32).T.astype(BF16)
        s.hg_out[index] = grad
        deal_one(*hg_move, index)
        s.acc_o[...] += dot(active, s.w_proj[at, :])
        s.acc_d[...] += right_transposed(grad, s.w_fc[:, at])
        s.sums[pl.ds(8 + index // 2, 1), pl.ds(pl.multiple_of(index % 2 * chunk, chunk), chunk)] = (
            jnp.sum(grad.astype(F32), 0, keepdims=True)
        )
        return 0

    lax.fori_loop(0, members, feed, 0)
    act_view = s.act_t.reshape(layers, members, ff // members // layers, rows)
    act_move = (
        lambda g: act_view.at[:, g],
        lambda g: s.act_all.at[:, :, part(g, rows)],
        s.act_sent,
        s.act_got,
    )
    deal_start(*act_move)
    upstream = cot_ref[...].astype(F32)
    normal, inverse = norm_parts(s.res[...])
    step_grad, gain_grad, shift_grad = norm_grads(s.acc_d[...], normal, inverse, vec_row(2))
    s.sums[2:3, :] = gain_grad[None]
    s.sums[3:4, :] = shift_grad[None]
    s.sums[7:8, :] = jnp.sum(upstream, 0, keepdims=True)
    res_grad = upstream + step_grad
    s.res_grad[...] = res_grad
    branch = res_grad.astype(BF16)
    s.bg_all[member] = branch
    s.sums[6:7, :] = jnp.sum(branch.astype(F32), 0, keepdims=True)
    for step in range(4):
        four = order(step)
        product = right_transposed(s.bg_all[member], s.w_out[part(four, 256), :])
        for pair in range(2):
            even, odd = pack_pair(product[:, pair * 128 : pair * 128 + 128])
            s.g_out[four * 4 + 2 * pair] = even.astype(BF16)
            s.g_out[four * 4 + 2 * pair + 1] = odd.astype(BF16)
        for head in range(4):
            swap_one(*g_move, four * 4 + head)
    gather_start(bg_at, s.bg_sent, s.bg_got)
    y_ref[...] = (s.res[...] + s.acc_o[...] + vec_row(7)).astype(BF16)
    swap_drain(*qkv_move)

    swap_wait(*g_move)
    upstream = s.g_in[...].astype(F32)
    s.g_low[0] = jnp.where(low_all, upstream, 0.0).astype(BF16)
    s.g_low[1] = jnp.where(low_all, swap(upstream), 0.0).astype(BF16)
    s.g_t[...] = upstream.T.astype(BF16)
    inner = upstream * s.mixed[...]
    s.stat[0, :, 1:2] = jnp.sum(jnp.where(low_all, inner, 0.0), 1, keepdims=True)
    s.stat[1, :, 1:2] = jnp.sum(jnp.where(low_all, 0.0, inner), 1, keepdims=True)
    s.dk_t[...] = jnp.zeros_like(s.dk_t)
    s.dv_t[...] = jnp.zeros_like(s.dv_t)

    def back_tile(side, region, at_q, at_k, masked, total):
        scores = right_transposed(s.q_low[side, at_q, :], key_block(region, at_k))
        probs = jnp.exp2(scores * factor - s.stat[side, at_q, 0:1])
        if masked:
            probs = jnp.where(masks[region], probs, 0.0)
        prob_grad = right_transposed(s.g_low[side, at_q, :], value_block(region, at_k))
        score_grad = (probs * (prob_grad - s.stat[side, at_q, 1:2])).astype(BF16)
        head = slice(side * 64, side * 64 + 64)
        into = slice(region * 64, region * 64 + 64)
        s.dk_t[into, at_k] += dot(s.q_t[head, at_q], score_grad)
        s.dv_t[into, at_k] += dot(s.g_t[head, at_q], probs.astype(BF16))
        more = dot(score_grad, key_block(region, at_k))
        return more if total is None else total + more

    def attend_back(index, _):
        at = part(index, tile)
        one = lax.fori_loop(
            0,
            index,
            lambda k, total: back_tile(0, 0, at, part(k, tile), False, total),
            back_tile(0, 0, at, at, True, None),
        )
        two = lax.fori_loop(
            index + 1,
            n_tiles,
            lambda k, total: back_tile(1, 1, at, part(k, tile), False, total),
            back_tile(1, 1, at, at, True, None),
        )
        two = lax.fori_loop(
            0,
            n_tiles // 2,
            lambda k, total: back_tile(1, 0, at, part(k, 2 * tile), False, total),
            two,
        )
        out = (jnp.where(low_tile, one, swap(two)) * scaling).astype(BF16)
        s.stage[part(index, per_tile), 0] = out.reshape(per_tile, half, 128)
        return 0

    lax.fori_loop(0, n_tiles, attend_back, 0)
    s.stage[:, 1] = (s.dk_t[...].T * scaling).astype(BF16).reshape(groups, half, 128)
    s.stage[:, 2] = s.dv_t[...].T.astype(BF16).reshape(groups, half, 128)
    for step in range(4):
        for head in range(4):
            swap_one(*back_move, order(step) * 4 + head)

    def spread_copy(buffer_out, buffer_in, sent, got, index, slot):
        return remote(
            buffer_out(index),
            buffer_in(slot),
            sent.at[index],
            got.at[slot],
            (index * PLANE + place, core),
        )

    def spread(move, product, own_ref):
        buffer_out, buffer_in, sent, got = move

        def each(index, _):
            value = product(index)
            buffer_out(index)[...] = value.astype(BF16)

            @pl.when(index == layer)
            def _():
                own_ref[...] = value

            @pl.when(index != layer)
            def _():
                spread_copy(*move, index, layer).start()

            return 0

        lax.fori_loop(0, layers, each, 0)

    def collect(move, own_ref):
        buffer_out, buffer_in, sent, got = move
        for step in range(1, layers):
            slot = (layer + step) % layers
            spread_copy(*move, slot, slot).wait_recv()
            own_ref[...] += buffer_in(slot)[...].astype(F32)

    def spread_drain(move):
        for step in range(1, layers):
            spread_copy(*move, (layer + step) % layers, layer).wait_send()

    proj_rows = ff // members // layers
    out_rows = share // layers
    fc_rows = width // layers

    def rows_of(ref, start, count, columns=slice(None)):
        return lambda i: ref.at[pl.ds(pl.multiple_of(start + i * count, count), count), columns]

    sum_proj = (
        rows_of(s.w_proj, 0, proj_rows),
        rows_of(s.w_proj, 512, proj_rows),
        s.rp_sent,
        s.rp_got,
    )
    sum_out = (
        rows_of(s.w_proj, 1024, out_rows),
        rows_of(s.w_proj, 1152, out_rows),
        s.ro_sent,
        s.ro_got,
    )
    sum_fc = (
        rows_of(s.w_fc, 0, fc_rows, pl.ds(0, chunk)),
        rows_of(s.w_fc, 0, fc_rows, pl.ds(chunk, chunk)),
        s.rf_sent,
        s.rf_got,
    )
    sum_qkv = (
        rows_of(s.w_fc, 0, fc_rows, pl.ds(2 * chunk, 3 * share)),
        rows_of(s.w_fc, 0, fc_rows, pl.ds(3 * chunk, 3 * share)),
        s.rq_sent,
        s.rq_got,
    )
    gather_forward(n2_at, s.n2_sent, s.n2_got)
    gather_forward(bg_at, s.bg_sent, s.bg_got)
    gather_finish(cot_at, s.cot_sent, s.cot_got)
    deal_wait(*act_move)
    spread(
        sum_proj,
        lambda i: dot(s.act_all[i], s.cot_all[...].reshape(tokens, width)),
        gproj_ref,
    )
    gather_finish(n2_at, s.n2_sent, s.n2_got)
    deal_wait(*hg_move)
    spread(
        sum_fc,
        lambda i: dot(s.n2_t[part(i, fc_rows), :], s.hg_all[...].reshape(tokens, chunk)),
        s.fc_own,
    )
    gather_finish(bg_at, s.bg_sent, s.bg_got)
    deal_wait(*att_move)
    spread(
        sum_out,
        lambda i: dot(s.att_all[i], s.bg_all[...].reshape(tokens, width)),
        gout_ref,
    )

    swap_wait(*back_move)
    for pair in range(HEADS // 2):
        for third in range(3):
            block = unpack_pair(
                s.back[2 * pair, third].astype(F32), s.back[2 * pair + 1, third].astype(F32)
            ).astype(BF16)
            s.qg_out[pair, :, third * 128 : third * 128 + 128] = block
            columns = slice(third * width + pair * 128, third * width + pair * 128 + 128)
            s.qg[:, columns] = block
    qg_move = (lambda g: s.qg_out.at[g], lambda g: s.qg_all.at[g], s.qg_sent, s.qg_got)
    deal_start(*qg_move)
    s.sums[4:5, :] = jnp.sum(s.qg[:, :width].astype(F32), 0, keepdims=True)
    s.sums[5:6, :] = jnp.sum(s.qg[:, 2 * width :].astype(F32), 0, keepdims=True)

    def project_back(index, _):
        s.acc_d[:, part(index, 256)] = right_transposed(s.qg[...], s.w_qkv[part(index, 256), :])
        return 0

    lax.fori_loop(0, width // 256, project_back, 0)
    normal, inverse = norm_parts(x_ref[...].astype(F32))
    step_grad, gain_grad, shift_grad = norm_grads(s.acc_d[...], normal, inverse, vec_row(0))
    s.sums[0:1, :] = gain_grad[None]
    s.sums[1:2, :] = shift_grad[None]
    gx_ref[...] = s.res_grad[...] + step_grad

    def sum_copy(index, slot, device):
        return remote(s.sums, s.sums_in.at[slot], s.s_sent.at[index], s.s_got.at[slot], device)

    sum_copy(0, 0, twin).start()

    gather_finish(n1_at, s.n1_sent, s.n1_got)
    deal_wait(*qg_move)
    spread(
        sum_qkv,
        lambda i: dot(s.n1_t[part(i, fc_rows), :], s.qg_all[...].reshape(tokens, 3 * share)),
        s.qkv_own,
    )
    sum_copy(0, 0, twin).wait()
    s.sums[...] += s.sums_in[0]
    for step in range(1, PLANE):
        sum_copy(step, step, (layer * PLANE + (place + step) % PLANE, core)).start()

    fx_move = (lambda g: s.fc_x.at[g], lambda g: s.fc_y.at[g], s.fx_sent, s.fx_got)
    qx_move = (lambda g: s.qkv_x.at[g], lambda g: s.qkv_y.at[g], s.qx_sent, s.qx_got)
    collect(sum_fc, s.fc_own)
    s.fc_x[...] = s.fc_own[...].astype(BF16).reshape(s.fc_x.shape)
    deal_start(*fx_move)
    for step in range(1, PLANE):
        sum_copy(step, step, twin).wait()
    s.sums[...] += s.sums_in[1] + s.sums_in[2] + s.sums_in[3]
    for step in range(1, layers):
        peer = ((layer + step) % layers) * PLANE + place
        sum_copy(3 + step, 3 + step, (peer, core)).start()
    collect(sum_proj, gproj_ref)
    collect(sum_out, gout_ref)
    collect(sum_qkv, s.qkv_own)
    s.qkv_x[...] = s.qkv_own[...].astype(BF16).reshape(s.qkv_x.shape)
    deal_start(*qx_move)
    for step in range(1, layers):
        sum_copy(3 + step, 3 + step, twin).wait()
    s.sums[...] += s.sums_in[4] + s.sums_in[5] + s.sums_in[6]
    owner = me * 2 + core
    gvec_ref[...] = jnp.zeros_like(gvec_ref)
    block = s.sums[0:8, part(owner // 4, 128)]
    gvec_ref[0:8, :] = pltpu.roll(block, (128 - (owner % 4) * 32) % 128, 1)
    block = s.sums[8:16, part(owner % 8, 128)]
    chosen = lax.broadcasted_iota(jnp.int32, block.shape, 0) == owner // 8
    gvec_ref[8:9, :] = jnp.sum(jnp.where(chosen, block, 0.0), 0, keepdims=True)
    deal_wait(*fx_move)
    for slot in range(members):
        gfc_ref[:, slot * chunk : slot * chunk + chunk] = s.fc_y[slot].astype(F32)
    deal_wait(*qx_move)
    for slot in range(members):
        for third in range(3):
            start = third * width + slot * 128
            gqkv_ref[:, start : start + 128] = s.qkv_y[
                slot, :, third * 128 : third * 128 + 128
            ].astype(F32)

    for step in range(4):
        for third in range(3):
            qkv_piece(step, third).wait_send()
    for index in range(3):
        big_piece(index).wait_send()
    vec_copy.wait_send()
    for move in (o_move, g_move, back_move):
        swap_drain(*move)
    for move in (att_move, hg_move, act_move, qg_move, fx_move, qx_move):
        deal_drain(*move)
    for where, sent, got in (
        (cot_at, s.cot_sent, s.cot_got),
        (n1_at, s.n1_sent, s.n1_got),
        (n2_at, s.n2_sent, s.n2_got),
        (bg_at, s.bg_sent, s.bg_got),
    ):
        gather_drain(where, sent, got)
    for move in (sum_proj, sum_fc, sum_out, sum_qkv):
        spread_drain(move)


def fused_layer(
    block_input,
    w_qkv,
    w_out,
    w_fc,
    w_proj,
    ln1_gain,
    ln1_bias,
    ln2_gain,
    ln2_bias,
    bias_q,
    bias_v,
    bias_out,
    bias_fc,
    bias_proj,
    cotangent,
):
    width = block_input.shape[4]
    rows = 2 * block_input.shape[3]
    ff = w_fc.shape[1]
    groups = lax.axis_size("ctx")
    shards = 2 * groups
    small = (ln1_gain, ln1_bias, ln2_gain, ln2_bias, bias_q, bias_v, bias_out, bias_proj, bias_fc)
    vectors = jnp.concatenate(small).astype(F32).reshape(-1, width // 2)
    vectors = jnp.pad(vectors, ((0, 16 - vectors.shape[0]), (0, 0)))
    shapes = layer_shapes(rows, width, ff, groups)
    names = tuple(shapes) + tuple(SEMAPHORES)
    scratch = [pltpu.VMEM(shape, kind) for shape, kind in shapes.values()]
    scratch += [pltpu.SemaphoreType.DMA((count,)) for count in SEMAPHORES.values()]
    in_vmem = pl.BlockSpec(memory_space=pltpu.VMEM)
    in_hbm = pl.BlockSpec(memory_space=pl.ANY)
    outs = pl.pallas_call(
        partial(layer_kernel, names),
        out_shape=(
            jax.ShapeDtypeStruct((rows, width), BF16),
            jax.ShapeDtypeStruct((rows, width), F32),
            jax.ShapeDtypeStruct((width // shards, 3 * width), F32),
            jax.ShapeDtypeStruct((width // shards, width), F32),
            jax.ShapeDtypeStruct((width // shards, ff), F32),
            jax.ShapeDtypeStruct((ff // shards, width), F32),
            jax.ShapeDtypeStruct((16, 128), F32),
        ),
        in_specs=[in_vmem] * 3 + [in_hbm] * 4,
        out_specs=(in_vmem,) * 7,
        scratch_shapes=scratch,
        compiler_params=pltpu.CompilerParams(
            collective_id=0, has_side_effects=True, vmem_limit_bytes=VMEM_BYTES
        ),
        cost_estimate=pl.CostEstimate(
            flops=14 * 10**9, bytes_accessed=30 * 10**6, transcendentals=5 * 10**6
        ),
    )(
        block_input.reshape(rows, width),
        cotangent.reshape(rows, width),
        vectors,
        w_qkv,
        w_out,
        w_fc,
        w_proj,
    )
    block_output, input_grad, grad_qkv, grad_out, grad_fc, grad_proj, sums = outs
    piece = width // shards
    return (
        block_output.reshape(block_input.shape),
        input_grad.reshape(block_input.shape),
        grad_qkv,
        grad_out,
        grad_fc,
        grad_proj,
        sums[0, :piece],
        sums[1, :piece],
        sums[2, :piece],
        sums[3, :piece],
        sums[4, :piece],
        sums[5, :piece],
        sums[6, :piece],
        sums[8, : ff // shards],
        sums[7, :piece],
    )


def on_device(*arrays):
    width, ff = arrays[0].shape[4], arrays[3].shape[1]
    fits = (
        lax.axis_size("ctx") == HEADS
        and lax.axis_size("fsdp") == 2
        and arrays[0].shape[:4] == (1, 1, 2, 64)
        and (width, ff) == (1024, 4096)
    )
    return fused_layer(*arrays) if fits else general_layer(*arrays)


def solution(mesh):
    placed = (
        P("fsdp", "ctx", None, None, None),
        P("fsdp", None),
        P("fsdp", None),
        P("fsdp", None),
        P("fsdp", None),
        P("fsdp"),
        P("fsdp"),
        P("fsdp"),
        P("fsdp"),
        P("fsdp"),
        P("fsdp"),
        P("fsdp"),
        P("fsdp"),
        P("fsdp"),
        P("fsdp", "ctx", None, None, None),
    )
    return jax.shard_map(
        on_device,
        mesh=mesh,
        in_specs=placed,
        out_specs=(
            P("fsdp", "ctx", None, None, None),
            P("fsdp", "ctx", None, None, None),
            P(("ctx", "fsdp"), None),
            P(("ctx", "fsdp"), None),
            P(("ctx", "fsdp"), None),
            P(("ctx", "fsdp"), None),
            P(("ctx", "fsdp")),
            P(("ctx", "fsdp")),
            P(("ctx", "fsdp")),
            P(("ctx", "fsdp")),
            P(("ctx", "fsdp")),
            P(("ctx", "fsdp")),
            P(("ctx", "fsdp")),
            P(("ctx", "fsdp")),
            P(("ctx", "fsdp")),
        ),
        check_vma=False,
    )
```

```python
from functools import partial
from types import SimpleNamespace

import jax
import jax.numpy as jnp
from jax import lax
from jax.experimental import pallas as pl
from jax.experimental.pallas import tpu as pltpu
from jax.sharding import PartitionSpec as P

HEADS = 16
VMEM_BYTES = 62 * 2**20


def norm_parts(values):
    average = jnp.mean(values, -1, keepdims=True)
    centered = values - average
    variance = jnp.mean(centered * centered, -1, keepdims=True)
    inverse = lax.rsqrt(variance + 1e-05)
    return (centered * inverse, inverse)


def norm_grads(upstream, normalized, inverse, gain):
    scaled = upstream * gain
    inner_part = (
        scaled
        - jnp.mean(scaled, -1, keepdims=True)
        - normalized * jnp.mean(scaled * normalized, -1, keepdims=True)
    )
    return (inverse * inner_part, jnp.sum(upstream * normalized, 0), jnp.sum(upstream, 0))


def rows_product(left, right):
    return lax.dot_general(
        left, right, (((0,), (0,)), ((), ())), preferred_element_type=jnp.float32
    )


def right_transposed(left, weight):
    return lax.dot_general(
        left, weight, (((1,), (1,)), ((), ())), preferred_element_type=jnp.float32
    )


def split_heads(matrix):
    return matrix.reshape(matrix.shape[0], HEADS, -1)


def head_scores(queries, keys, allowed, scaling):
    scores = (
        jnp.einsum(
            "qhd,khd->hqk",
            split_heads(queries),
            split_heads(keys),
            preferred_element_type=jnp.float32,
        )
        * scaling
    )
    return jnp.where(allowed[None], scores, -1e30)


def general_layer(
    block_input,
    w_qkv,
    w_out,
    w_fc,
    w_proj,
    ln1_gain,
    ln1_bias,
    ln2_gain,
    ln2_bias,
    bias_q,
    bias_v,
    bias_out,
    bias_fc,
    bias_proj,
    cotangent,
):
    seq_count = block_input.shape[0]
    blk_rows = block_input.shape[3]
    width = block_input.shape[4]
    seq_rows = 2 * blk_rows
    row_count = seq_count * seq_rows
    groups = lax.axis_size("ctx")
    member = lax.axis_index("ctx")
    head_size = width // HEADS
    scaling = head_size ** (-0.5)
    full_rows = groups * seq_rows
    gathered = (
        lax.all_gather(w_qkv, "fsdp", axis=0, tiled=True),
        lax.all_gather(w_out, "fsdp", axis=0, tiled=True),
        lax.all_gather(w_fc, "fsdp", axis=0, tiled=True),
        lax.all_gather(w_proj, "fsdp", axis=0, tiled=True),
        lax.all_gather(ln1_gain, "fsdp", axis=0, tiled=True),
        lax.all_gather(ln1_bias, "fsdp", axis=0, tiled=True),
        lax.all_gather(ln2_gain, "fsdp", axis=0, tiled=True),
        lax.all_gather(ln2_bias, "fsdp", axis=0, tiled=True),
        lax.all_gather(bias_q, "fsdp", axis=0, tiled=True),
        lax.all_gather(bias_v, "fsdp", axis=0, tiled=True),
        lax.all_gather(bias_out, "fsdp", axis=0, tiled=True),
        lax.all_gather(bias_fc, "fsdp", axis=0, tiled=True),
        lax.all_gather(bias_proj, "fsdp", axis=0, tiled=True),
    )
    weight_qkv, weight_out, weight_fc, weight_proj = (
        gathered[0],
        gathered[1],
        gathered[2],
        gathered[3],
    )
    vectors = [piece.astype(jnp.float32) for piece in gathered[4:]]
    (
        gain_one,
        shift_one,
        gain_two,
        shift_two,
        query_bias,
        value_bias,
        out_bias,
        fc_bias,
        proj_bias,
    ) = vectors
    local_index = jnp.arange(seq_rows)
    own_block = jnp.where(local_index // blk_rows == 0, member, 2 * groups - 1 - member)
    own_pos = own_block * blk_rows + local_index % blk_rows
    every_index = jnp.arange(full_rows)
    every_owner = every_index // seq_rows
    every_block = jnp.where(
        every_index // blk_rows % 2 == 0, every_owner, 2 * groups - 1 - every_owner
    )
    every_pos = every_block * blk_rows + every_index % blk_rows
    allowed = every_pos[None, :] <= own_pos[:, None]
    inputs = block_input.reshape(row_count, width).astype(jnp.float32)
    normal_one, inverse_one = norm_parts(inputs)
    normed_one = (normal_one * gain_one + shift_one).astype(jnp.bfloat16)
    bias_all = jnp.concatenate([query_bias, jnp.zeros_like(query_bias), value_bias])
    projected = (
        jnp.dot(normed_one, weight_qkv, preferred_element_type=jnp.float32) + bias_all
    ).astype(jnp.bfloat16)
    queries = projected[:, :width]
    keys = projected[:, width : 2 * width]
    values = projected[:, 2 * width :]
    key_all = lax.all_gather(keys, "ctx", axis=0, tiled=True)
    value_all = lax.all_gather(values, "ctx", axis=0, tiled=True)
    scores = head_scores(queries, key_all, allowed, scaling)
    row_top = jnp.max(scores, -1, keepdims=True)
    log_sum = row_top + jnp.log(jnp.sum(jnp.exp(scores - row_top), -1, keepdims=True))
    probs_low = jnp.exp(scores - log_sum).astype(jnp.bfloat16)
    mixed = jnp.einsum(
        "hqk,khd->qhd", probs_low, split_heads(value_all), preferred_element_type=jnp.float32
    )
    mixed_rows = mixed.reshape(seq_rows, width)
    attended = mixed_rows.astype(jnp.bfloat16)
    residual = inputs + jnp.dot(attended, weight_out, preferred_element_type=jnp.float32) + out_bias
    normal_two, inverse_two = norm_parts(residual)
    normed_two = (normal_two * gain_two + shift_two).astype(jnp.bfloat16)
    hidden = jnp.dot(normed_two, weight_fc, preferred_element_type=jnp.float32) + fc_bias
    activated, gelu_pullback = jax.vjp(partial(jax.nn.gelu, approximate=True), hidden)
    activated_low = activated.astype(jnp.bfloat16)
    result = (
        residual
        + jnp.dot(activated_low, weight_proj, preferred_element_type=jnp.float32)
        + proj_bias
    )
    block_output = result.astype(jnp.bfloat16).reshape(block_input.shape)
    weight_qkv, weight_out, weight_fc, weight_proj, gain_low_one, gain_low_two = (
        lax.all_gather(w_qkv, "fsdp", axis=0, tiled=True),
        lax.all_gather(w_out, "fsdp", axis=0, tiled=True),
        lax.all_gather(w_fc, "fsdp", axis=0, tiled=True),
        lax.all_gather(w_proj, "fsdp", axis=0, tiled=True),
        lax.all_gather(ln1_gain, "fsdp", axis=0, tiled=True),
        lax.all_gather(ln2_gain, "fsdp", axis=0, tiled=True),
    )
    gain_one = gain_low_one.astype(jnp.float32)
    gain_two = gain_low_two.astype(jnp.float32)
    out_grad_low = cotangent.reshape(row_count, width)
    upstream = out_grad_low.astype(jnp.float32)
    grad_proj = rows_product(activated_low, out_grad_low)
    grad_proj_bias = jnp.sum(upstream, 0)
    hidden_grad = gelu_pullback(right_transposed(out_grad_low, weight_proj))[0].astype(jnp.bfloat16)
    grad_fc = rows_product(normed_two, hidden_grad)
    grad_fc_bias = jnp.sum(hidden_grad.astype(jnp.float32), 0)
    residual_part, grad_gain_two, grad_shift_two = norm_grads(
        right_transposed(hidden_grad, weight_fc), normal_two, inverse_two, gain_two
    )
    residual_grad = upstream + residual_part
    branch_grad = residual_grad.astype(jnp.bfloat16)
    grad_out = rows_product(attended, branch_grad)
    grad_out_bias = jnp.sum(branch_grad.astype(jnp.float32), 0)
    attended_grad = right_transposed(branch_grad, weight_out).astype(jnp.bfloat16)
    key_all = lax.all_gather(keys, "ctx", axis=0, tiled=True)
    value_all = lax.all_gather(values, "ctx", axis=0, tiled=True)
    scores = head_scores(queries, key_all, allowed, scaling)
    probs = jnp.exp(scores - log_sum)
    prob_grad = jnp.einsum(
        "qhd,khd->hqk",
        split_heads(attended_grad),
        split_heads(value_all),
        preferred_element_type=jnp.float32,
    )
    inner_sum = jnp.sum(probs * prob_grad, -1, keepdims=True)
    score_grad = (probs * (prob_grad - inner_sum)).astype(jnp.bfloat16)
    query_part = (
        jnp.einsum(
            "hqk,khd->qhd", score_grad, split_heads(key_all), preferred_element_type=jnp.float32
        )
        * scaling
    )
    query_grads = query_part.reshape(seq_rows, width)
    probs_low = probs.astype(jnp.bfloat16)
    query_heads = split_heads(queries)
    grad_heads = split_heads(attended_grad)

    def key_terms(
        start,
        count,
        score_grad=score_grad,
        probs_low=probs_low,
        query_heads=query_heads,
        grad_heads=grad_heads,
    ):
        key_part = (
            jnp.einsum("hqk,qhd->khd", score_grad, query_heads, preferred_element_type=jnp.float32)
            * scaling
        )
        value_part = jnp.einsum(
            "hqk,qhd->khd", probs_low, grad_heads, preferred_element_type=jnp.float32
        )
        return jnp.concatenate(
            [key_part.reshape(count, width), value_part.reshape(count, width)], 1
        )

    own_terms = lax.psum_scatter(
        key_terms(jnp.int32(0), lax.axis_size("ctx") * seq_rows),
        "ctx",
        scatter_dimension=0,
        tiled=True,
    )
    key_grads = own_terms[:, :width]
    value_grads = own_terms[:, width:]
    qkv_grad = jnp.concatenate([query_grads, key_grads, value_grads], 1).astype(jnp.bfloat16)
    grad_qkv = rows_product(normed_one, qkv_grad)
    qkv_sums = jnp.sum(qkv_grad.astype(jnp.float32), 0)
    grad_query_bias = qkv_sums[:width]
    grad_value_bias = qkv_sums[2 * width :]
    input_part, grad_gain_one, grad_shift_one = norm_grads(
        right_transposed(qkv_grad, weight_qkv), normal_one, inverse_one, gain_one
    )
    input_grad = (residual_grad + input_part).reshape(block_input.shape)
    sharded = (
        lax.psum_scatter(grad_qkv, ("ctx", "fsdp"), scatter_dimension=0, tiled=True),
        lax.psum_scatter(grad_out, ("ctx", "fsdp"), scatter_dimension=0, tiled=True),
        lax.psum_scatter(grad_fc, ("ctx", "fsdp"), scatter_dimension=0, tiled=True),
        lax.psum_scatter(grad_proj, ("ctx", "fsdp"), scatter_dimension=0, tiled=True),
        lax.psum_scatter(grad_gain_one, ("ctx", "fsdp"), scatter_dimension=0, tiled=True),
        lax.psum_scatter(grad_shift_one, ("ctx", "fsdp"), scatter_dimension=0, tiled=True),
        lax.psum_scatter(grad_gain_two, ("ctx", "fsdp"), scatter_dimension=0, tiled=True),
        lax.psum_scatter(grad_shift_two, ("ctx", "fsdp"), scatter_dimension=0, tiled=True),
        lax.psum_scatter(grad_query_bias, ("ctx", "fsdp"), scatter_dimension=0, tiled=True),
        lax.psum_scatter(grad_value_bias, ("ctx", "fsdp"), scatter_dimension=0, tiled=True),
        lax.psum_scatter(grad_out_bias, ("ctx", "fsdp"), scatter_dimension=0, tiled=True),
        lax.psum_scatter(grad_fc_bias, ("ctx", "fsdp"), scatter_dimension=0, tiled=True),
        lax.psum_scatter(grad_proj_bias, ("ctx", "fsdp"), scatter_dimension=0, tiled=True),
    )
    return (
        block_output,
        input_grad,
        sharded[0],
        sharded[1],
        sharded[2],
        sharded[3],
        sharded[4],
        sharded[5],
        sharded[6],
        sharded[7],
        sharded[8],
        sharded[9],
        sharded[10],
        sharded[11],
        sharded[12],
    )


MESH = pl.DeviceIdType.MESH
BF16, F32 = jnp.bfloat16, jnp.float32
PLANE = 4
NEG = -1e30


def remote(src, dst, sent, received, device):
    return pltpu.make_async_remote_copy(
        src_ref=src,
        dst_ref=dst,
        send_sem=sent,
        recv_sem=received,
        device_id=device,
        device_id_type=MESH,
    )


def dot(left, right):
    return jnp.dot(left, right, preferred_element_type=F32)


def low_lanes(rows):
    return lax.broadcasted_iota(jnp.int32, (rows, 128), 1) < 64


def swap(block):
    return pltpu.roll(block, 64, 1)


def pack_pair(pair):
    half = pair.shape[0] // 2
    low = low_lanes(half)
    top, bottom = pair[:half], pair[half:]
    return jnp.where(low, top, swap(bottom)), jnp.where(low, swap(top), bottom)


def unpack_pair(even, odd):
    low = low_lanes(even.shape[0])
    return jnp.concatenate(
        [jnp.where(low, even, swap(odd)), jnp.where(low, swap(even), odd)], 0
    )


def part(index, size):
    return pl.ds(pl.multiple_of(index * size, size), size)


def layer_shapes(rows, width, ff, groups):
    members = 2 * PLANE
    layers = groups // PLANE
    tokens = members * rows
    half = rows // 2
    keys = groups * half
    share = width // members
    return dict(
        w_qkv=((width, 3 * width), BF16),
        w_out=((width, width), BF16),
        w_fc=((width, ff), BF16),
        w_proj=((ff, width), BF16),
        vec_low=((2, 16, width // 2), BF16),
        vec=((2, 16, width // 2), F32),
        row=((8, width), F32),
        cot_all=((members, rows, width), BF16),
        n1=((rows, width), BF16),
        n1_t=((width, tokens), BF16),
        stage=((groups, 3, half, 128), BF16),
        qkv=((3, keys, 128), BF16),
        kv_roll=((2, keys, 128), BF16),
        q_low=((2, keys, 128), BF16),
        g_low=((2, keys, 128), BF16),
        q_t=((128, keys), BF16),
        g_t=((128, keys), BF16),
        stat=((2, keys, 128), F32),
        mixed=((keys, 128), F32),
        o_out=((groups, half, 128), BF16),
        o_in=((groups, half, 128), BF16),
        att=((rows, width), BF16),
        att_t=((layers, members, width // members // layers, rows), BF16),
        att_all=((layers, width // members // layers, tokens), BF16),
        res=((rows, width), F32),
        n2=((rows, width), BF16),
        n2_t=((width, tokens), BF16),
        act_t=((members, layers, ff // members // layers, rows), BF16),
        act_all=((layers, ff // members // layers, tokens), BF16),
        hg_out=((members, rows, ff // members), BF16),
        hg_all=((members, rows, ff // members), BF16),
        acc_o=((rows, width), F32),
        acc_d=((rows, width), F32),
        res_grad=((rows, width), F32),
        bg_all=((members, rows, width), BF16),
        g_out=((groups, half, 128), BF16),
        g_in=((keys, 128), BF16),
        dk_t=((128, keys), F32),
        dv_t=((128, keys), F32),
        back=((groups, 3, half, 128), BF16),
        qg=((rows, 3 * width), BF16),
        qg_out=((members, rows, 3 * share), BF16),
        qg_all=((members, rows, 3 * share), BF16),
        fc_own=((width // layers, ff // members), F32),
        qkv_own=((width // layers, 3 * share), F32),
        fc_x=((members, width // layers // members, ff // members), BF16),
        fc_y=((members, width // layers // members, ff // members), BF16),
        qkv_x=((members, width // layers // members, 3 * share), BF16),
        qkv_y=((members, width // layers // members, 3 * share), BF16),
        sums=((16, width), F32),
        sums_in=((7, 16, width), F32),
    )


SEMAPHORES = dict(
    local=4,
    w_sent=15,
    w_got=15,
    v_sent=1,
    v_got=1,
    qkv_sent=16,
    qkv_got=16,
    o_sent=16,
    o_got=16,
    g_sent=16,
    g_got=16,
    back_sent=16,
    back_got=16,
    cot_sent=8,
    cot_got=8,
    n1_sent=8,
    n1_got=8,
    n2_sent=8,
    n2_got=8,
    bg_sent=8,
    bg_got=8,
    act_sent=8,
    act_got=8,
    hg_sent=8,
    hg_got=8,
    att_sent=8,
    att_got=8,
    qg_sent=8,
    qg_got=8,
    rp_sent=4,
    rp_got=4,
    rf_sent=4,
    rf_got=4,
    ro_sent=4,
    ro_got=4,
    rq_sent=4,
    rq_got=4,
    fx_sent=8,
    fx_got=8,
    qx_sent=8,
    qx_got=8,
    s_sent=8,
    s_got=8,
)


def layer_kernel(names, *refs):
    x_ref, cot_ref, vec_ref, wq_hbm, wo_hbm, wf_hbm, wp_hbm = refs[:7]
    y_ref, gx_ref, gqkv_ref, gout_ref, gfc_ref, gproj_ref, gvec_ref = refs[7:14]
    s = SimpleNamespace(**dict(zip(names, refs[14:])))
    rows, width = x_ref.shape
    ff = s.w_fc.shape[1]
    half = rows // 2
    groups = s.stage.shape[0]
    members = 2 * PLANE
    layers = groups // PLANE
    tokens = members * rows
    keys = groups * half
    chunk = ff // members
    share = width // members
    scaling = float(width // HEADS) ** (-0.5)
    factor = scaling * 1.4426950408889634
    me = lax.axis_index("ctx")
    core = lax.axis_index("fsdp")
    other = 1 - core
    layer, place = me // PLANE, me % PLANE
    member = place * 2 + core
    twin = (me, other)

    barrier = pltpu.get_barrier_semaphore()
    for step in range(1, groups):
        pl.semaphore_signal(
            barrier, inc=1, device_id=((me + step) % groups, core), device_id_type=MESH
        )
    for step in range(PLANE):
        pl.semaphore_signal(
            barrier,
            inc=1,
            device_id=(layer * PLANE + (place + step) % PLANE, other),
            device_id_type=MESH,
        )
    pl.semaphore_wait(barrier, groups - 1 + PLANE)

    def at_member(index):
        return (layer * PLANE + index // 2, index % 2)

    def top_rows(ref, source):
        count = source.shape[0]
        return ref.at[pl.ds(pl.multiple_of(core * count, count), count)]

    def peer_rows(ref, source):
        count = source.shape[0]
        return ref.at[pl.ds(pl.multiple_of(other * count, count), count)]

    first = 2 * (1 - layer // 2)

    def order(step):
        return (step + first) % 4

    pltpu.make_async_copy(wq_hbm, top_rows(s.w_qkv, wq_hbm), s.local.at[0]).start()

    def qkv_piece(step, third):
        columns = part(third * 4 + order(step), 256)
        index = step * 3 + third
        return remote(
            wq_hbm.at[:, columns],
            top_rows(s.w_qkv, wq_hbm).at[:, columns],
            s.w_sent.at[index],
            s.w_got.at[index],
            twin,
        )

    vec_copy = remote(vec_ref, s.vec_low.at[core], s.v_sent.at[0], s.v_got.at[0], twin)
    vec_copy.start()
    for step in range(4):
        for third in range(3):
            qkv_piece(step, third).start()
    big = ((wo_hbm, s.w_out), (wf_hbm, s.w_fc), (wp_hbm, s.w_proj))

    def big_piece(index):
        source, target = big[index]
        return remote(
            source, top_rows(target, source), s.w_sent.at[12 + index], s.w_got.at[12 + index], twin
        )

    def big_local(index):
        source, target = big[index]
        return pltpu.make_async_copy(source, top_rows(target, source), s.local.at[1 + index])

    for index in range(3):
        big_piece(index).start()
        big_local(index).start()

    def gather_copy(where, sent, got, index, slot, device):
        return remote(where(slot), where(slot), sent.at[index], got.at[slot], device)

    def gather_start(where, sent, got):
        for step in range(1, PLANE):
            peer = layer * PLANE + (place + step) % PLANE
            gather_copy(where, sent, got, step, member, (peer, core)).start()
        gather_copy(where, sent, got, 0, member, twin).start()

    def gather_forward(where, sent, got):
        for step in range(1, PLANE):
            slot = ((place + step) % PLANE) * 2 + core
            gather_copy(where, sent, got, 0, slot, twin).wait_recv()
            gather_copy(where, sent, got, PLANE - 1 + step, slot, twin).start()

    def gather_finish(where, sent, got):
        for step in range(PLANE):
            slot = ((place + step) % PLANE) * 2 + other
            gather_copy(where, sent, got, 0, slot, twin).wait_recv()

    def gather_drain(where, sent, got):
        for index in range(2 * PLANE - 1):
            gather_copy(where, sent, got, index, member, twin).wait_send()

    def cot_at(slot):
        return s.cot_all.at[slot]

    def bg_at(slot):
        return s.bg_all.at[slot]

    def n1_at(slot):
        return s.n1_t.at[:, part(slot, rows)]

    def n2_at(slot):
        return s.n2_t.at[:, part(slot, rows)]

    def deal_copy(source, target, sent, got, index, slot):
        return remote(source(index), target(slot), sent.at[index], got.at[slot], at_member(index))

    def deal_one(source, target, sent, got, index):
        @pl.when(index == member)
        def _():
            pltpu.make_async_copy(source(index), target(member), got.at[member]).start()

        @pl.when(index != member)
        def _():
            deal_copy(source, target, sent, got, index, member).start()

    def deal_start(source, target, sent, got):
        for step in range(members):
            if step == 0:
                pltpu.make_async_copy(source(member), target(member), got.at[member]).start()
            else:
                deal_copy(source, target, sent, got, (member + step) % members, member).start()

    def deal_wait(source, target, sent, got):
        for slot in range(members):
            pltpu.make_async_copy(source(0), target(slot), got.at[slot]).wait()

    def deal_drain(source, target, sent, got):
        for step in range(1, members):
            deal_copy(source, target, sent, got, (member + step) % members, member).wait_send()

    def swap_one(source, target, sent, got, index):
        @pl.when(index == me)
        def _():
            pltpu.make_async_copy(source(index), target(me), got.at[me]).start()

        @pl.when(index != me)
        def _():
            remote(source(index), target(me), sent.at[index], got.at[me], (index, core)).start()

    def swap_wait(source, target, sent, got):
        for slot in range(groups):
            pltpu.make_async_copy(source(0), target(slot), got.at[slot]).wait()

    def swap_drain(source, target, sent, got):
        for step in range(1, groups):
            peer = (me + step) % groups
            remote(source(peer), target(me), sent.at[peer], got.at[me], (peer, core)).wait_send()

    qkv_move = (
        lambda h: s.stage.at[h],
        lambda i: s.qkv.at[:, part(i, half)],
        s.qkv_sent,
        s.qkv_got,
    )
    o_move = (lambda h: s.o_out.at[h], lambda h: s.o_in.at[h], s.o_sent, s.o_got)
    g_move = (lambda h: s.g_out.at[h], lambda i: s.g_in.at[part(i, half)], s.g_sent, s.g_got)
    back_move = (lambda h: s.stage.at[h], lambda h: s.back.at[h], s.back_sent, s.back_got)

    def vec_row(index):
        return jnp.concatenate([s.vec[0, index : index + 1, :], s.vec[1, index : index + 1, :]], 1)

    s.cot_all[member] = cot_ref[...]
    gather_start(cot_at, s.cot_sent, s.cot_got)
    remote(vec_ref, s.vec_low.at[other], s.v_sent.at[0], s.v_got.at[0], twin).wait_recv()
    s.vec[core] = vec_ref[...].astype(F32)
    s.vec[other] = s.vec_low[other].astype(F32)
    s.row[0:1, :] = vec_row(4)
    s.row[1:2, :] = vec_row(5)
    for quarter in range(4):
        at = 8 + quarter % 2 * 2
        s.row[4 + quarter : 5 + quarter, :] = jnp.concatenate(
            [s.vec[quarter // 2, at : at + 1, :], s.vec[quarter // 2, at + 1 : at + 2, :]], 1
        )
    inputs = x_ref[...].astype(F32)
    normal, _ = norm_parts(inputs)
    normed = (normal * vec_row(0) + vec_row(1)).astype(BF16)
    s.n1[...] = normed
    s.n1_t[:, part(member, rows)] = normed.astype(F32).T.astype(BF16)
    pltpu.make_async_copy(wq_hbm, top_rows(s.w_qkv, wq_hbm), s.local.at[0]).wait()

    for step in range(4):
        four = order(step)
        for third in range(3):
            index = step * 3 + third
            columns = part(third * 4 + four, 256)
            remote(
                wq_hbm.at[:, columns],
                peer_rows(s.w_qkv, wq_hbm).at[:, columns],
                s.w_sent.at[index],
                s.w_got.at[index],
                twin,
            ).wait_recv()
            product = dot(s.n1[...], s.w_qkv[:, columns])
            if third == 0:
                product = product + s.row[0:1, part(four, 256)]
            if third == 2:
                product = product + s.row[1:2, part(four, 256)]
            for pair in range(2):
                even, odd = pack_pair(product[:, pair * 128 : pair * 128 + 128])
                s.stage[four * 4 + 2 * pair, third] = even.astype(BF16)
                s.stage[four * 4 + 2 * pair + 1, third] = odd.astype(BF16)
        for head in range(4):
            swap_one(*qkv_move, four * 4 + head)

    swap_wait(*qkv_move)
    gather_start(n1_at, s.n1_sent, s.n1_got)
    low_all = low_lanes(keys)
    query = s.qkv[0].astype(F32)
    s.q_low[0] = jnp.where(low_all, query, 0.0).astype(BF16)
    s.q_low[1] = jnp.where(low_all, swap(query), 0.0).astype(BF16)
    s.q_t[...] = query.T.astype(BF16)
    s.kv_roll[0] = swap(s.qkv[1].astype(F32)).astype(BF16)
    s.kv_roll[1] = swap(s.qkv[2].astype(F32)).astype(BF16)

    tile = 256
    per_tile = tile // half
    low_tile = low_lanes(tile)
    row_at = lax.broadcasted_iota(jnp.int32, (tile, tile), 0)
    col_at = lax.broadcasted_iota(jnp.int32, (tile, tile), 1)

    def late(index):
        return index + (per_tile - 1 - 2 * (index // half)) * half

    masks = (col_at <= row_at, late(col_at) <= late(row_at))

    def key_block(region, at):
        return s.qkv[1, at, :] if region == 0 else s.kv_roll[0, at, :]

    def value_block(region, at):
        return s.qkv[2, at, :] if region == 0 else s.kv_roll[1, at, :]

    def first_tile(queries, region, at):
        scores = jnp.where(
            masks[region], right_transposed(queries, key_block(region, at)), NEG
        )
        top = jnp.max(scores, 1, keepdims=True)
        probs = jnp.exp2((scores - top) * factor)
        total = jnp.sum(probs, 1, keepdims=True)
        return top, total, dot(probs.astype(BF16), value_block(region, at))

    def next_tile(queries, region, at, carry):
        top, total, mix = carry
        scores = right_transposed(queries, key_block(region, at))
        higher = jnp.maximum(top, jnp.max(scores, 1, keepdims=True))
        probs = jnp.exp2((scores - higher) * factor)
        shrink = jnp.exp2((top - higher) * factor)
        total = total * shrink + jnp.sum(probs, 1, keepdims=True)
        return higher, total, mix * shrink + dot(probs.astype(BF16), value_block(region, at))

    n_tiles = keys // tile

    def attend(index, _):
        at = part(index, tile)
        early_q, late_q = s.q_low[0, at, :], s.q_low[1, at, :]
        one = lax.fori_loop(
            0,
            index,
            lambda k, carry: next_tile(early_q, 0, part(k, tile), carry),
            first_tile(early_q, 0, at),
        )
        two = lax.fori_loop(
            index + 1,
            n_tiles,
            lambda k, carry: next_tile(late_q, 1, part(k, tile), carry),
            first_tile(late_q, 1, at),
        )
        two = lax.fori_loop(
            0, n_tiles // 2, lambda k, carry: next_tile(late_q, 0, part(k, 2 * tile), carry), two
        )
        s.stat[0, at, 0:1] = one[0] * factor + jnp.log2(one[1])
        s.stat[1, at, 0:1] = two[0] * factor + jnp.log2(two[1])
        out = jnp.where(low_tile, one[2] / one[1], swap(two[2] / two[1]))
        s.mixed[at, :] = out
        s.o_out[part(index, per_tile)] = out.astype(BF16).reshape(per_tile, half, 128)
        for block in range(per_tile):
            swap_one(*o_move, index * per_tile + block)
        return 0

    lax.fori_loop(0, n_tiles, attend, 0)

    for index in range(3):
        source, target = big[index]
        remote(
            source,
            peer_rows(target, source),
            s.w_sent.at[12 + index],
            s.w_got.at[12 + index],
            twin,
        ).wait_recv()
        big_local(index).wait()
    swap_wait(*o_move)
    for pair in range(HEADS // 2):
        columns = slice(pair * 128, pair * 128 + 128)
        s.att[:, columns] = unpack_pair(
            s.o_in[2 * pair].astype(F32), s.o_in[2 * pair + 1].astype(F32)
        ).astype(BF16)
    turned = s.att[...].astype(F32).T.astype(BF16)
    s.att_t[...] = turned.reshape(s.att_t.shape)
    att_move = (
        lambda g: s.att_t.at[:, g],
        lambda g: s.att_all.at[:, :, part(g, rows)],
        s.att_sent,
        s.att_got,
    )
    def project(index, _):
        at = part(index, 256)
        s.acc_d[:, at] = dot(s.att[...], s.w_out[:, at])
        return 0

    lax.fori_loop(0, width // 256, project, 0)
    s.res[...] = x_ref[...].astype(F32) + s.acc_d[...] + vec_row(6)
    normal, _ = norm_parts(s.res[...])
    normed = (normal * vec_row(2) + vec_row(3)).astype(BF16)
    s.n2[...] = normed
    s.n2_t[:, part(member, rows)] = normed.astype(F32).T.astype(BF16)
    s.acc_o[...] = jnp.zeros_like(s.acc_o)
    s.acc_d[...] = jnp.zeros_like(s.acc_d)
    s.sums[...] = jnp.zeros_like(s.sums)
    hg_move = (lambda g: s.hg_out.at[g], lambda g: s.hg_all.at[g], s.hg_sent, s.hg_got)
    curve = 0.7978845608028654

    act_move = (
        lambda g: s.act_t.at[g],
        lambda g: s.act_all.at[:, :, part(g, rows)],
        s.act_sent,
        s.act_got,
    )
    quarters = ff // width
    piece = width // members

    def feed(step, _):
        index = (member + 1 + step) % members
        places = [part(quarter * members + index, piece) for quarter in range(quarters)]
        bias = jnp.concatenate(
            [s.row[4 + quarter : 5 + quarter, part(index, piece)] for quarter in range(quarters)], 1
        )
        into = jnp.concatenate([s.w_fc[:, at] for at in places], 1)
        back = jnp.concatenate([s.w_proj[at, :] for at in places], 0)
        hidden = dot(s.n2[...], into) + bias
        upstream = right_transposed(cot_ref[...], back)
        square = hidden * hidden
        bend = jnp.tanh(curve * hidden * (1.0 + 0.044715 * square))
        rise = 0.5 * (1.0 + bend)
        active = (hidden * rise).astype(BF16)
        slope = rise + 0.5 * hidden * (1.0 - bend * bend) * (
            curve * (1.0 + 3.0 * 0.044715 * square)
        )
        grad = (upstream * slope).astype(BF16)
        s.act_t[index] = active.astype(F32).T.astype(BF16).reshape(s.act_t.shape[1:])
        deal_one(*act_move, index)
        s.hg_out[index] = grad
        s.acc_o[...] += dot(active, back)
        s.acc_d[...] += right_transposed(grad, into)
        total = jnp.sum(grad.astype(F32), 0, keepdims=True)
        for quarter in range(quarters):
            s.sums[8 + quarter : 9 + quarter, part(index, piece)] = total[
                :, quarter * piece : quarter * piece + piece
            ]
        return 0

    lax.fori_loop(0, members, feed, 0)
    upstream = cot_ref[...].astype(F32)
    normal, inverse = norm_parts(s.res[...])
    step_grad, gain_grad, shift_grad = norm_grads(s.acc_d[...], normal, inverse, vec_row(2))
    s.sums[2:3, :] = gain_grad[None]
    s.sums[3:4, :] = shift_grad[None]
    s.sums[7:8, :] = jnp.sum(upstream, 0, keepdims=True)
    res_grad = upstream + step_grad
    s.res_grad[...] = res_grad
    branch = res_grad.astype(BF16)
    s.bg_all[member] = branch
    s.sums[6:7, :] = jnp.sum(branch.astype(F32), 0, keepdims=True)
    for step in range(4):
        four = order(step)
        product = right_transposed(s.bg_all[member], s.w_out[part(four, 256), :])
        for pair in range(2):
            even, odd = pack_pair(product[:, pair * 128 : pair * 128 + 128])
            s.g_out[four * 4 + 2 * pair] = even.astype(BF16)
            s.g_out[four * 4 + 2 * pair + 1] = odd.astype(BF16)
        for head in range(4):
            swap_one(*g_move, four * 4 + head)
    deal_start(*hg_move)
    gather_start(n2_at, s.n2_sent, s.n2_got)
    y_ref[...] = (s.res[...] + s.acc_o[...] + vec_row(7)).astype(BF16)
    gather_forward(cot_at, s.cot_sent, s.cot_got)
    gather_forward(n1_at, s.n1_sent, s.n1_got)
    swap_drain(*qkv_move)

    beside = layer + 1 - 2 * (layer % 2)
    beyond = (layer + 2) % layers
    across = (beside + 2) % layers

    def spread_copy(move, slot, target):
        buffer_out, buffer_in, sent, got = move
        return remote(
            buffer_out(slot),
            buffer_in(slot),
            sent.at[slot],
            got.at[slot],
            (target * PLANE + place, core),
        )

    def spread(move, product, own_ref):
        for slot, index in enumerate((beside, across, beyond)):
            move[0](slot)[...] = product(index).astype(BF16)
            if slot < 2:
                spread_copy(move, slot, beside).start()
        own_ref[...] = product(layer)

    def spread_on(move):
        spread_copy(move, 1, beside).wait_recv()
        pair = move[0](2)[...].astype(F32) + move[1](1)[...].astype(F32)
        move[0](2)[...] = pair.astype(BF16)
        spread_copy(move, 2, beyond).start()

    def collect(move, own_ref):
        for slot in (0, 2):
            spread_copy(move, slot, beside).wait_recv()
        own_ref[...] += move[1](0)[...].astype(F32) + move[1](2)[...].astype(F32)

    def spread_drain(move):
        for slot in range(3):
            spread_copy(move, slot, beside).wait_send()

    proj_rows = ff // members // layers
    out_rows = share // layers
    fc_rows = width // layers

    def rows_of(ref, start, count, columns=slice(None)):
        return lambda i: ref.at[pl.ds(pl.multiple_of(start + i * count, count), count), columns]

    sum_proj = (
        rows_of(s.w_proj, 0, proj_rows),
        rows_of(s.w_proj, 512, proj_rows),
        s.rp_sent,
        s.rp_got,
    )
    sum_out = (
        rows_of(s.w_proj, 1024, out_rows),
        rows_of(s.w_proj, 1152, out_rows),
        s.ro_sent,
        s.ro_got,
    )
    sum_fc = (
        rows_of(s.w_fc, 0, fc_rows, pl.ds(0, chunk)),
        rows_of(s.w_fc, 0, fc_rows, pl.ds(chunk, chunk)),
        s.rf_sent,
        s.rf_got,
    )
    sum_qkv = (
        rows_of(s.w_fc, 0, fc_rows, pl.ds(2 * chunk, 3 * share)),
        rows_of(s.w_fc, 0, fc_rows, pl.ds(3 * chunk, 3 * share)),
        s.rq_sent,
        s.rq_got,
    )
    def grad_of_proj():
        gather_finish(cot_at, s.cot_sent, s.cot_got)
        deal_wait(*act_move)
        spread(
            sum_proj,
            lambda i: dot(s.act_all[i], s.cot_all[...].reshape(tokens, width)),
            gproj_ref,
        )

    def grad_of_fc():
        gather_forward(n2_at, s.n2_sent, s.n2_got)
        gather_finish(n2_at, s.n2_sent, s.n2_got)
        deal_wait(*hg_move)
        spread(
            sum_fc,
            lambda i: dot(s.n2_t[part(i, fc_rows), :], s.hg_all[...].reshape(tokens, chunk)),
            s.fc_own,
        )

    def grad_of_out():
        gather_finish(bg_at, s.bg_sent, s.bg_got)
        deal_wait(*att_move)
        spread(
            sum_out,
            lambda i: dot(s.att_all[i], s.bg_all[...].reshape(tokens, width)),
            gout_ref,
        )

    swap_wait(*g_move)
    upstream = s.g_in[...].astype(F32)
    s.g_low[0] = jnp.where(low_all, upstream, 0.0).astype(BF16)
    s.g_low[1] = jnp.where(low_all, swap(upstream), 0.0).astype(BF16)
    s.g_t[...] = upstream.T.astype(BF16)
    inner = upstream * s.mixed[...]
    s.stat[0, :, 1:2] = jnp.sum(jnp.where(low_all, inner, 0.0), 1, keepdims=True)
    s.stat[1, :, 1:2] = jnp.sum(jnp.where(low_all, 0.0, inner), 1, keepdims=True)
    s.dk_t[...] = jnp.zeros_like(s.dk_t)
    s.dv_t[...] = jnp.zeros_like(s.dv_t)

    def back_tile(side, region, at_q, at_k, masked, total):
        scores = right_transposed(s.q_low[side, at_q, :], key_block(region, at_k))
        probs = jnp.exp2(scores * factor - s.stat[side, at_q, 0:1])
        if masked:
            probs = jnp.where(masks[region], probs, 0.0)
        prob_grad = right_transposed(s.g_low[side, at_q, :], value_block(region, at_k))
        score_grad = (probs * (prob_grad - s.stat[side, at_q, 1:2])).astype(BF16)
        head = slice(side * 64, side * 64 + 64)
        into = slice(region * 64, region * 64 + 64)
        s.dk_t[into, at_k] += dot(s.q_t[head, at_q], score_grad)
        s.dv_t[into, at_k] += dot(s.g_t[head, at_q], probs.astype(BF16))
        more = dot(score_grad, key_block(region, at_k))
        return more if total is None else total + more

    def attend_back(index, _):
        at = part(index, tile)
        one = lax.fori_loop(
            0,
            index,
            lambda k, total: back_tile(0, 0, at, part(k, tile), False, total),
            back_tile(0, 0, at, at, True, None),
        )
        two = lax.fori_loop(
            index + 1,
            n_tiles,
            lambda k, total: back_tile(1, 1, at, part(k, tile), False, total),
            back_tile(1, 1, at, at, True, None),
        )
        two = lax.fori_loop(
            0,
            n_tiles // 2,
            lambda k, total: back_tile(1, 0, at, part(k, 2 * tile), False, total),
            two,
        )
        out = (jnp.where(low_tile, one, swap(two)) * scaling).astype(BF16)
        s.stage[part(index, per_tile), 0] = out.reshape(per_tile, half, 128)
        return 0

    attend_back(0, 0)
    grad_of_proj()
    attend_back(1, 0)
    attend_back(2, 0)
    spread_on(sum_proj)
    gather_start(bg_at, s.bg_sent, s.bg_got)
    deal_start(*att_move)
    attend_back(3, 0)
    s.stage[:, 1] = (s.dk_t[...].T * scaling).astype(BF16).reshape(groups, half, 128)
    s.stage[:, 2] = s.dv_t[...].T.astype(BF16).reshape(groups, half, 128)
    for step in range(4):
        for head in range(4):
            swap_one(*back_move, order(step) * 4 + head)
    grad_of_fc()
    gather_forward(bg_at, s.bg_sent, s.bg_got)
    grad_of_out()
    spread_on(sum_fc)

    swap_wait(*back_move)
    spread_on(sum_out)
    for pair in range(HEADS // 2):
        for third in range(3):
            block = unpack_pair(
                s.back[2 * pair, third].astype(F32), s.back[2 * pair + 1, third].astype(F32)
            ).astype(BF16)
            s.qg_out[pair, :, third * 128 : third * 128 + 128] = block
            columns = slice(third * width + pair * 128, third * width + pair * 128 + 128)
            s.qg[:, columns] = block
    qg_move = (lambda g: s.qg_out.at[g], lambda g: s.qg_all.at[g], s.qg_sent, s.qg_got)
    deal_start(*qg_move)
    s.sums[4:5, :] = jnp.sum(s.qg[:, :width].astype(F32), 0, keepdims=True)
    s.sums[5:6, :] = jnp.sum(s.qg[:, 2 * width :].astype(F32), 0, keepdims=True)

    def project_back(index, _):
        s.acc_d[:, part(index, 256)] = right_transposed(s.qg[...], s.w_qkv[part(index, 256), :])
        return 0

    lax.fori_loop(0, width // 256, project_back, 0)
    normal, inverse = norm_parts(x_ref[...].astype(F32))
    step_grad, gain_grad, shift_grad = norm_grads(s.acc_d[...], normal, inverse, vec_row(0))
    s.sums[0:1, :] = gain_grad[None]
    s.sums[1:2, :] = shift_grad[None]
    gx_ref[...] = s.res_grad[...] + step_grad

    def sum_copy(index, slot, device):
        return remote(s.sums, s.sums_in.at[slot], s.s_sent.at[index], s.s_got.at[slot], device)

    sum_copy(0, 0, twin).start()

    gather_finish(n1_at, s.n1_sent, s.n1_got)
    deal_wait(*qg_move)
    spread(
        sum_qkv,
        lambda i: dot(s.n1_t[part(i, fc_rows), :], s.qg_all[...].reshape(tokens, 3 * share)),
        s.qkv_own,
    )
    sum_copy(0, 0, twin).wait()
    s.sums[...] += s.sums_in[0]
    for step in range(1, PLANE):
        sum_copy(step, step, (layer * PLANE + (place + step) % PLANE, core)).start()

    fx_move = (lambda g: s.fc_x.at[g], lambda g: s.fc_y.at[g], s.fx_sent, s.fx_got)
    qx_move = (lambda g: s.qkv_x.at[g], lambda g: s.qkv_y.at[g], s.qx_sent, s.qx_got)
    collect(sum_fc, s.fc_own)
    s.fc_x[...] = s.fc_own[...].astype(BF16).reshape(s.fc_x.shape)
    deal_start(*fx_move)
    for step in range(1, PLANE):
        sum_copy(step, step, twin).wait()
    s.sums[...] += s.sums_in[1] + s.sums_in[2] + s.sums_in[3]
    for step in range(1, layers):
        peer = ((layer + step) % layers) * PLANE + place
        sum_copy(3 + step, 3 + step, (peer, core)).start()
    collect(sum_proj, gproj_ref)
    collect(sum_out, gout_ref)
    spread_on(sum_qkv)
    collect(sum_qkv, s.qkv_own)
    s.qkv_x[...] = s.qkv_own[...].astype(BF16).reshape(s.qkv_x.shape)
    deal_start(*qx_move)
    for step in range(1, layers):
        sum_copy(3 + step, 3 + step, twin).wait()
    s.sums[...] += s.sums_in[4] + s.sums_in[5] + s.sums_in[6]
    owner = me * 2 + core
    gvec_ref[...] = jnp.zeros_like(gvec_ref)
    block = s.sums[0:8, part(owner // 4, 128)]
    gvec_ref[0:8, :] = pltpu.roll(block, (128 - (owner % 4) * 32) % 128, 1)
    block = s.sums[8:16, part(owner % 8, 128)]
    chosen = lax.broadcasted_iota(jnp.int32, block.shape, 0) == owner // 8
    gvec_ref[8:9, :] = jnp.sum(jnp.where(chosen, block, 0.0), 0, keepdims=True)
    deal_wait(*fx_move)
    for slot in range(members):
        for quarter in range(quarters):
            start = quarter * width + slot * piece
            gfc_ref[:, start : start + piece] = s.fc_y[
                slot, :, quarter * piece : quarter * piece + piece
            ].astype(F32)
    deal_wait(*qx_move)
    for slot in range(members):
        for third in range(3):
            start = third * width + slot * 128
            gqkv_ref[:, start : start + 128] = s.qkv_y[
                slot, :, third * 128 : third * 128 + 128
            ].astype(F32)

    for step in range(4):
        for third in range(3):
            qkv_piece(step, third).wait_send()
    for index in range(3):
        big_piece(index).wait_send()
    vec_copy.wait_send()
    for move in (o_move, g_move, back_move):
        swap_drain(*move)
    for move in (att_move, hg_move, act_move, qg_move, fx_move, qx_move):
        deal_drain(*move)
    for where, sent, got in (
        (cot_at, s.cot_sent, s.cot_got),
        (n1_at, s.n1_sent, s.n1_got),
        (n2_at, s.n2_sent, s.n2_got),
        (bg_at, s.bg_sent, s.bg_got),
    ):
        gather_drain(where, sent, got)
    for move in (sum_proj, sum_fc, sum_out, sum_qkv):
        spread_drain(move)


def hand_over(*refs):
    for source, target in zip(refs[:6], refs[7:13]):
        target[...] = source[...]
    for index, low in enumerate(refs[13:]):
        low[...] = refs[6][index : index + 1, : low.shape[1]]


def fused_layer(
    block_input,
    w_qkv,
    w_out,
    w_fc,
    w_proj,
    ln1_gain,
    ln1_bias,
    ln2_gain,
    ln2_bias,
    bias_q,
    bias_v,
    bias_out,
    bias_fc,
    bias_proj,
    cotangent,
):
    width = block_input.shape[4]
    rows = 2 * block_input.shape[3]
    ff = w_fc.shape[1]
    groups = lax.axis_size("ctx")
    shards = 2 * groups
    small = (ln1_gain, ln1_bias, ln2_gain, ln2_bias, bias_q, bias_v, bias_out, bias_proj, bias_fc)
    line = lax.broadcasted_iota(jnp.int32, (16, width // 2), 0)
    vectors, at = jnp.zeros(line.shape, BF16), 0
    for vector in small:
        for start in range(0, vector.shape[0], width // 2):
            piece = lax.broadcast_in_dim(vector[start : start + width // 2], line.shape, (1,))
            vectors = jnp.where(line == at, piece, vectors)
            at += 1
    shapes = layer_shapes(rows, width, ff, groups)
    names = tuple(shapes) + tuple(SEMAPHORES)
    scratch = [pltpu.VMEM(shape, kind) for shape, kind in shapes.values()]
    scratch += [pltpu.SemaphoreType.DMA((count,)) for count in SEMAPHORES.values()]
    in_vmem = pl.BlockSpec(memory_space=pltpu.VMEM)
    in_hbm = pl.BlockSpec(memory_space=pl.ANY)
    outs = pl.pallas_call(
        partial(layer_kernel, names),
        out_shape=(
            jax.ShapeDtypeStruct((rows, width), BF16),
            jax.ShapeDtypeStruct((rows, width), F32),
            jax.ShapeDtypeStruct((width // shards, 3 * width), F32),
            jax.ShapeDtypeStruct((width // shards, width), F32),
            jax.ShapeDtypeStruct((width // shards, ff), F32),
            jax.ShapeDtypeStruct((ff // shards, width), F32),
            jax.ShapeDtypeStruct((16, 128), F32),
        ),
        in_specs=[in_vmem] * 3 + [in_hbm] * 4,
        out_specs=(in_vmem,) * 7,
        scratch_shapes=scratch,
        compiler_params=pltpu.CompilerParams(
            collective_id=0, has_side_effects=True, vmem_limit_bytes=VMEM_BYTES
        ),
        cost_estimate=pl.CostEstimate(
            flops=14 * 10**9, bytes_accessed=30 * 10**6, transcendentals=5 * 10**6
        ),
    )(
        block_input.reshape(rows, width),
        cotangent.reshape(rows, width),
        vectors,
        w_qkv,
        w_out,
        w_fc,
        w_proj,
    )
    piece = width // shards
    wide = ff // shards
    results = pl.pallas_call(
        hand_over,
        out_shape=tuple(jax.ShapeDtypeStruct(out.shape, out.dtype) for out in outs[:6])
        + (jax.ShapeDtypeStruct((1, piece), F32),) * 8
        + (jax.ShapeDtypeStruct((1, wide), F32),),
        in_specs=[in_vmem] * 7,
        out_specs=(in_vmem,) * 15,
    )(*outs)
    block_output, input_grad, grad_qkv, grad_out, grad_fc, grad_proj = results[:6]
    lows = [result.reshape(-1) for result in results[6:]]
    return (
        block_output.reshape(block_input.shape),
        input_grad.reshape(block_input.shape),
        grad_qkv,
        grad_out,
        grad_fc,
        grad_proj,
        *lows[:7],
        lows[8],
        lows[7],
    )


def on_device(*arrays):
    width, ff = arrays[0].shape[4], arrays[3].shape[1]
    fits = (
        lax.axis_size("ctx") == HEADS
        and lax.axis_size("fsdp") == 2
        and arrays[0].shape[:4] == (1, 1, 2, 64)
        and (width, ff) == (1024, 4096)
    )
    return fused_layer(*arrays) if fits else general_layer(*arrays)


def solution(mesh):
    placed = (
        P("fsdp", "ctx", None, None, None),
        P("fsdp", None),
        P("fsdp", None),
        P("fsdp", None),
        P("fsdp", None),
        P("fsdp"),
        P("fsdp"),
        P("fsdp"),
        P("fsdp"),
        P("fsdp"),
        P("fsdp"),
        P("fsdp"),
        P("fsdp"),
        P("fsdp"),
        P("fsdp", "ctx", None, None, None),
    )
    return jax.shard_map(
        on_device,
        mesh=mesh,
        in_specs=placed,
        out_specs=(
            P("fsdp", "ctx", None, None, None),
            P("fsdp", "ctx", None, None, None),
            P(("ctx", "fsdp"), None),
            P(("ctx", "fsdp"), None),
            P(("ctx", "fsdp"), None),
            P(("ctx", "fsdp"), None),
            P(("ctx", "fsdp")),
            P(("ctx", "fsdp")),
            P(("ctx", "fsdp")),
            P(("ctx", "fsdp")),
            P(("ctx", "fsdp")),
            P(("ctx", "fsdp")),
            P(("ctx", "fsdp")),
            P(("ctx", "fsdp")),
            P(("ctx", "fsdp")),
        ),
        check_vma=False,
    )
```

```python
from functools import partial
from types import SimpleNamespace

import jax
import jax.numpy as jnp
from jax import lax
from jax.experimental import pallas as pl
from jax.experimental.pallas import tpu as pltpu
from jax.sharding import PartitionSpec as P

HEADS = 16
VMEM_BYTES = 127 * 2**19


def norm_parts(values):
    average = jnp.mean(values, -1, keepdims=True)
    centered = values - average
    variance = jnp.mean(centered * centered, -1, keepdims=True)
    inverse = lax.rsqrt(variance + 1e-05)
    return (centered * inverse, inverse)


def norm_grads(upstream, normalized, inverse, gain):
    scaled = upstream * gain
    inner_part = (
        scaled
        - jnp.mean(scaled, -1, keepdims=True)
        - normalized * jnp.mean(scaled * normalized, -1, keepdims=True)
    )
    return (inverse * inner_part, jnp.sum(upstream * normalized, 0), jnp.sum(upstream, 0))


def rows_product(left, right):
    return lax.dot_general(
        left, right, (((0,), (0,)), ((), ())), preferred_element_type=jnp.float32
    )


def right_transposed(left, weight):
    return lax.dot_general(
        left, weight, (((1,), (1,)), ((), ())), preferred_element_type=jnp.float32
    )


def split_heads(matrix):
    return matrix.reshape(matrix.shape[0], HEADS, -1)


def head_scores(queries, keys, allowed, scaling):
    scores = (
        jnp.einsum(
            "qhd,khd->hqk",
            split_heads(queries),
            split_heads(keys),
            preferred_element_type=jnp.float32,
        )
        * scaling
    )
    return jnp.where(allowed[None], scores, -1e30)


def general_layer(
    block_input,
    w_qkv,
    w_out,
    w_fc,
    w_proj,
    ln1_gain,
    ln1_bias,
    ln2_gain,
    ln2_bias,
    bias_q,
    bias_v,
    bias_out,
    bias_fc,
    bias_proj,
    cotangent,
):
    seq_count = block_input.shape[0]
    blk_rows = block_input.shape[3]
    width = block_input.shape[4]
    seq_rows = 2 * blk_rows
    row_count = seq_count * seq_rows
    groups = lax.axis_size("ctx")
    member = lax.axis_index("ctx")
    head_size = width // HEADS
    scaling = head_size ** (-0.5)
    full_rows = groups * seq_rows
    gathered = (
        lax.all_gather(w_qkv, "fsdp", axis=0, tiled=True),
        lax.all_gather(w_out, "fsdp", axis=0, tiled=True),
        lax.all_gather(w_fc, "fsdp", axis=0, tiled=True),
        lax.all_gather(w_proj, "fsdp", axis=0, tiled=True),
        lax.all_gather(ln1_gain, "fsdp", axis=0, tiled=True),
        lax.all_gather(ln1_bias, "fsdp", axis=0, tiled=True),
        lax.all_gather(ln2_gain, "fsdp", axis=0, tiled=True),
        lax.all_gather(ln2_bias, "fsdp", axis=0, tiled=True),
        lax.all_gather(bias_q, "fsdp", axis=0, tiled=True),
        lax.all_gather(bias_v, "fsdp", axis=0, tiled=True),
        lax.all_gather(bias_out, "fsdp", axis=0, tiled=True),
        lax.all_gather(bias_fc, "fsdp", axis=0, tiled=True),
        lax.all_gather(bias_proj, "fsdp", axis=0, tiled=True),
    )
    weight_qkv, weight_out, weight_fc, weight_proj = (
        gathered[0],
        gathered[1],
        gathered[2],
        gathered[3],
    )
    vectors = [piece.astype(jnp.float32) for piece in gathered[4:]]
    (
        gain_one,
        shift_one,
        gain_two,
        shift_two,
        query_bias,
        value_bias,
        out_bias,
        fc_bias,
        proj_bias,
    ) = vectors
    local_index = jnp.arange(seq_rows)
    own_block = jnp.where(local_index // blk_rows == 0, member, 2 * groups - 1 - member)
    own_pos = own_block * blk_rows + local_index % blk_rows
    every_index = jnp.arange(full_rows)
    every_owner = every_index // seq_rows
    every_block = jnp.where(
        every_index // blk_rows % 2 == 0, every_owner, 2 * groups - 1 - every_owner
    )
    every_pos = every_block * blk_rows + every_index % blk_rows
    allowed = every_pos[None, :] <= own_pos[:, None]
    inputs = block_input.reshape(row_count, width).astype(jnp.float32)
    normal_one, inverse_one = norm_parts(inputs)
    normed_one = (normal_one * gain_one + shift_one).astype(jnp.bfloat16)
    bias_all = jnp.concatenate([query_bias, jnp.zeros_like(query_bias), value_bias])
    projected = (
        jnp.dot(normed_one, weight_qkv, preferred_element_type=jnp.float32) + bias_all
    ).astype(jnp.bfloat16)
    queries = projected[:, :width]
    keys = projected[:, width : 2 * width]
    values = projected[:, 2 * width :]
    key_all = lax.all_gather(keys, "ctx", axis=0, tiled=True)
    value_all = lax.all_gather(values, "ctx", axis=0, tiled=True)
    scores = head_scores(queries, key_all, allowed, scaling)
    row_top = jnp.max(scores, -1, keepdims=True)
    log_sum = row_top + jnp.log(jnp.sum(jnp.exp(scores - row_top), -1, keepdims=True))
    probs_low = jnp.exp(scores - log_sum).astype(jnp.bfloat16)
    mixed = jnp.einsum(
        "hqk,khd->qhd", probs_low, split_heads(value_all), preferred_element_type=jnp.float32
    )
    mixed_rows = mixed.reshape(seq_rows, width)
    attended = mixed_rows.astype(jnp.bfloat16)
    residual = inputs + jnp.dot(attended, weight_out, preferred_element_type=jnp.float32) + out_bias
    normal_two, inverse_two = norm_parts(residual)
    normed_two = (normal_two * gain_two + shift_two).astype(jnp.bfloat16)
    hidden = jnp.dot(normed_two, weight_fc, preferred_element_type=jnp.float32) + fc_bias
    activated, gelu_pullback = jax.vjp(partial(jax.nn.gelu, approximate=True), hidden)
    activated_low = activated.astype(jnp.bfloat16)
    result = (
        residual
        + jnp.dot(activated_low, weight_proj, preferred_element_type=jnp.float32)
        + proj_bias
    )
    block_output = result.astype(jnp.bfloat16).reshape(block_input.shape)
    weight_qkv, weight_out, weight_fc, weight_proj, gain_low_one, gain_low_two = (
        lax.all_gather(w_qkv, "fsdp", axis=0, tiled=True),
        lax.all_gather(w_out, "fsdp", axis=0, tiled=True),
        lax.all_gather(w_fc, "fsdp", axis=0, tiled=True),
        lax.all_gather(w_proj, "fsdp", axis=0, tiled=True),
        lax.all_gather(ln1_gain, "fsdp", axis=0, tiled=True),
        lax.all_gather(ln2_gain, "fsdp", axis=0, tiled=True),
    )
    gain_one = gain_low_one.astype(jnp.float32)
    gain_two = gain_low_two.astype(jnp.float32)
    out_grad_low = cotangent.reshape(row_count, width)
    upstream = out_grad_low.astype(jnp.float32)
    grad_proj = rows_product(activated_low, out_grad_low)
    grad_proj_bias = jnp.sum(upstream, 0)
    hidden_grad = gelu_pullback(right_transposed(out_grad_low, weight_proj))[0].astype(jnp.bfloat16)
    grad_fc = rows_product(normed_two, hidden_grad)
    grad_fc_bias = jnp.sum(hidden_grad.astype(jnp.float32), 0)
    residual_part, grad_gain_two, grad_shift_two = norm_grads(
        right_transposed(hidden_grad, weight_fc), normal_two, inverse_two, gain_two
    )
    residual_grad = upstream + residual_part
    branch_grad = residual_grad.astype(jnp.bfloat16)
    grad_out = rows_product(attended, branch_grad)
    grad_out_bias = jnp.sum(branch_grad.astype(jnp.float32), 0)
    attended_grad = right_transposed(branch_grad, weight_out).astype(jnp.bfloat16)
    key_all = lax.all_gather(keys, "ctx", axis=0, tiled=True)
    value_all = lax.all_gather(values, "ctx", axis=0, tiled=True)
    scores = head_scores(queries, key_all, allowed, scaling)
    probs = jnp.exp(scores - log_sum)
    prob_grad = jnp.einsum(
        "qhd,khd->hqk",
        split_heads(attended_grad),
        split_heads(value_all),
        preferred_element_type=jnp.float32,
    )
    inner_sum = jnp.sum(probs * prob_grad, -1, keepdims=True)
    score_grad = (probs * (prob_grad - inner_sum)).astype(jnp.bfloat16)
    query_part = (
        jnp.einsum(
            "hqk,khd->qhd", score_grad, split_heads(key_all), preferred_element_type=jnp.float32
        )
        * scaling
    )
    query_grads = query_part.reshape(seq_rows, width)
    probs_low = probs.astype(jnp.bfloat16)
    query_heads = split_heads(queries)
    grad_heads = split_heads(attended_grad)

    def key_terms(
        start,
        count,
        score_grad=score_grad,
        probs_low=probs_low,
        query_heads=query_heads,
        grad_heads=grad_heads,
    ):
        key_part = (
            jnp.einsum("hqk,qhd->khd", score_grad, query_heads, preferred_element_type=jnp.float32)
            * scaling
        )
        value_part = jnp.einsum(
            "hqk,qhd->khd", probs_low, grad_heads, preferred_element_type=jnp.float32
        )
        return jnp.concatenate(
            [key_part.reshape(count, width), value_part.reshape(count, width)], 1
        )

    own_terms = lax.psum_scatter(
        key_terms(jnp.int32(0), lax.axis_size("ctx") * seq_rows),
        "ctx",
        scatter_dimension=0,
        tiled=True,
    )
    key_grads = own_terms[:, :width]
    value_grads = own_terms[:, width:]
    qkv_grad = jnp.concatenate([query_grads, key_grads, value_grads], 1).astype(jnp.bfloat16)
    grad_qkv = rows_product(normed_one, qkv_grad)
    qkv_sums = jnp.sum(qkv_grad.astype(jnp.float32), 0)
    grad_query_bias = qkv_sums[:width]
    grad_value_bias = qkv_sums[2 * width :]
    input_part, grad_gain_one, grad_shift_one = norm_grads(
        right_transposed(qkv_grad, weight_qkv), normal_one, inverse_one, gain_one
    )
    input_grad = (residual_grad + input_part).reshape(block_input.shape)
    sharded = (
        lax.psum_scatter(grad_qkv, ("ctx", "fsdp"), scatter_dimension=0, tiled=True),
        lax.psum_scatter(grad_out, ("ctx", "fsdp"), scatter_dimension=0, tiled=True),
        lax.psum_scatter(grad_fc, ("ctx", "fsdp"), scatter_dimension=0, tiled=True),
        lax.psum_scatter(grad_proj, ("ctx", "fsdp"), scatter_dimension=0, tiled=True),
        lax.psum_scatter(grad_gain_one, ("ctx", "fsdp"), scatter_dimension=0, tiled=True),
        lax.psum_scatter(grad_shift_one, ("ctx", "fsdp"), scatter_dimension=0, tiled=True),
        lax.psum_scatter(grad_gain_two, ("ctx", "fsdp"), scatter_dimension=0, tiled=True),
        lax.psum_scatter(grad_shift_two, ("ctx", "fsdp"), scatter_dimension=0, tiled=True),
        lax.psum_scatter(grad_query_bias, ("ctx", "fsdp"), scatter_dimension=0, tiled=True),
        lax.psum_scatter(grad_value_bias, ("ctx", "fsdp"), scatter_dimension=0, tiled=True),
        lax.psum_scatter(grad_out_bias, ("ctx", "fsdp"), scatter_dimension=0, tiled=True),
        lax.psum_scatter(grad_fc_bias, ("ctx", "fsdp"), scatter_dimension=0, tiled=True),
        lax.psum_scatter(grad_proj_bias, ("ctx", "fsdp"), scatter_dimension=0, tiled=True),
    )
    return (
        block_output,
        input_grad,
        sharded[0],
        sharded[1],
        sharded[2],
        sharded[3],
        sharded[4],
        sharded[5],
        sharded[6],
        sharded[7],
        sharded[8],
        sharded[9],
        sharded[10],
        sharded[11],
        sharded[12],
    )


MESH = pl.DeviceIdType.MESH
BF16, F32 = jnp.bfloat16, jnp.float32
PLANE = 4
NEG = -1e30


def remote(src, dst, sent, received, device):
    return pltpu.make_async_remote_copy(
        src_ref=src,
        dst_ref=dst,
        send_sem=sent,
        recv_sem=received,
        device_id=device,
        device_id_type=MESH,
    )


def dot(left, right):
    return jnp.dot(left, right, preferred_element_type=F32)


def low_lanes(rows):
    return lax.broadcasted_iota(jnp.int32, (rows, 128), 1) < 64


def swap(block):
    return pltpu.roll(block, 64, 1)


def pack_pair(pair):
    half = pair.shape[0] // 2
    low = low_lanes(half)
    top, bottom = pair[:half], pair[half:]
    return jnp.where(low, top, swap(bottom)), jnp.where(low, swap(top), bottom)


def unpack_pair(even, odd):
    low = low_lanes(even.shape[0])
    return jnp.concatenate(
        [jnp.where(low, even, swap(odd)), jnp.where(low, swap(even), odd)], 0
    )


def part(index, size):
    return pl.ds(pl.multiple_of(index * size, size), size)


def layer_shapes(rows, width, ff, groups):
    members = 2 * PLANE
    layers = groups // PLANE
    tokens = members * rows
    half = rows // 2
    keys = groups * half
    share = width // members
    return dict(
        w_qkv=((width, 3 * width), BF16),
        w_out=((width, width), BF16),
        w_fc=((width, ff), BF16),
        w_proj=((ff, width), BF16),
        vec_low=((2, 16, width // 2), BF16),
        vec=((2, 16, width // 2), F32),
        row=((8, width), F32),
        cot_all=((members, rows, width), BF16),
        n1=((rows, width), BF16),
        n1_t=((width, tokens), BF16),
        stage=((groups, 3, half, 128), BF16),
        qkv=((3, keys, 128), BF16),
        kv_roll=((2, keys, 128), BF16),
        q_low=((2, keys, 128), BF16),
        g_low=((2, keys, 128), BF16),
        q_t=((128, keys), BF16),
        g_t=((128, keys), BF16),
        stat=((2, 2, keys, 128), F32),
        mixed=((keys, 128), F32),
        scores=((256, 9 * 256), F32),
        dq=((2, keys, 128), F32),
        o_out=((groups, half, 128), BF16),
        o_in=((groups, half, 128), BF16),
        att=((rows, width), BF16),
        att_t=((layers, members, width // members // layers, rows), BF16),
        att_all=((layers, width // members // layers, tokens), BF16),
        res=((rows, width), F32),
        n2=((rows, width), BF16),
        n2_t=((width, tokens), BF16),
        fc_t=((ff // members, width), BF16),
        bias_t=((ff // members, 128), F32),
        proj_own=((ff // members, width), BF16),
        act_all=((ff // members, tokens), BF16),
        hg_all=((ff // members, tokens), BF16),
        acc_o=((rows, width), F32),
        acc_d=((rows, width), F32),
        res_grad=((rows, width), F32),
        bg_all=((members, rows, width), BF16),
        g_out=((groups, half, 128), BF16),
        g_in=((keys, 128), BF16),
        back=((groups, 3, half, 128), BF16),
        qg=((rows, 3 * width), BF16),
        qg_out=((members, rows, 3 * share), BF16),
        qg_all=((members, rows, 3 * share), BF16),
        fc_own=((width // layers, ff // members), F32),
        qkv_own=((width // layers, 3 * share), F32),
        fc_x=((members, width // layers // members, ff // members), BF16),
        fc_y=((members, width // layers // members, ff // members), BF16),
        qkv_x=((members, width // layers // members, 3 * share), BF16),
        qkv_y=((members, width // layers // members, 3 * share), BF16),
        sums=((16, width), F32),
        sums_out=((layers, 16, width // layers), F32),
        sums_in=((3, 16, width // layers), F32),
        sums_all=((members, 16, width // layers), F32),
    )


SEMAPHORES = dict(
    local=4,
    w_sent=4,
    w_got=7,
    vec_sent=1,
    vec_got=1,
    swap_sent=5,
    swap_got=5,
    cot_sent=1,
    cot_got=5,
    n1_sent=1,
    n1_got=5,
    n2_sent=1,
    n2_got=5,
    bg_sent=1,
    bg_got=5,
    deal_sent=4,
    deal_got=4,
    sum_sent=4,
    sum_got=8,
    low_sent=2,
    low_got=2,
)


def settle(ref, semaphore):
    pltpu.make_async_copy(ref, ref, semaphore).wait()


def layer_kernel(names, *refs):
    x_ref, cot_ref, vec_ref, wq_hbm, wo_hbm, wf_hbm, wp_hbm = refs[:7]
    y_ref, gx_ref, gqkv_ref, gout_ref, gfc_ref, gproj_ref, gvec_ref = refs[7:14]
    s = SimpleNamespace(**dict(zip(names, refs[14:])))
    rows, width = x_ref.shape
    ff = s.w_fc.shape[1]
    half = rows // 2
    groups = s.stage.shape[0]
    members = 2 * PLANE
    layers = groups // PLANE
    tokens = members * rows
    keys = groups * half
    chunk = ff // members
    share = width // members
    scaling = float(width // HEADS) ** (-0.5)
    factor = scaling * 1.4426950408889634
    me = lax.axis_index("ctx")
    core = lax.axis_index("fsdp")
    other = 1 - core
    layer, place = me // PLANE, me % PLANE
    member = place * 2 + core
    twin = (me, other)

    barrier = pltpu.get_barrier_semaphore()
    for step in range(1, groups):
        pl.semaphore_signal(
            barrier, inc=1, device_id=((me + step) % groups, core), device_id_type=MESH
        )
    for step in range(PLANE):
        pl.semaphore_signal(
            barrier,
            inc=1,
            device_id=(layer * PLANE + (place + step) % PLANE, other),
            device_id_type=MESH,
        )
    pl.semaphore_wait(barrier, groups - 1 + PLANE)

    def at_member(index):
        return (layer * PLANE + index // 2, index % 2)

    def top_rows(ref, source):
        count = source.shape[0]
        return ref.at[pl.ds(pl.multiple_of(core * count, count), count)]

    def peer_rows(ref, source):
        count = source.shape[0]
        return ref.at[pl.ds(pl.multiple_of(other * count, count), count)]


    def order(step):
        return (layer + 2 + step) % 4

    def order_in(step):
        return (place + 1 + step) % 4

    pltpu.make_async_copy(wq_hbm, top_rows(s.w_qkv, wq_hbm), s.local.at[0]).start()

    def qkv_piece(step, third):
        columns = part(third * 4 + order(step), 256)
        return remote(
            wq_hbm.at[:, columns],
            top_rows(s.w_qkv, wq_hbm).at[:, columns],
            s.w_sent.at[0],
            s.w_got.at[step],
            twin,
        )

    vec_copy = remote(vec_ref, s.vec_low.at[core], s.vec_sent.at[0], s.vec_got.at[0], twin)
    vec_copy.start()
    for step in range(4):
        for third in range(3):
            qkv_piece(step, third).start()
    big = ((wo_hbm, s.w_out), (wf_hbm, s.w_fc), (wp_hbm, s.w_proj))

    def big_piece(index):
        source, target = big[index]
        return remote(
            source, top_rows(target, source), s.w_sent.at[1 + index], s.w_got.at[4 + index], twin
        )

    def big_local(index):
        source, target = big[index]
        return pltpu.make_async_copy(source, top_rows(target, source), s.local.at[1 + index])

    def gather_copy(where, sent, got, slot, index, device):
        return remote(where(slot), where(slot), sent.at[0], got.at[index], device)

    def gather_start(where, sent, got):
        for step in range(1, PLANE):
            peer = layer * PLANE + (place + step) % PLANE
            gather_copy(where, sent, got, member, place, (peer, core)).start()
        gather_copy(where, sent, got, member, PLANE, twin).start()

    def gather_forward(where, sent, got):
        for step in range(1, PLANE):
            peer = (place + step) % PLANE
            settle(where(peer * 2 + core), got.at[peer])
            gather_copy(where, sent, got, peer * 2 + core, PLANE, twin).start()

    def gather_finish(where, sent, got):
        settle(where(0, PLANE), got.at[PLANE])

    def gather_drain(where, sent, got):
        settle(where(0, 2 * PLANE - 1), sent.at[0])

    def cot_at(slot, count=None):
        return s.cot_all.at[slot if count is None else pl.ds(slot, count)]

    def bg_at(slot, count=None):
        return s.bg_all.at[slot if count is None else pl.ds(slot, count)]

    def columns_at(ref, slot, count):
        return ref.at[:, part(slot, rows) if count is None else pl.ds(slot * rows, count * rows)]

    def n1_at(slot, count=None):
        return columns_at(s.n1_t, slot, count)

    def n2_at(slot, count=None):
        return columns_at(s.n2_t, slot, count)

    def deal_copy(source, target, number, index):
        return remote(
            source(index),
            target(member),
            s.deal_sent.at[number],
            s.deal_got.at[number],
            at_member(index),
        )

    def deal_own(source, target, number):
        return pltpu.make_async_copy(source(member), target(member), s.deal_got.at[number])

    def deal_start(source, target, number):
        for step in range(1, members):
            deal_copy(source, target, number, (member + step) % members).start()
        deal_own(source, target, number).start()

    def deal_wait(source, target, number):
        settle(target(None), s.deal_got.at[number])

    def deal_drain(source, target, number):
        settle(source(None), s.deal_sent.at[number])

    def seven(index):
        return pl.ds(0, members - 1) if index is None else index

    def whole(index):
        return slice(None) if index is None else index

    def lanes(index):
        return slice(None) if index is None else part(index, rows)

    def swap_one(source, target, number, index):
        @pl.when(index == me)
        def _():
            pltpu.make_async_copy(source(index), target(me), s.swap_got.at[number]).start()

        @pl.when(index != me)
        def _():
            remote(
                source(index),
                target(me),
                s.swap_sent.at[number],
                s.swap_got.at[number],
                (index, core),
            ).start()

    def swap_wait(source, target, number):
        settle(target(None), s.swap_got.at[number])

    def swap_drain(source, target, number):
        settle(source(None), s.swap_sent.at[number])

    def others(index):
        return pl.ds(0, groups - 1) if index is None else index

    def block(index):
        return slice(None) if index is None else part(index, half)

    qkv_move = (lambda h: s.stage.at[others(h)], lambda i: s.qkv.at[:, block(i)], 0)
    o_move = (lambda h: s.o_out.at[others(h)], lambda h: s.o_in.at[whole(h)], 1)
    g_move = (lambda h: s.g_out.at[others(h)], lambda i: s.g_in.at[block(i)], 2)
    kv_back = (
        lambda h: s.stage.at[others(h), pl.ds(1, 2)],
        lambda h: s.back.at[whole(h), pl.ds(1, 2)],
        3,
    )
    q_back = (lambda h: s.stage.at[others(h), 0], lambda h: s.back.at[whole(h), 0], 4)
    att_move = (lambda g: s.att_t.at[:, seven(g)], lambda g: s.att_all.at[:, :, lanes(g)], 0)
    qg_move = (lambda g: s.qg_out.at[seven(g)], lambda g: s.qg_all.at[whole(g)], 1)
    fx_move = (lambda g: s.fc_x.at[seven(g)], lambda g: s.fc_y.at[whole(g)], 2)
    qx_move = (lambda g: s.qkv_x.at[seven(g)], lambda g: s.qkv_y.at[whole(g)], 3)

    def vec_row(index):
        return jnp.concatenate([s.vec[0, index : index + 1, :], s.vec[1, index : index + 1, :]], 1)

    s.cot_all[member] = cot_ref[...]
    settle(vec_ref, s.vec_got.at[0])
    s.vec[core] = vec_ref[...].astype(F32)
    s.vec[other] = s.vec_low[other].astype(F32)
    s.row[0:1, :] = vec_row(4)
    s.row[1:2, :] = vec_row(5)
    for quarter in range(4):
        at = 8 + quarter % 2 * 2
        s.row[4 + quarter : 5 + quarter, :] = jnp.concatenate(
            [s.vec[quarter // 2, at : at + 1, :], s.vec[quarter // 2, at + 1 : at + 2, :]], 1
        )
    inputs = x_ref[...].astype(F32)
    normal, _ = norm_parts(inputs)
    normed = (normal * vec_row(0) + vec_row(1)).astype(BF16)
    s.n1[...] = normed
    s.n1_t[:, part(member, rows)] = normed.astype(F32).T.astype(BF16)
    pltpu.make_async_copy(wq_hbm, top_rows(s.w_qkv, wq_hbm), s.local.at[0]).wait()

    for step in range(4):
        four = order(step)
        settle(peer_rows(s.w_qkv, wq_hbm).at[:, pl.ds(0, 768)], s.w_got.at[step])
        for third in range(3):
            columns = part(third * 4 + four, 256)
            product = dot(s.n1[...], s.w_qkv[:, columns])
            if third == 0:
                product = product + s.row[0:1, part(four, 256)]
            if third == 2:
                product = product + s.row[1:2, part(four, 256)]
            for pair in range(2):
                even, odd = pack_pair(product[:, pair * 128 : pair * 128 + 128])
                s.stage[four * 4 + 2 * pair, third] = even.astype(BF16)
                s.stage[four * 4 + 2 * pair + 1, third] = odd.astype(BF16)
        for head in range(4):
            swap_one(*qkv_move, four * 4 + order_in(head))
    gather_start(cot_at, s.cot_sent, s.cot_got)
    for index in range(3):
        big_piece(index).start()
        big_local(index).start()

    swap_wait(*qkv_move)
    low_all = low_lanes(keys)
    query = s.qkv[0].astype(F32)
    s.q_low[0] = jnp.where(low_all, query, 0.0).astype(BF16)
    s.q_low[1] = jnp.where(low_all, swap(query), 0.0).astype(BF16)
    s.q_t[...] = query.T.astype(BF16)
    s.kv_roll[0] = swap(s.qkv[1].astype(F32)).astype(BF16)
    s.kv_roll[1] = swap(s.qkv[2].astype(F32)).astype(BF16)

    tile = 256
    per_tile = tile // half
    low_tile = low_lanes(tile)
    row_at = lax.broadcasted_iota(jnp.int32, (tile, tile), 0)
    col_at = lax.broadcasted_iota(jnp.int32, (tile, tile), 1)

    def late(index):
        return index + (per_tile - 1 - 2 * (index // half)) * half

    masks = (col_at <= row_at, late(col_at) <= late(row_at))

    def key_block(region, at):
        return s.qkv[1, at, :] if region == 0 else s.kv_roll[0, at, :]

    def value_block(region, at):
        return s.qkv[2, at, :] if region == 0 else s.kv_roll[1, at, :]

    n_tiles = keys // tile

    def span(start, count=1):
        return slice(start * tile, (start + count) * tile)

    def score_block(queries, region, first, count, column, masked):
        scores = right_transposed(queries, key_block(region, span(first, count)))
        if masked:
            scores = jnp.where(masks[region], scores, NEG)
        s.scores[:, span(column, count)] = scores
        return scores

    def fold(values, combine):
        out = values[:, :128]
        for start in range(128, values.shape[1], 128):
            out = combine(out, values[:, start : start + 128])
        return out

    def softmax_rows(side, blocks, at):
        queries = s.q_low[side, at, :]
        top = None
        for block in blocks:
            high = fold(score_block(queries, *block), jnp.maximum)
            top = high if top is None else jnp.maximum(top, high)
        top = jnp.max(top, 1, keepdims=True) * factor
        total, mix = None, None
        for region, first, count, column, _ in blocks:
            probs = jnp.exp2(s.scores[:, span(column, count)] * factor - top)
            folded = fold(probs, jnp.add)
            total = folded if total is None else total + folded
            more = dot(probs.astype(BF16), value_block(region, span(first, count)))
            mix = more if mix is None else mix + more
        total = jnp.sum(total, 1, keepdims=True)
        s.stat[0, side, at, :] = jnp.broadcast_to(top + jnp.log2(total), (tile, 128))
        return mix / total

    def attend(index):
        at = span(index)
        early = [(0, index, 1, 0, True)]
        if index:
            early.append((0, 0, index, 1, False))
        late_blocks = [(1, index, 1, index + 1, True)]
        if index + 1 < n_tiles:
            late_blocks.append((1, index + 1, n_tiles - 1 - index, index + 2, False))
        late_blocks.append((0, 0, n_tiles, n_tiles + 1, False))
        one = softmax_rows(0, early, at)
        two = softmax_rows(1, late_blocks, at)
        out = jnp.where(low_tile, one, swap(two))
        s.mixed[at, :] = out
        s.o_out[pl.ds(index * per_tile, per_tile)] = out.astype(BF16).reshape(per_tile, half, 128)
        for step in range(per_tile):
            swap_one(*o_move, index * per_tile + order_in(step))

    for index in range(n_tiles):
        attend(index)

    for index in range(3):
        settle(peer_rows(big[index][1], big[index][0]), s.w_got.at[4 + index])
        big_local(index).wait()
    quarters = ff // width
    piece = width // members

    curve = 0.7978845608028654

    def features(index):
        return [part(quarter * members + index, piece) for quarter in range(quarters)]

    mine = features(member)
    s.proj_own[...] = jnp.concatenate([s.w_proj[at, :] for at in mine], 0)
    for quarter, at in enumerate(mine):
        into = slice(quarter * piece, quarter * piece + piece)
        s.fc_t[into, :] = s.w_fc[:, at].astype(F32).T.astype(BF16)
        bias = s.row[4 + quarter : 5 + quarter, part(member, piece)]
        s.bias_t[into, :] = jnp.broadcast_to(bias, (128, piece)).T
    swap_wait(*o_move)
    for pair in range(HEADS // 2):
        columns = slice(pair * 128, pair * 128 + 128)
        s.att[:, columns] = unpack_pair(
            s.o_in[2 * pair].astype(F32), s.o_in[2 * pair + 1].astype(F32)
        ).astype(BF16)
    turned = s.att[...].astype(F32).T.astype(BF16)
    s.att_t[...] = turned.reshape(s.att_t.shape)
    def project(index, _):
        at = part(index, 256)
        s.acc_d[:, at] = dot(s.att[...], s.w_out[:, at])
        return 0

    lax.fori_loop(0, width // 256, project, 0)
    s.res[...] = x_ref[...].astype(F32) + s.acc_d[...] + vec_row(6)
    normal, _ = norm_parts(s.res[...])
    normed = (normal * vec_row(2) + vec_row(3)).astype(BF16)
    s.n2[...] = normed
    s.n2_t[:, part(member, rows)] = normed.astype(F32).T.astype(BF16)
    gather_start(n2_at, s.n2_sent, s.n2_got)
    s.acc_o[...] = jnp.zeros_like(s.acc_o)
    s.acc_d[...] = jnp.zeros_like(s.acc_d)
    s.sums[...] = jnp.zeros_like(s.sums)


    def gelu_parts(hidden):
        square = hidden * hidden
        bend = jnp.tanh(curve * hidden * (1.0 + 0.044715 * square))
        rise = 0.5 * (1.0 + bend)
        slope = rise + 0.5 * hidden * (1.0 - bend * bend) * (
            curve * (1.0 + 3.0 * 0.044715 * square)
        )
        return hidden * rise, slope

    def feed(index, _):
        places = features(index)
        bias = jnp.concatenate(
            [s.row[4 + quarter : 5 + quarter, part(index, piece)] for quarter in range(quarters)], 1
        )
        into = jnp.concatenate([s.w_fc[:, at] for at in places], 1)
        back = jnp.concatenate([s.w_proj[at, :] for at in places], 0)
        hidden = dot(s.n2[...], into) + bias
        upstream = right_transposed(cot_ref[...], back)
        active, slope = gelu_parts(hidden)
        active = active.astype(BF16)
        grad = (upstream * slope).astype(BF16)
        s.acc_o[...] += dot(active, back)
        s.acc_d[...] += right_transposed(grad, into)
        total = jnp.sum(grad.astype(F32), 0, keepdims=True)
        for quarter in range(quarters):
            s.sums[8 + quarter : 9 + quarter, part(index, piece)] = total[
                :, quarter * piece : quarter * piece + piece
            ]
        return 0

    lax.fori_loop(0, members, feed, 0)
    upstream = cot_ref[...].astype(F32)
    normal, inverse = norm_parts(s.res[...])
    step_grad, gain_grad, shift_grad = norm_grads(s.acc_d[...], normal, inverse, vec_row(2))
    s.sums[2:3, :] = gain_grad[None]
    s.sums[3:4, :] = shift_grad[None]
    s.sums[7:8, :] = jnp.sum(upstream, 0, keepdims=True)
    res_grad = upstream + step_grad
    s.res_grad[...] = res_grad
    branch = res_grad.astype(BF16)
    s.bg_all[member] = branch
    s.sums[6:7, :] = jnp.sum(branch.astype(F32), 0, keepdims=True)
    for step in range(4):
        four = order(step)
        product = right_transposed(s.bg_all[member], s.w_out[part(four, 256), :])
        for pair in range(2):
            even, odd = pack_pair(product[:, pair * 128 : pair * 128 + 128])
            s.g_out[four * 4 + 2 * pair] = even.astype(BF16)
            s.g_out[four * 4 + 2 * pair + 1] = odd.astype(BF16)
        for head in range(4):
            swap_one(*g_move, four * 4 + order_in(head))
    y_ref[...] = (s.res[...] + s.acc_o[...] + vec_row(7)).astype(BF16)
    gather_start(bg_at, s.bg_sent, s.bg_got)
    deal_start(*att_move)
    gather_forward(cot_at, s.cot_sent, s.cot_got)
    gather_forward(n2_at, s.n2_sent, s.n2_got)
    swap_drain(*qkv_move)

    beside = layer + 1 - 2 * (layer % 2)
    beyond = (layer + 2) % layers
    across = (beside + 2) % layers

    def spread_copy(move, slot, target):
        buffer_out, buffer_in, number = move
        return remote(
            buffer_out(slot),
            buffer_in(slot),
            s.sum_sent.at[number],
            s.sum_got.at[2 * number + (slot + 1) // 2],
            (target * PLANE + place, core),
        )

    def spread_prepare(move, product, own_ref):
        for slot, index in enumerate((across, beside, beyond)):
            move[0](slot)[...] = product(index).astype(BF16)
        own_ref[...] = product(layer)

    def spread_start(move):
        for slot in range(2):
            spread_copy(move, slot, beside).start()

    def spread(move, product, own_ref):
        for slot, index in enumerate((across, beside, beyond)):
            move[0](slot)[...] = product(index).astype(BF16)
            if slot < 2:
                spread_copy(move, slot, beside).start()
        own_ref[...] = product(layer)

    def spread_on(move):
        settle(move[1](0), s.sum_got.at[2 * move[2]])
        pair = move[0](2)[...].astype(F32) + move[1](0)[...].astype(F32)
        move[0](2)[...] = pair.astype(BF16)
        spread_copy(move, 2, beyond).start()

    def collect(move, own_ref):
        settle(move[1](1, 2), s.sum_got.at[2 * move[2] + 1])
        own_ref[...] += move[1](1)[...].astype(F32) + move[1](2)[...].astype(F32)

    def spread_drain(move):
        settle(move[0](0, 3), s.sum_sent.at[move[2]])

    proj_rows = ff // members // layers
    out_rows = share // layers
    fc_rows = width // layers

    def rows_of(ref, start, size, columns=slice(None)):
        return lambda slot, count=1: ref.at[pl.ds(start + slot * size, count * size), columns]

    sum_proj = (rows_of(s.w_proj, 0, proj_rows), rows_of(s.w_proj, 512, proj_rows), 0)
    sum_out = (rows_of(s.w_proj, 1024, out_rows), rows_of(s.w_proj, 1152, out_rows), 1)
    sum_fc = (
        rows_of(s.w_fc, 0, fc_rows, pl.ds(0, chunk)),
        rows_of(s.w_fc, 0, fc_rows, pl.ds(chunk, chunk)),
        2,
    )
    sum_qkv = (
        rows_of(s.w_fc, 0, fc_rows, pl.ds(2 * chunk, 3 * share)),
        rows_of(s.w_fc, 0, fc_rows, pl.ds(3 * chunk, 3 * share)),
        3,
    )

    def feed_again(index, _):
        at = part(index, 2 * rows)
        hidden = dot(s.fc_t[...], s.n2_t[:, at]) + jnp.concatenate([s.bias_t[...]] * 2, 1)
        cotangents = s.cot_all[pl.ds(2 * index, 2)].reshape(2 * rows, width)
        upstream = right_transposed(s.proj_own[...], cotangents)
        active, slope = gelu_parts(hidden)
        s.act_all[:, at] = active.astype(BF16)
        s.hg_all[:, at] = (upstream * slope).astype(BF16)
        return 0

    def grads_of_feed():
        gather_finish(cot_at, s.cot_sent, s.cot_got)
        gather_finish(n2_at, s.n2_sent, s.n2_got)
        lax.fori_loop(0, PLANE, feed_again, 0)
        spread_prepare(
            sum_proj,
            lambda i: dot(s.act_all[part(i, proj_rows), :], s.cot_all[...].reshape(tokens, width)),
            gproj_ref,
        )
        spread_prepare(
            sum_fc,
            lambda i: right_transposed(s.n2_t[part(i, fc_rows), :], s.hg_all[...]),
            s.fc_own,
        )

    def grad_of_out():
        gather_finish(bg_at, s.bg_sent, s.bg_got)
        deal_wait(*att_move)
        spread(
            sum_out,
            lambda i: dot(s.att_all[i], s.bg_all[...].reshape(tokens, width)),
            gout_ref,
        )

    grads_of_feed()
    swap_wait(*g_move)
    upstream = s.g_in[...].astype(F32)
    s.g_low[0] = jnp.where(low_all, upstream, 0.0).astype(BF16)
    s.g_low[1] = jnp.where(low_all, swap(upstream), 0.0).astype(BF16)
    s.g_t[...] = upstream.T.astype(BF16)
    inner = upstream * s.mixed[...]
    for side in range(2):
        kept = jnp.where(low_all == (side == 0), inner, 0.0)
        s.stat[1, side] = jnp.broadcast_to(jnp.sum(kept, 1, keepdims=True), (keys, 128))
    s.dq[...] = jnp.zeros_like(s.dq)

    def wide(block):
        return jnp.concatenate([block] * (tile // 128), 1)

    def back_tile(side, region, at_q, at_k, masked):
        scores = right_transposed(s.q_low[side, at_q, :], key_block(region, at_k))
        probs = jnp.exp2(scores * factor - wide(s.stat[0, side, at_q, :]))
        if masked:
            probs = jnp.where(masks[region], probs, 0.0)
        prob_grad = right_transposed(s.g_low[side, at_q, :], value_block(region, at_k))
        score_grad = (probs * (prob_grad - wide(s.stat[1, side, at_q, :]))).astype(BF16)
        head = slice(side * 64, side * 64 + 64)
        s.dq[side, at_q, :] += dot(score_grad, key_block(region, at_k))
        return dot(s.q_t[head, at_q], score_grad), dot(s.g_t[head, at_q], probs.astype(BF16))

    def attend_back(index):
        at = span(index)
        early = [(0, 0, k, k == index) for k in range(index, n_tiles)]
        early += [(1, 0, k, False) for k in range(n_tiles)]
        late_pairs = [(1, 1, k, k == index) for k in range(index + 1)]
        grads = []
        for pairs in (early, late_pairs):
            both = [
                back_tile(side, region, span(k), at, masked) for side, region, k, masked in pairs
            ]
            grads.append([sum(parts) for parts in zip(*both)])
        for third, scale in ((1, scaling), (2, 1.0)):
            rows_t = jnp.concatenate([grads[0][third - 1], grads[1][third - 1]], 0)
            s.stage[pl.ds(index * per_tile, per_tile), third] = (
                (rows_t.T * scale).astype(BF16).reshape(per_tile, half, 128)
            )
        for step in range(per_tile):
            swap_one(*kv_back, index * per_tile + order_in(step))

    spread_start(sum_proj)
    attend_back(0)
    attend_back(1)
    attend_back(2)
    attend_back(3)
    out = jnp.where(low_all, s.dq[0], swap(s.dq[1])) * scaling
    s.stage[:, 0] = out.astype(BF16).reshape(groups, half, 128)
    for step in range(4):
        for head in range(4):
            swap_one(*q_back, order(step) * 4 + order_in(head))
    spread_start(sum_fc)
    gather_start(n1_at, s.n1_sent, s.n1_got)
    gather_forward(bg_at, s.bg_sent, s.bg_got)
    grad_of_out()
    spread_on(sum_proj)

    swap_wait(*kv_back)
    swap_wait(*q_back)
    for pair in range(HEADS // 2):
        for third in range(3):
            block = unpack_pair(
                s.back[2 * pair, third].astype(F32), s.back[2 * pair + 1, third].astype(F32)
            ).astype(BF16)
            s.qg_out[pair, :, third * 128 : third * 128 + 128] = block
            columns = slice(third * width + pair * 128, third * width + pair * 128 + 128)
            s.qg[:, columns] = block
    deal_start(*qg_move)
    s.sums[4:5, :] = jnp.sum(s.qg[:, :width].astype(F32), 0, keepdims=True)
    s.sums[5:6, :] = jnp.sum(s.qg[:, 2 * width :].astype(F32), 0, keepdims=True)

    def project_back(index, _):
        s.acc_d[:, part(index, 256)] = right_transposed(s.qg[...], s.w_qkv[part(index, 256), :])
        return 0

    lax.fori_loop(0, width // 256, project_back, 0)
    normal, inverse = norm_parts(x_ref[...].astype(F32))
    step_grad, gain_grad, shift_grad = norm_grads(s.acc_d[...], normal, inverse, vec_row(0))
    s.sums[0:1, :] = gain_grad[None]
    s.sums[1:2, :] = shift_grad[None]
    gx_ref[...] = s.res_grad[...] + step_grad

    lanes_of_layer = width // layers
    for index in range(layers):
        columns = slice(index * lanes_of_layer, (index + 1) * lanes_of_layer)
        s.sums_out[index, 0:8, :] = s.sums[0:8, columns]
        for quarter in range(layers):
            columns = slice(quarter * lanes_of_layer, (quarter + 1) * lanes_of_layer)
            s.sums_out[index, 8 + quarter : 9 + quarter, :] = s.sums[8 + index : 9 + index, columns]
    for step in range(1, layers):
        target = (layer + step) % layers
        remote(
            s.sums_out.at[target],
            s.sums_in.at[step - 1],
            s.low_sent.at[0],
            s.low_got.at[0],
            (target * PLANE + place, core),
        ).start()

    def low_copy(step):
        return remote(
            s.sums_all.at[member],
            s.sums_all.at[member],
            s.low_sent.at[1],
            s.low_got.at[1],
            at_member((member + step) % members),
        )

    gather_forward(n1_at, s.n1_sent, s.n1_got)
    gather_finish(n1_at, s.n1_sent, s.n1_got)
    deal_wait(*qg_move)
    spread(
        sum_qkv,
        lambda i: dot(s.n1_t[part(i, fc_rows), :], s.qg_all[...].reshape(tokens, 3 * share)),
        s.qkv_own,
    )
    spread_on(sum_fc)
    spread_on(sum_out)
    settle(s.sums_in, s.low_got.at[0])
    s.sums_all[member] = s.sums_out[layer] + s.sums_in[0] + s.sums_in[1] + s.sums_in[2]
    for step in range(1, members):
        low_copy(step).start()
    spread_on(sum_qkv)
    collect(sum_proj, gproj_ref)
    collect(sum_fc, s.fc_own)
    s.fc_x[...] = s.fc_own[...].astype(BF16).reshape(s.fc_x.shape)
    deal_start(*fx_move)
    collect(sum_out, gout_ref)
    settle(s.sums_all.at[pl.ds(0, members - 1)], s.low_got.at[1])
    total = s.sums_all[0]
    for slot in range(1, members):
        total = total + s.sums_all[slot]
    s.sums[:, :lanes_of_layer] = total
    collect(sum_qkv, s.qkv_own)
    s.qkv_x[...] = s.qkv_own[...].astype(BF16).reshape(s.qkv_x.shape)
    deal_start(*qx_move)
    gvec_ref[...] = jnp.zeros_like(gvec_ref)
    block = s.sums[0:8, part(member // 4, 128)]
    gvec_ref[0:8, :] = pltpu.roll(block, (128 - (member % 4) * 32) % 128, 1)
    block = s.sums[8:16, part(member % 2, 128)]
    chosen = lax.broadcasted_iota(jnp.int32, block.shape, 0) == member // 2
    gvec_ref[8:9, :] = jnp.sum(jnp.where(chosen, block, 0.0), 0, keepdims=True)
    deal_wait(*fx_move)
    for slot in range(members):
        for quarter in range(quarters):
            start = quarter * width + slot * piece
            gfc_ref[:, start : start + piece] = s.fc_y[
                slot, :, quarter * piece : quarter * piece + piece
            ].astype(F32)
    deal_wait(*qx_move)
    for slot in range(members):
        for third in range(3):
            start = third * width + slot * 128
            gqkv_ref[:, start : start + 128] = s.qkv_y[
                slot, :, third * 128 : third * 128 + 128
            ].astype(F32)

    settle(s.sums_in, s.low_sent.at[0])
    settle(s.sums_all.at[pl.ds(0, members - 1)], s.low_sent.at[1])
    settle(peer_rows(s.w_qkv, wq_hbm), s.w_sent.at[0])
    for index in range(3):
        big_piece(index).wait_send()
    vec_copy.wait_send()
    for move in (o_move, g_move, kv_back, q_back):
        swap_drain(*move)
    for move in (att_move, qg_move, fx_move, qx_move):
        deal_drain(*move)
    for where, sent, got in (
        (cot_at, s.cot_sent, s.cot_got),
        (n1_at, s.n1_sent, s.n1_got),
        (n2_at, s.n2_sent, s.n2_got),
        (bg_at, s.bg_sent, s.bg_got),
    ):
        gather_drain(where, sent, got)
    for move in (sum_proj, sum_fc, sum_out, sum_qkv):
        spread_drain(move)


def hand_over(*refs):
    for source, target in zip(refs[:6], refs[7:13]):
        target[...] = source[...]
    for index, low in enumerate(refs[13:]):
        low[...] = refs[6][index : index + 1, : low.shape[1]]


def fused_layer(
    block_input,
    w_qkv,
    w_out,
    w_fc,
    w_proj,
    ln1_gain,
    ln1_bias,
    ln2_gain,
    ln2_bias,
    bias_q,
    bias_v,
    bias_out,
    bias_fc,
    bias_proj,
    cotangent,
):
    width = block_input.shape[4]
    rows = 2 * block_input.shape[3]
    ff = w_fc.shape[1]
    groups = lax.axis_size("ctx")
    shards = 2 * groups
    small = (ln1_gain, ln1_bias, ln2_gain, ln2_bias, bias_q, bias_v, bias_out, bias_proj, bias_fc)
    line = lax.broadcasted_iota(jnp.int32, (16, width // 2), 0)
    vectors, at = jnp.zeros(line.shape, BF16), 0
    for vector in small:
        for start in range(0, vector.shape[0], width // 2):
            piece = lax.broadcast_in_dim(vector[start : start + width // 2], line.shape, (1,))
            vectors = jnp.where(line == at, piece, vectors)
            at += 1
    shapes = layer_shapes(rows, width, ff, groups)
    names = tuple(shapes) + tuple(SEMAPHORES)
    scratch = [pltpu.VMEM(shape, kind) for shape, kind in shapes.values()]
    scratch += [pltpu.SemaphoreType.DMA((count,)) for count in SEMAPHORES.values()]
    in_vmem = pl.BlockSpec(memory_space=pltpu.VMEM)
    in_hbm = pl.BlockSpec(memory_space=pl.ANY)
    outs = pl.pallas_call(
        partial(layer_kernel, names),
        out_shape=(
            jax.ShapeDtypeStruct((rows, width), BF16),
            jax.ShapeDtypeStruct((rows, width), F32),
            jax.ShapeDtypeStruct((width // shards, 3 * width), F32),
            jax.ShapeDtypeStruct((width // shards, width), F32),
            jax.ShapeDtypeStruct((width // shards, ff), F32),
            jax.ShapeDtypeStruct((ff // shards, width), F32),
            jax.ShapeDtypeStruct((16, 128), F32),
        ),
        in_specs=[in_vmem] * 3 + [in_hbm] * 4,
        out_specs=(in_vmem,) * 7,
        scratch_shapes=scratch,
        compiler_params=pltpu.CompilerParams(
            collective_id=0, has_side_effects=True, vmem_limit_bytes=VMEM_BYTES
        ),
        cost_estimate=pl.CostEstimate(
            flops=14 * 10**9, bytes_accessed=30 * 10**6, transcendentals=5 * 10**6
        ),
    )(
        block_input.reshape(rows, width),
        cotangent.reshape(rows, width),
        vectors,
        w_qkv,
        w_out,
        w_fc,
        w_proj,
    )
    piece = width // shards
    wide = ff // shards
    results = pl.pallas_call(
        hand_over,
        out_shape=tuple(jax.ShapeDtypeStruct(out.shape, out.dtype) for out in outs[:6])
        + (jax.ShapeDtypeStruct((1, piece), F32),) * 8
        + (jax.ShapeDtypeStruct((1, wide), F32),),
        in_specs=[in_vmem] * 7,
        out_specs=(in_vmem,) * 15,
    )(*outs)
    block_output, input_grad, grad_qkv, grad_out, grad_fc, grad_proj = results[:6]
    lows = [result.reshape(-1) for result in results[6:]]
    return (
        block_output.reshape(block_input.shape),
        input_grad.reshape(block_input.shape),
        grad_qkv,
        grad_out,
        grad_fc,
        grad_proj,
        *lows[:7],
        lows[8],
        lows[7],
    )


def on_device(*arrays):
    width, ff = arrays[0].shape[4], arrays[3].shape[1]
    fits = (
        lax.axis_size("ctx") == HEADS
        and lax.axis_size("fsdp") == 2
        and arrays[0].shape[:4] == (1, 1, 2, 64)
        and (width, ff) == (1024, 4096)
    )
    return fused_layer(*arrays) if fits else general_layer(*arrays)


def solution(mesh):
    placed = (
        P("fsdp", "ctx", None, None, None),
        P("fsdp", None),
        P("fsdp", None),
        P("fsdp", None),
        P("fsdp", None),
        P("fsdp"),
        P("fsdp"),
        P("fsdp"),
        P("fsdp"),
        P("fsdp"),
        P("fsdp"),
        P("fsdp"),
        P("fsdp"),
        P("fsdp"),
        P("fsdp", "ctx", None, None, None),
    )
    return jax.shard_map(
        on_device,
        mesh=mesh,
        in_specs=placed,
        out_specs=(
            P("fsdp", "ctx", None, None, None),
            P("fsdp", "ctx", None, None, None),
            P(("ctx", "fsdp"), None),
            P(("ctx", "fsdp"), None),
            P(("ctx", "fsdp"), None),
            P(("ctx", "fsdp"), None),
            P(("ctx", "fsdp")),
            P(("ctx", "fsdp")),
            P(("ctx", "fsdp")),
            P(("ctx", "fsdp")),
            P(("ctx", "fsdp")),
            P(("ctx", "fsdp")),
            P(("ctx", "fsdp")),
            P(("ctx", "fsdp")),
            P(("ctx", "fsdp")),
        ),
        check_vma=False,
    )
```

```python
from functools import partial
from types import SimpleNamespace

import jax
import jax.numpy as jnp
from jax import lax
from jax.experimental import pallas as pl
from jax.experimental.pallas import tpu as pltpu
from jax.sharding import PartitionSpec as P

HEADS = 16
VMEM_BYTES = 127 * 2**19


def norm_parts(values):
    average = jnp.mean(values, -1, keepdims=True)
    centered = values - average
    variance = jnp.mean(centered * centered, -1, keepdims=True)
    inverse = lax.rsqrt(variance + 1e-05)
    return (centered * inverse, inverse)


def norm_grads(upstream, normalized, inverse, gain):
    scaled = upstream * gain
    inner_part = (
        scaled
        - jnp.mean(scaled, -1, keepdims=True)
        - normalized * jnp.mean(scaled * normalized, -1, keepdims=True)
    )
    return (inverse * inner_part, jnp.sum(upstream * normalized, 0), jnp.sum(upstream, 0))


def rows_product(left, right):
    return lax.dot_general(
        left, right, (((0,), (0,)), ((), ())), preferred_element_type=jnp.float32
    )


def right_transposed(left, weight):
    return lax.dot_general(
        left, weight, (((1,), (1,)), ((), ())), preferred_element_type=jnp.float32
    )


def split_heads(matrix):
    return matrix.reshape(matrix.shape[0], HEADS, -1)


def head_scores(queries, keys, allowed, scaling):
    scores = (
        jnp.einsum(
            "qhd,khd->hqk",
            split_heads(queries),
            split_heads(keys),
            preferred_element_type=jnp.float32,
        )
        * scaling
    )
    return jnp.where(allowed[None], scores, -1e30)


def general_layer(
    block_input,
    w_qkv,
    w_out,
    w_fc,
    w_proj,
    ln1_gain,
    ln1_bias,
    ln2_gain,
    ln2_bias,
    bias_q,
    bias_v,
    bias_out,
    bias_fc,
    bias_proj,
    cotangent,
):
    seq_count = block_input.shape[0]
    blk_rows = block_input.shape[3]
    width = block_input.shape[4]
    seq_rows = 2 * blk_rows
    row_count = seq_count * seq_rows
    groups = lax.axis_size("ctx")
    member = lax.axis_index("ctx")
    head_size = width // HEADS
    scaling = head_size ** (-0.5)
    full_rows = groups * seq_rows
    gathered = (
        lax.all_gather(w_qkv, "fsdp", axis=0, tiled=True),
        lax.all_gather(w_out, "fsdp", axis=0, tiled=True),
        lax.all_gather(w_fc, "fsdp", axis=0, tiled=True),
        lax.all_gather(w_proj, "fsdp", axis=0, tiled=True),
        lax.all_gather(ln1_gain, "fsdp", axis=0, tiled=True),
        lax.all_gather(ln1_bias, "fsdp", axis=0, tiled=True),
        lax.all_gather(ln2_gain, "fsdp", axis=0, tiled=True),
        lax.all_gather(ln2_bias, "fsdp", axis=0, tiled=True),
        lax.all_gather(bias_q, "fsdp", axis=0, tiled=True),
        lax.all_gather(bias_v, "fsdp", axis=0, tiled=True),
        lax.all_gather(bias_out, "fsdp", axis=0, tiled=True),
        lax.all_gather(bias_fc, "fsdp", axis=0, tiled=True),
        lax.all_gather(bias_proj, "fsdp", axis=0, tiled=True),
    )
    weight_qkv, weight_out, weight_fc, weight_proj = (
        gathered[0],
        gathered[1],
        gathered[2],
        gathered[3],
    )
    vectors = [piece.astype(jnp.float32) for piece in gathered[4:]]
    (
        gain_one,
        shift_one,
        gain_two,
        shift_two,
        query_bias,
        value_bias,
        out_bias,
        fc_bias,
        proj_bias,
    ) = vectors
    local_index = jnp.arange(seq_rows)
    own_block = jnp.where(local_index // blk_rows == 0, member, 2 * groups - 1 - member)
    own_pos = own_block * blk_rows + local_index % blk_rows
    every_index = jnp.arange(full_rows)
    every_owner = every_index // seq_rows
    every_block = jnp.where(
        every_index // blk_rows % 2 == 0, every_owner, 2 * groups - 1 - every_owner
    )
    every_pos = every_block * blk_rows + every_index % blk_rows
    allowed = every_pos[None, :] <= own_pos[:, None]
    inputs = block_input.reshape(row_count, width).astype(jnp.float32)
    normal_one, inverse_one = norm_parts(inputs)
    normed_one = (normal_one * gain_one + shift_one).astype(jnp.bfloat16)
    bias_all = jnp.concatenate([query_bias, jnp.zeros_like(query_bias), value_bias])
    projected = (
        jnp.dot(normed_one, weight_qkv, preferred_element_type=jnp.float32) + bias_all
    ).astype(jnp.bfloat16)
    queries = projected[:, :width]
    keys = projected[:, width : 2 * width]
    values = projected[:, 2 * width :]
    key_all = lax.all_gather(keys, "ctx", axis=0, tiled=True)
    value_all = lax.all_gather(values, "ctx", axis=0, tiled=True)
    scores = head_scores(queries, key_all, allowed, scaling)
    row_top = jnp.max(scores, -1, keepdims=True)
    log_sum = row_top + jnp.log(jnp.sum(jnp.exp(scores - row_top), -1, keepdims=True))
    probs_low = jnp.exp(scores - log_sum).astype(jnp.bfloat16)
    mixed = jnp.einsum(
        "hqk,khd->qhd", probs_low, split_heads(value_all), preferred_element_type=jnp.float32
    )
    mixed_rows = mixed.reshape(seq_rows, width)
    attended = mixed_rows.astype(jnp.bfloat16)
    residual = inputs + jnp.dot(attended, weight_out, preferred_element_type=jnp.float32) + out_bias
    normal_two, inverse_two = norm_parts(residual)
    normed_two = (normal_two * gain_two + shift_two).astype(jnp.bfloat16)
    hidden = jnp.dot(normed_two, weight_fc, preferred_element_type=jnp.float32) + fc_bias
    activated, gelu_pullback = jax.vjp(partial(jax.nn.gelu, approximate=True), hidden)
    activated_low = activated.astype(jnp.bfloat16)
    result = (
        residual
        + jnp.dot(activated_low, weight_proj, preferred_element_type=jnp.float32)
        + proj_bias
    )
    block_output = result.astype(jnp.bfloat16).reshape(block_input.shape)
    weight_qkv, weight_out, weight_fc, weight_proj, gain_low_one, gain_low_two = (
        lax.all_gather(w_qkv, "fsdp", axis=0, tiled=True),
        lax.all_gather(w_out, "fsdp", axis=0, tiled=True),
        lax.all_gather(w_fc, "fsdp", axis=0, tiled=True),
        lax.all_gather(w_proj, "fsdp", axis=0, tiled=True),
        lax.all_gather(ln1_gain, "fsdp", axis=0, tiled=True),
        lax.all_gather(ln2_gain, "fsdp", axis=0, tiled=True),
    )
    gain_one = gain_low_one.astype(jnp.float32)
    gain_two = gain_low_two.astype(jnp.float32)
    out_grad_low = cotangent.reshape(row_count, width)
    upstream = out_grad_low.astype(jnp.float32)
    grad_proj = rows_product(activated_low, out_grad_low)
    grad_proj_bias = jnp.sum(upstream, 0)
    hidden_grad = gelu_pullback(right_transposed(out_grad_low, weight_proj))[0].astype(jnp.bfloat16)
    grad_fc = rows_product(normed_two, hidden_grad)
    grad_fc_bias = jnp.sum(hidden_grad.astype(jnp.float32), 0)
    residual_part, grad_gain_two, grad_shift_two = norm_grads(
        right_transposed(hidden_grad, weight_fc), normal_two, inverse_two, gain_two
    )
    residual_grad = upstream + residual_part
    branch_grad = residual_grad.astype(jnp.bfloat16)
    grad_out = rows_product(attended, branch_grad)
    grad_out_bias = jnp.sum(branch_grad.astype(jnp.float32), 0)
    attended_grad = right_transposed(branch_grad, weight_out).astype(jnp.bfloat16)
    key_all = lax.all_gather(keys, "ctx", axis=0, tiled=True)
    value_all = lax.all_gather(values, "ctx", axis=0, tiled=True)
    scores = head_scores(queries, key_all, allowed, scaling)
    probs = jnp.exp(scores - log_sum)
    prob_grad = jnp.einsum(
        "qhd,khd->hqk",
        split_heads(attended_grad),
        split_heads(value_all),
        preferred_element_type=jnp.float32,
    )
    inner_sum = jnp.sum(probs * prob_grad, -1, keepdims=True)
    score_grad = (probs * (prob_grad - inner_sum)).astype(jnp.bfloat16)
    query_part = (
        jnp.einsum(
            "hqk,khd->qhd", score_grad, split_heads(key_all), preferred_element_type=jnp.float32
        )
        * scaling
    )
    query_grads = query_part.reshape(seq_rows, width)
    probs_low = probs.astype(jnp.bfloat16)
    query_heads = split_heads(queries)
    grad_heads = split_heads(attended_grad)

    def key_terms(
        start,
        count,
        score_grad=score_grad,
        probs_low=probs_low,
        query_heads=query_heads,
        grad_heads=grad_heads,
    ):
        key_part = (
            jnp.einsum("hqk,qhd->khd", score_grad, query_heads, preferred_element_type=jnp.float32)
            * scaling
        )
        value_part = jnp.einsum(
            "hqk,qhd->khd", probs_low, grad_heads, preferred_element_type=jnp.float32
        )
        return jnp.concatenate(
            [key_part.reshape(count, width), value_part.reshape(count, width)], 1
        )

    own_terms = lax.psum_scatter(
        key_terms(jnp.int32(0), lax.axis_size("ctx") * seq_rows),
        "ctx",
        scatter_dimension=0,
        tiled=True,
    )
    key_grads = own_terms[:, :width]
    value_grads = own_terms[:, width:]
    qkv_grad = jnp.concatenate([query_grads, key_grads, value_grads], 1).astype(jnp.bfloat16)
    grad_qkv = rows_product(normed_one, qkv_grad)
    qkv_sums = jnp.sum(qkv_grad.astype(jnp.float32), 0)
    grad_query_bias = qkv_sums[:width]
    grad_value_bias = qkv_sums[2 * width :]
    input_part, grad_gain_one, grad_shift_one = norm_grads(
        right_transposed(qkv_grad, weight_qkv), normal_one, inverse_one, gain_one
    )
    input_grad = (residual_grad + input_part).reshape(block_input.shape)
    sharded = (
        lax.psum_scatter(grad_qkv, ("ctx", "fsdp"), scatter_dimension=0, tiled=True),
        lax.psum_scatter(grad_out, ("ctx", "fsdp"), scatter_dimension=0, tiled=True),
        lax.psum_scatter(grad_fc, ("ctx", "fsdp"), scatter_dimension=0, tiled=True),
        lax.psum_scatter(grad_proj, ("ctx", "fsdp"), scatter_dimension=0, tiled=True),
        lax.psum_scatter(grad_gain_one, ("ctx", "fsdp"), scatter_dimension=0, tiled=True),
        lax.psum_scatter(grad_shift_one, ("ctx", "fsdp"), scatter_dimension=0, tiled=True),
        lax.psum_scatter(grad_gain_two, ("ctx", "fsdp"), scatter_dimension=0, tiled=True),
        lax.psum_scatter(grad_shift_two, ("ctx", "fsdp"), scatter_dimension=0, tiled=True),
        lax.psum_scatter(grad_query_bias, ("ctx", "fsdp"), scatter_dimension=0, tiled=True),
        lax.psum_scatter(grad_value_bias, ("ctx", "fsdp"), scatter_dimension=0, tiled=True),
        lax.psum_scatter(grad_out_bias, ("ctx", "fsdp"), scatter_dimension=0, tiled=True),
        lax.psum_scatter(grad_fc_bias, ("ctx", "fsdp"), scatter_dimension=0, tiled=True),
        lax.psum_scatter(grad_proj_bias, ("ctx", "fsdp"), scatter_dimension=0, tiled=True),
    )
    return (
        block_output,
        input_grad,
        sharded[0],
        sharded[1],
        sharded[2],
        sharded[3],
        sharded[4],
        sharded[5],
        sharded[6],
        sharded[7],
        sharded[8],
        sharded[9],
        sharded[10],
        sharded[11],
        sharded[12],
    )


MESH = pl.DeviceIdType.MESH
BF16, F32 = jnp.bfloat16, jnp.float32
PLANE = 4
NEG = -1e30


def remote(src, dst, sent, received, device):
    return pltpu.make_async_remote_copy(
        src_ref=src,
        dst_ref=dst,
        send_sem=sent,
        recv_sem=received,
        device_id=device,
        device_id_type=MESH,
    )


def dot(left, right):
    return jnp.dot(left, right, preferred_element_type=F32)


def low_lanes(rows):
    return lax.broadcasted_iota(jnp.int32, (rows, 128), 1) < 64


def swap(block):
    return pltpu.roll(block, 64, 1)


def pack_pair(pair):
    half = pair.shape[0] // 2
    low = low_lanes(half)
    top, bottom = pair[:half], pair[half:]
    return jnp.where(low, top, swap(bottom)), jnp.where(low, swap(top), bottom)


def unpack_pair(even, odd):
    low = low_lanes(even.shape[0])
    return jnp.concatenate(
        [jnp.where(low, even, swap(odd)), jnp.where(low, swap(even), odd)], 0
    )


def part(index, size):
    return pl.ds(pl.multiple_of(index * size, size), size)


def layer_shapes(rows, width, ff, groups):
    members = 2 * PLANE
    layers = groups // PLANE
    tokens = members * rows
    half = rows // 2
    keys = groups * half
    share = width // members
    return dict(
        w_qkv=((width, 3 * width), BF16),
        w_out=((width, width), BF16),
        w_fc=((width, ff), BF16),
        w_proj=((ff, width), BF16),
        vec_low=((2, 16, width // 2), BF16),
        vec=((2, 16, width // 2), F32),
        row=((8, width), F32),
        cot_all=((members, rows, width), BF16),
        n1=((rows, width), BF16),
        n1_t=((width, tokens), BF16),
        stage=((groups, 3, half, 128), BF16),
        qkv=((3, keys, 128), BF16),
        kv_roll=((2, keys, 128), BF16),
        q_low=((2, keys, 128), BF16),
        g_low=((2, keys, 128), BF16),
        q_t=((128, keys), BF16),
        g_t=((128, keys), BF16),
        stat=((2, 2, keys, 128), F32),
        mixed=((keys, 128), F32),
        scores=((256, 9 * 256), F32),
        dq=((2, keys, 128), F32),
        o_out=((groups, half, 128), BF16),
        o_in=((groups, half, 128), BF16),
        att=((rows, width), BF16),
        att_t=((layers, members, width // members // layers, rows), BF16),
        att_all=((layers, width // members // layers, tokens), BF16),
        res=((rows, width), F32),
        n2=((rows, width), BF16),
        n2_t=((width, tokens), BF16),
        fc_t=((ff // members, width), BF16),
        bias_t=((ff // members, 128), F32),
        proj_own=((ff // members, width), BF16),
        proj_in=((3 * (ff // members // layers), width), BF16),
        act_all=((ff // members, tokens), BF16),
        hg_all=((ff // members, tokens), BF16),
        upstream=((members, rows, ff // members), F32),
        acc_o=((rows, width), F32),
        acc_d=((rows, width), F32),
        res_grad=((rows, width), F32),
        bg_all=((members, rows, width), BF16),
        g_out=((groups, half, 128), BF16),
        g_in=((keys, 128), BF16),
        back=((groups, 3, half, 128), BF16),
        qg=((rows, 3 * width), BF16),
        qg_out=((members, rows, 3 * share), BF16),
        qg_all=((members, rows, 3 * share), BF16),
        fc_own=((width // layers, ff // members), F32),
        qkv_own=((width // layers, 3 * share), F32),
        qkv_next=((width // layers, 3 * share), F32),
        fc_x=((members, width // layers // members, ff // members), BF16),
        fc_y=((members, width // layers // members, ff // members), BF16),
        qkv_x=((2 * members, width // layers // members, 3 * share), BF16),
        qkv_y=((2 * members, width // layers // members, 3 * share), BF16),
        sums=((16, width), F32),
        sums_out=((layers, 16, width // layers), F32),
        sums_in=((3, 16, width // layers), F32),
        sums_all=((members, 16, width // layers), F32),
    )


SEMAPHORES = dict(
    local=4,
    w_sent=4,
    w_got=7,
    vec_sent=1,
    vec_got=1,
    swap_sent=5,
    swap_got=5,
    cot_sent=1,
    cot_got=5,
    n1_sent=1,
    n1_got=5,
    n2_sent=1,
    n2_got=5,
    bg_sent=1,
    bg_got=5,
    deal_sent=4,
    deal_got=4,
    sum_sent=4,
    sum_got=8,
    low_sent=2,
    low_got=2,
)


def settle(ref, semaphore):
    pltpu.make_async_copy(ref, ref, semaphore).wait()


def layer_kernel(names, *refs):
    x_ref, cot_ref, vec_ref, wq_hbm, wo_hbm, wf_hbm, wp_hbm = refs[:7]
    y_ref, gx_ref, gqkv_ref, gout_ref, gfc_ref, gproj_ref, gvec_ref = refs[7:14]
    s = SimpleNamespace(**dict(zip(names, refs[14:])))
    rows, width = x_ref.shape
    ff = s.w_fc.shape[1]
    half = rows // 2
    groups = s.stage.shape[0]
    members = 2 * PLANE
    layers = groups // PLANE
    tokens = members * rows
    keys = groups * half
    chunk = ff // members
    share = width // members
    scaling = float(width // HEADS) ** (-0.5)
    factor = scaling * 1.4426950408889634
    me = lax.axis_index("ctx")
    core = lax.axis_index("fsdp")
    other = 1 - core
    layer, place = me // PLANE, me % PLANE
    member = place * 2 + core
    twin = (me, other)

    barrier = pltpu.get_barrier_semaphore()
    for step in range(1, groups):
        pl.semaphore_signal(
            barrier, inc=1, device_id=((me + step) % groups, core), device_id_type=MESH
        )
    for step in range(PLANE):
        pl.semaphore_signal(
            barrier,
            inc=1,
            device_id=(layer * PLANE + (place + step) % PLANE, other),
            device_id_type=MESH,
        )
    pl.semaphore_wait(barrier, groups - 1 + PLANE)

    def at_member(index):
        return (layer * PLANE + index // 2, index % 2)

    def top_rows(ref, source):
        count = source.shape[0]
        return ref.at[pl.ds(pl.multiple_of(core * count, count), count)]

    def peer_rows(ref, source):
        count = source.shape[0]
        return ref.at[pl.ds(pl.multiple_of(other * count, count), count)]


    def order(step):
        return (layer + 2 + step) % 4

    def order_in(step):
        return (place + 1 + step) % 4

    pltpu.make_async_copy(wq_hbm, top_rows(s.w_qkv, wq_hbm), s.local.at[0]).start()

    def qkv_piece(step, third):
        columns = part(third * 4 + order(step), 256)
        return remote(
            wq_hbm.at[:, columns],
            top_rows(s.w_qkv, wq_hbm).at[:, columns],
            s.w_sent.at[0],
            s.w_got.at[step],
            twin,
        )

    vec_copy = remote(vec_ref, s.vec_low.at[core], s.vec_sent.at[0], s.vec_got.at[0], twin)
    vec_copy.start()
    for step in range(4):
        for third in range(3):
            qkv_piece(step, third).start()
    big = ((wp_hbm, s.w_proj), (wo_hbm, s.w_out), (wf_hbm, s.w_fc))

    def big_piece(index):
        source, target = big[index]
        return remote(
            source, top_rows(target, source), s.w_sent.at[1 + index], s.w_got.at[4 + index], twin
        )

    def big_local(index):
        source, target = big[index]
        return pltpu.make_async_copy(source, top_rows(target, source), s.local.at[1 + index])

    def gather_copy(where, sent, got, slot, index, device):
        return remote(where(slot), where(slot), sent.at[0], got.at[index], device)

    near_x = place + 1 - 2 * (place % 2)
    near_y = (place + 2) % PLANE
    diagonal = (near_x + 2) % PLANE

    def gather_start(where, sent, got):
        for peer in (near_x, near_y):
            gather_copy(where, sent, got, member, place, (layer * PLANE + peer, core)).start()
        gather_copy(where, sent, got, member, PLANE, twin).start()

    def gather_relay(where, sent, got):
        for peer, onward, lower in ((near_x, near_y, 0), (near_y, near_x, 1)):
            slot = peer * 2 + core
            settle(where(slot), got.at[peer])
            size = where(slot).shape[0] // 2
            half_block = where(slot).at[pl.ds(lower * size, size)]
            remote(
                half_block, half_block, sent.at[0], got.at[peer], (layer * PLANE + onward, core)
            ).start()
            gather_copy(where, sent, got, slot, PLANE, twin).start()

    def gather_forward(where, sent, got):
        slot = diagonal * 2 + core
        settle(where(slot), got.at[diagonal])
        gather_copy(where, sent, got, slot, PLANE, twin).start()

    def gather_finish(where, sent, got):
        settle(where(0, PLANE), got.at[PLANE])

    def gather_drain(where, sent, got):
        settle(where(0, 2 * PLANE - 1), sent.at[0])

    def cot_at(slot, count=None):
        return s.cot_all.at[slot if count is None else pl.ds(slot, count)]

    def bg_at(slot, count=None):
        return s.bg_all.at[slot if count is None else pl.ds(slot, count)]

    def columns_at(ref, slot, count):
        return ref.at[:, part(slot, rows) if count is None else pl.ds(slot * rows, count * rows)]

    def n1_at(slot, count=None):
        return columns_at(s.n1_t, slot, count)

    def n2_at(slot, count=None):
        return columns_at(s.n2_t, slot, count)

    def deal_copy(source, target, number, index):
        return remote(
            source(index),
            target(member),
            s.deal_sent.at[number],
            s.deal_got.at[number],
            at_member(index),
        )

    def deal_own(source, target, number):
        return pltpu.make_async_copy(source(member), target(member), s.deal_got.at[number])

    def deal_start(source, target, number):
        for step in range(1, members):
            deal_copy(source, target, number, (member + step) % members).start()
        deal_own(source, target, number).start()

    def deal_wait(source, target, number):
        settle(target(None), s.deal_got.at[number])

    def deal_drain(source, target, number):
        settle(source(None), s.deal_sent.at[number])

    def seven(index):
        return pl.ds(0, members - 1) if index is None else index

    def whole(index):
        return slice(None) if index is None else index

    def lanes(index):
        return slice(None) if index is None else part(index, rows)

    def swap_one(source, target, number, index):
        @pl.when(index == me)
        def _():
            pltpu.make_async_copy(source(index), target(me), s.swap_got.at[number]).start()

        @pl.when(index != me)
        def _():
            remote(
                source(index),
                target(me),
                s.swap_sent.at[number],
                s.swap_got.at[number],
                (index, core),
            ).start()

    def swap_wait(source, target, number):
        settle(target(None), s.swap_got.at[number])

    def swap_drain(source, target, number):
        settle(source(None), s.swap_sent.at[number])

    def others(index):
        return pl.ds(0, groups - 1) if index is None else index

    def block(index):
        return slice(None) if index is None else part(index, half)

    qkv_move = (lambda h: s.stage.at[others(h)], lambda i: s.qkv.at[:, block(i)], 0)
    o_move = (lambda h: s.o_out.at[others(h)], lambda h: s.o_in.at[whole(h)], 1)
    g_move = (lambda h: s.g_out.at[others(h)], lambda i: s.g_in.at[block(i)], 2)
    kv_back = (
        lambda h: s.stage.at[others(h), pl.ds(1, 2)],
        lambda h: s.back.at[whole(h), pl.ds(1, 2)],
        3,
    )
    q_back = (lambda h: s.stage.at[others(h), 0], lambda h: s.back.at[whole(h), 0], 4)
    att_move = (lambda g: s.att_t.at[:, seven(g)], lambda g: s.att_all.at[:, :, lanes(g)], 0)
    qg_move = (lambda g: s.qg_out.at[seven(g)], lambda g: s.qg_all.at[whole(g)], 1)
    fx_move = (lambda g: s.fc_x.at[seven(g)], lambda g: s.fc_y.at[whole(g)], 2)
    qx_move = (lambda g: s.qkv_x.at[g], lambda g: s.qkv_y.at[whole(g)], 3)

    def vec_row(index):
        return jnp.concatenate([s.vec[0, index : index + 1, :], s.vec[1, index : index + 1, :]], 1)

    s.cot_all[member] = cot_ref[...]
    settle(vec_ref, s.vec_got.at[0])
    s.vec[core] = vec_ref[...].astype(F32)
    s.vec[other] = s.vec_low[other].astype(F32)
    s.row[0:1, :] = vec_row(4)
    s.row[1:2, :] = vec_row(5)
    for quarter in range(4):
        at = 8 + quarter % 2 * 2
        s.row[4 + quarter : 5 + quarter, :] = jnp.concatenate(
            [s.vec[quarter // 2, at : at + 1, :], s.vec[quarter // 2, at + 1 : at + 2, :]], 1
        )
    inputs = x_ref[...].astype(F32)
    normal, _ = norm_parts(inputs)
    normed = (normal * vec_row(0) + vec_row(1)).astype(BF16)
    s.n1[...] = normed
    s.n1_t[:, part(member, rows)] = normed.astype(F32).T.astype(BF16)
    pltpu.make_async_copy(wq_hbm, top_rows(s.w_qkv, wq_hbm), s.local.at[0]).wait()

    for step in range(4):
        four = order(step)
        settle(peer_rows(s.w_qkv, wq_hbm).at[:, pl.ds(0, 768)], s.w_got.at[step])
        for third in range(3):
            columns = part(third * 4 + four, 256)
            product = dot(s.n1[...], s.w_qkv[:, columns])
            if third == 0:
                product = product + s.row[0:1, part(four, 256)]
            if third == 2:
                product = product + s.row[1:2, part(four, 256)]
            for pair in range(2):
                even, odd = pack_pair(product[:, pair * 128 : pair * 128 + 128])
                s.stage[four * 4 + 2 * pair, third] = even.astype(BF16)
                s.stage[four * 4 + 2 * pair + 1, third] = odd.astype(BF16)
        for head in range(4):
            swap_one(*qkv_move, four * 4 + order_in(head))
    gather_start(cot_at, s.cot_sent, s.cot_got)
    for index in range(3):
        big_piece(index).start()
        big_local(index).start()

    settle(peer_rows(s.w_proj, wp_hbm), s.w_got.at[4])
    big_local(0).wait()

    def send_back(index, _):
        s.upstream[index] = right_transposed(cot_ref[...], s.w_proj[part(index, chunk), :])
        return 0

    lax.fori_loop(0, members, send_back, 0)

    swap_wait(*qkv_move)
    gather_relay(cot_at, s.cot_sent, s.cot_got)
    low_all = low_lanes(keys)
    query = s.qkv[0].astype(F32)
    s.q_low[0] = jnp.where(low_all, query, 0.0).astype(BF16)
    s.q_low[1] = jnp.where(low_all, swap(query), 0.0).astype(BF16)
    s.q_t[...] = query.T.astype(BF16)
    s.kv_roll[0] = swap(s.qkv[1].astype(F32)).astype(BF16)
    s.kv_roll[1] = swap(s.qkv[2].astype(F32)).astype(BF16)

    tile = 256
    per_tile = tile // half
    low_tile = low_lanes(tile)
    row_at = lax.broadcasted_iota(jnp.int32, (tile, tile), 0)
    col_at = lax.broadcasted_iota(jnp.int32, (tile, tile), 1)

    def late(index):
        return index + (per_tile - 1 - 2 * (index // half)) * half

    masks = (col_at <= row_at, late(col_at) <= late(row_at))

    def key_block(region, at):
        return s.qkv[1, at, :] if region == 0 else s.kv_roll[0, at, :]

    def value_block(region, at):
        return s.qkv[2, at, :] if region == 0 else s.kv_roll[1, at, :]

    n_tiles = keys // tile

    def span(start, count=1):
        return slice(start * tile, (start + count) * tile)

    def score_block(queries, region, first, count, column, masked):
        scores = right_transposed(queries, key_block(region, span(first, count)))
        if masked:
            scores = jnp.where(masks[region], scores, NEG)
        s.scores[:, span(column, count)] = scores
        return scores

    def fold(values, combine):
        out = values[:, :128]
        for start in range(128, values.shape[1], 128):
            out = combine(out, values[:, start : start + 128])
        return out

    def softmax_rows(side, blocks, at):
        queries = s.q_low[side, at, :]
        top = None
        for block in blocks:
            high = fold(score_block(queries, *block), jnp.maximum)
            top = high if top is None else jnp.maximum(top, high)
        top = jnp.max(top, 1, keepdims=True) * factor
        total, mix = None, None
        for region, first, count, column, _ in blocks:
            probs = jnp.exp2(s.scores[:, span(column, count)] * factor - top)
            folded = fold(probs, jnp.add)
            total = folded if total is None else total + folded
            more = dot(probs.astype(BF16), value_block(region, span(first, count)))
            mix = more if mix is None else mix + more
        total = jnp.sum(total, 1, keepdims=True)
        s.stat[0, side, at, :] = jnp.broadcast_to(top + jnp.log2(total), (tile, 128))
        return mix / total

    def attend(index):
        at = span(index)
        early = [(0, index, 1, 0, True)]
        if index:
            early.append((0, 0, index, 1, False))
        late_blocks = [(1, index, 1, index + 1, True)]
        if index + 1 < n_tiles:
            late_blocks.append((1, index + 1, n_tiles - 1 - index, index + 2, False))
        late_blocks.append((0, 0, n_tiles, n_tiles + 1, False))
        one = softmax_rows(0, early, at)
        two = softmax_rows(1, late_blocks, at)
        out = jnp.where(low_tile, one, swap(two))
        s.mixed[at, :] = out
        s.o_out[pl.ds(index * per_tile, per_tile)] = out.astype(BF16).reshape(per_tile, half, 128)
        for step in range(per_tile):
            swap_one(*o_move, index * per_tile + order_in(step))

    for index in range(n_tiles):
        attend(index)

    for index in range(1, 3):
        settle(peer_rows(big[index][1], big[index][0]), s.w_got.at[4 + index])
        big_local(index).wait()
    quarters = ff // width
    piece = width // members

    curve = 0.7978845608028654

    def features(index):
        return [part(quarter * members + index, piece) for quarter in range(quarters)]

    mine = features(member)
    s.proj_own[...] = jnp.concatenate([s.w_proj[at, :] for at in mine], 0)
    for quarter, at in enumerate(mine):
        into = slice(quarter * piece, quarter * piece + piece)
        s.fc_t[into, :] = s.w_fc[:, at].astype(F32).T.astype(BF16)
        bias = s.row[4 + quarter : 5 + quarter, part(member, piece)]
        s.bias_t[into, :] = jnp.broadcast_to(bias, (128, piece)).T
    swap_wait(*o_move)
    gather_forward(cot_at, s.cot_sent, s.cot_got)
    for pair in range(HEADS // 2):
        columns = slice(pair * 128, pair * 128 + 128)
        s.att[:, columns] = unpack_pair(
            s.o_in[2 * pair].astype(F32), s.o_in[2 * pair + 1].astype(F32)
        ).astype(BF16)
    turned = s.att[...].astype(F32).T.astype(BF16)
    s.att_t[...] = turned.reshape(s.att_t.shape)
    def project(index, _):
        at = part(index, 256)
        s.acc_d[:, at] = dot(s.att[...], s.w_out[:, at])
        return 0

    lax.fori_loop(0, width // 256, project, 0)
    s.res[...] = x_ref[...].astype(F32) + s.acc_d[...] + vec_row(6)
    normal, _ = norm_parts(s.res[...])
    normed = (normal * vec_row(2) + vec_row(3)).astype(BF16)
    s.n2[...] = normed
    s.n2_t[:, part(member, rows)] = normed.astype(F32).T.astype(BF16)
    gather_start(n2_at, s.n2_sent, s.n2_got)
    s.acc_o[...] = jnp.zeros_like(s.acc_o)
    s.acc_d[...] = jnp.zeros_like(s.acc_d)
    s.sums[...] = jnp.zeros_like(s.sums)


    def gelu_parts(hidden):
        square = hidden * hidden
        bend = jnp.tanh(curve * hidden * (1.0 + 0.044715 * square))
        rise = 0.5 * (1.0 + bend)
        slope = rise + 0.5 * hidden * (1.0 - bend * bend) * (
            curve * (1.0 + 3.0 * 0.044715 * square)
        )
        return hidden * rise, slope

    def feed(index, _):
        at = part(index, chunk)
        bias = s.vec.at[index // 4][pl.ds(8 + index % 4, 1), :]
        active, slope = gelu_parts(dot(s.n2[...], s.w_fc[:, at]) + bias)
        active = active.astype(BF16)
        grad = (s.upstream[index] * slope).astype(BF16)
        s.acc_o[...] += dot(active, s.w_proj[at, :])
        s.acc_d[...] += right_transposed(grad, s.w_fc[:, at])
        s.sums[pl.ds(8 + index // 2, 1), part(index % 2, chunk)] = jnp.sum(
            grad.astype(F32), 0, keepdims=True
        )
        return 0

    lax.fori_loop(0, members - 3, feed, 0)
    gather_relay(n2_at, s.n2_sent, s.n2_got)
    lax.fori_loop(members - 3, members, feed, 0)
    upstream = cot_ref[...].astype(F32)
    normal, inverse = norm_parts(s.res[...])
    step_grad, gain_grad, shift_grad = norm_grads(s.acc_d[...], normal, inverse, vec_row(2))
    s.sums[2:3, :] = gain_grad[None]
    s.sums[3:4, :] = shift_grad[None]
    s.sums[7:8, :] = jnp.sum(upstream, 0, keepdims=True)
    res_grad = upstream + step_grad
    s.res_grad[...] = res_grad
    branch = res_grad.astype(BF16)
    s.bg_all[member] = branch
    s.sums[6:7, :] = jnp.sum(branch.astype(F32), 0, keepdims=True)
    for step in range(4):
        four = order(step)
        product = right_transposed(s.bg_all[member], s.w_out[part(four, 256), :])
        for pair in range(2):
            even, odd = pack_pair(product[:, pair * 128 : pair * 128 + 128])
            s.g_out[four * 4 + 2 * pair] = even.astype(BF16)
            s.g_out[four * 4 + 2 * pair + 1] = odd.astype(BF16)
        for head in range(4):
            swap_one(*g_move, four * 4 + order_in(head))
    y_ref[...] = (s.res[...] + s.acc_o[...] + vec_row(7)).astype(BF16)
    gather_start(bg_at, s.bg_sent, s.bg_got)
    deal_start(*att_move)
    gather_forward(n2_at, s.n2_sent, s.n2_got)
    swap_drain(*qkv_move)

    beside = layer + 1 - 2 * (layer % 2)
    beyond = (layer + 2) % layers
    across = (beside + 2) % layers

    def spread_copy(move, slot, target):
        buffer_out, buffer_in, number = move
        return remote(
            buffer_out(slot),
            buffer_in(slot),
            s.sum_sent.at[number],
            s.sum_got.at[2 * number + (slot + 1) // 2],
            (target * PLANE + place, core),
        )

    def spread_prepare(move, product, own_ref):
        for slot, index in enumerate((across, beside, beyond)):
            move[0](slot)[...] = product(index).astype(BF16)
        own_ref[...] = product(layer)

    def spread_start(move):
        for slot in range(2):
            spread_copy(move, slot, beside).start()

    def spread(move, product, own_ref):
        for slot, index in enumerate((across, beside, beyond)):
            move[0](slot)[...] = product(index).astype(BF16)
            if slot < 2:
                spread_copy(move, slot, beside).start()
        own_ref[...] = product(layer)

    def spread_on(move):
        settle(move[1](0), s.sum_got.at[2 * move[2]])
        pair = move[0](2)[...].astype(F32) + move[1](0)[...].astype(F32)
        move[0](2)[...] = pair.astype(BF16)
        spread_copy(move, 2, beyond).start()

    def collect(move, own_ref):
        settle(move[1](1, 2), s.sum_got.at[2 * move[2] + 1])
        own_ref[...] += move[1](1)[...].astype(F32) + move[1](2)[...].astype(F32)

    def spread_drain(move):
        settle(move[0](0, 3), s.sum_sent.at[move[2]])

    proj_rows = ff // members // layers
    out_rows = share // layers
    fc_rows = width // layers

    def rows_of(ref, start, size, columns=slice(None)):
        return lambda slot, count=1: ref.at[pl.ds(start + slot * size, count * size), columns]

    sum_proj = (rows_of(s.w_proj, 0, proj_rows), rows_of(s.proj_in, 0, proj_rows), 0)
    sum_out = (rows_of(s.w_proj, 1024, out_rows), rows_of(s.w_proj, 1152, out_rows), 1)
    sum_fc = (
        rows_of(s.w_fc, 0, fc_rows, pl.ds(0, chunk)),
        rows_of(s.w_fc, 0, fc_rows, pl.ds(chunk, chunk)),
        2,
    )
    sum_qkv = (
        rows_of(s.w_fc, 0, fc_rows, pl.ds(2 * chunk, 3 * share)),
        rows_of(s.w_fc, 0, fc_rows, pl.ds(3 * chunk, 3 * share)),
        3,
    )

    part_rows = chunk // 2

    def tokens_of(first, second):
        return [part(first, rows), part(second, rows)]

    def feed_again(first, second):
        here = tokens_of(first, second)
        normed = jnp.concatenate([s.n2_t[:, at] for at in here], 1)
        hidden = dot(s.fc_t[...], normed) + jnp.concatenate([s.bias_t[...]] * 2, 1)
        active, slope = gelu_parts(hidden)
        active = active.astype(BF16)
        for index, at in enumerate(here):
            columns = slice(index * rows, (index + 1) * rows)
            s.act_all[:, at] = active[:, columns]
            s.scores[:, at] = slope[:part_rows, columns]
            s.scores[:, part((first, second)[index] + members, rows)] = slope[part_rows:, columns]

    def back_again(first, second):
        cotangents = jnp.concatenate([s.cot_all[first], s.cot_all[second]], 0)
        upstream = right_transposed(s.proj_own[...], cotangents)
        for index, slot in enumerate((first, second)):
            at = part(slot, rows)
            columns = slice(index * rows, (index + 1) * rows)
            grad = upstream[:part_rows, columns] * s.scores[:, at]
            s.hg_all[:part_rows, at] = grad.astype(BF16)
            grad = upstream[part_rows:, columns] * s.scores[:, part(slot + members, rows)]
            s.hg_all[part_rows:, at] = grad.astype(BF16)

    def grads_of_feed():
        pairs = (
            (member, near_x * 2 + core),
            (near_y * 2 + core, diagonal * 2 + core),
            (place * 2 + other, near_x * 2 + other),
            (near_y * 2 + other, diagonal * 2 + other),
        )
        gather_finish(cot_at, s.cot_sent, s.cot_got)
        for index, pair in enumerate(pairs):
            if index == 2:
                gather_finish(n2_at, s.n2_sent, s.n2_got)
            feed_again(*pair)
        spread(
            sum_proj,
            lambda i: dot(s.act_all[part(i, proj_rows), :], s.cot_all[...].reshape(tokens, width)),
            gproj_ref,
        )
        for pair in pairs:
            back_again(*pair)

    def grad_of_fc():
        spread_prepare(
            sum_fc,
            lambda i: right_transposed(s.n2_t[part(i, fc_rows), :], s.hg_all[...]),
            s.fc_own,
        )

    def grad_of_out():
        gather_finish(bg_at, s.bg_sent, s.bg_got)
        deal_wait(*att_move)
        spread(
            sum_out,
            lambda i: dot(s.att_all[i], s.bg_all[...].reshape(tokens, width)),
            gout_ref,
        )

    grads_of_feed()
    swap_wait(*g_move)
    upstream = s.g_in[...].astype(F32)
    s.g_low[0] = jnp.where(low_all, upstream, 0.0).astype(BF16)
    s.g_low[1] = jnp.where(low_all, swap(upstream), 0.0).astype(BF16)
    s.g_t[...] = upstream.T.astype(BF16)
    inner = upstream * s.mixed[...]
    for side in range(2):
        kept = jnp.where(low_all == (side == 0), inner, 0.0)
        s.stat[1, side] = jnp.broadcast_to(jnp.sum(kept, 1, keepdims=True), (keys, 128))
    s.dq[...] = jnp.zeros_like(s.dq)

    def wide(block):
        return jnp.concatenate([block] * (tile // 128), 1)

    def back_tile(side, region, at_q, at_k, masked):
        scores = right_transposed(s.q_low[side, at_q, :], key_block(region, at_k))
        probs = jnp.exp2(scores * factor - wide(s.stat[0, side, at_q, :]))
        if masked:
            probs = jnp.where(masks[region], probs, 0.0)
        prob_grad = right_transposed(s.g_low[side, at_q, :], value_block(region, at_k))
        score_grad = (probs * (prob_grad - wide(s.stat[1, side, at_q, :]))).astype(BF16)
        head = slice(side * 64, side * 64 + 64)
        s.dq[side, at_q, :] += dot(score_grad, key_block(region, at_k))
        return dot(s.q_t[head, at_q], score_grad), dot(s.g_t[head, at_q], probs.astype(BF16))

    def attend_back(index):
        at = span(index)
        early = [(0, 0, k, k == index) for k in range(index, n_tiles)]
        early += [(1, 0, k, False) for k in range(n_tiles)]
        late_pairs = [(1, 1, k, k == index) for k in range(index + 1)]
        grads = []
        for pairs in (early, late_pairs):
            both = [
                back_tile(side, region, span(k), at, masked) for side, region, k, masked in pairs
            ]
            grads.append([sum(parts) for parts in zip(*both)])
        for third, scale in ((1, scaling), (2, 1.0)):
            rows_t = jnp.concatenate([grads[0][third - 1], grads[1][third - 1]], 0)
            s.stage[pl.ds(index * per_tile, per_tile), third] = (
                (rows_t.T * scale).astype(BF16).reshape(per_tile, half, 128)
            )
        for step in range(per_tile):
            swap_one(*kv_back, index * per_tile + order_in(step))

    gather_relay(bg_at, s.bg_sent, s.bg_got)
    attend_back(0)
    attend_back(1)
    grad_of_fc()
    attend_back(2)
    gather_forward(bg_at, s.bg_sent, s.bg_got)
    attend_back(3)
    out = jnp.where(low_all, s.dq[0], swap(s.dq[1])) * scaling
    s.stage[:, 0] = out.astype(BF16).reshape(groups, half, 128)
    for step in range(4):
        for head in range(4):
            swap_one(*q_back, order(step) * 4 + order_in(head))
    spread_start(sum_fc)
    gather_start(n1_at, s.n1_sent, s.n1_got)
    grad_of_out()
    spread_on(sum_proj)

    swap_wait(*kv_back)
    gather_relay(n1_at, s.n1_sent, s.n1_got)
    swap_wait(*q_back)
    for pair in range(HEADS // 2):
        for third in range(3):
            block = unpack_pair(
                s.back[2 * pair, third].astype(F32), s.back[2 * pair + 1, third].astype(F32)
            ).astype(BF16)
            s.qg_out[pair, :, third * 128 : third * 128 + 128] = block
            columns = slice(third * width + pair * 128, third * width + pair * 128 + 128)
            s.qg[:, columns] = block
    deal_start(*qg_move)
    gather_forward(n1_at, s.n1_sent, s.n1_got)
    s.sums[4:5, :] = jnp.sum(s.qg[:, :width].astype(F32), 0, keepdims=True)
    s.sums[5:6, :] = jnp.sum(s.qg[:, 2 * width :].astype(F32), 0, keepdims=True)

    def project_back(index, _):
        s.acc_d[:, part(index, 256)] = right_transposed(s.qg[...], s.w_qkv[part(index, 256), :])
        return 0

    lax.fori_loop(0, width // 256, project_back, 0)
    normal, inverse = norm_parts(x_ref[...].astype(F32))
    step_grad, gain_grad, shift_grad = norm_grads(s.acc_d[...], normal, inverse, vec_row(0))
    s.sums[0:1, :] = gain_grad[None]
    s.sums[1:2, :] = shift_grad[None]
    gx_ref[...] = s.res_grad[...] + step_grad

    lanes_of_layer = width // layers
    for index in range(layers):
        columns = slice(index * lanes_of_layer, (index + 1) * lanes_of_layer)
        s.sums_out[index, 0:8, :] = s.sums[0:8, columns]
        for quarter in range(layers):
            columns = slice(quarter * lanes_of_layer, (quarter + 1) * lanes_of_layer)
            s.sums_out[index, 8 + quarter : 9 + quarter, :] = s.sums[8 + index : 9 + index, columns]
    for step in range(1, layers):
        target = (layer + step) % layers
        remote(
            s.sums_out.at[target],
            s.sums_in.at[step - 1],
            s.low_sent.at[0],
            s.low_got.at[0],
            (target * PLANE + place, core),
        ).start()

    def low_copy(step):
        return remote(
            s.sums_all.at[member],
            s.sums_all.at[member],
            s.low_sent.at[1],
            s.low_got.at[1],
            at_member((member + step) % members),
        )

    spread_on(sum_fc)
    gather_finish(n1_at, s.n1_sent, s.n1_got)
    deal_wait(*qg_move)
    def qkv_product(index):
        return dot(
            s.n1_t[part(index, fc_rows), :], s.qg_all[...].reshape(tokens, 3 * share)
        )

    for slot, index in enumerate((across, beside)):
        sum_qkv[0](slot)[...] = qkv_product(index).astype(BF16)
        spread_copy(sum_qkv, slot, beside).start()
    s.qkv_next[...] = qkv_product(beyond)
    s.qkv_own[...] = qkv_product(layer)

    def pair_sum(move, slot, own, into):
        settle(move[1](slot), s.sum_got.at[2 * move[2] + slot])
        both = own[...] + move[1](slot)[...].astype(F32)
        s.qkv_x[pl.ds(into, members)] = both.astype(BF16).reshape(members, -1, 3 * share)

    spread_on(sum_out)
    pair_sum(sum_qkv, 0, s.qkv_next, members)
    for index in range(members):
        remote(
            s.qkv_x.at[members + index],
            s.qkv_y.at[members + member],
            s.deal_sent.at[3],
            s.deal_got.at[3],
            (beyond * PLANE + index // 2, index % 2),
        ).start()
    settle(s.sums_in, s.low_got.at[0])
    s.sums_all[member] = s.sums_out[layer] + s.sums_in[0] + s.sums_in[1] + s.sums_in[2]
    for step in range(1, members):
        low_copy(step).start()
    collect(sum_proj, gproj_ref)
    collect(sum_fc, s.fc_own)
    s.fc_x[...] = s.fc_own[...].astype(BF16).reshape(s.fc_x.shape)
    deal_start(*fx_move)
    collect(sum_out, gout_ref)
    settle(s.sums_all.at[pl.ds(0, members - 1)], s.low_got.at[1])
    total = s.sums_all[0]
    for slot in range(1, members):
        total = total + s.sums_all[slot]
    s.sums[:, :lanes_of_layer] = total
    pair_sum(sum_qkv, 1, s.qkv_own, 0)
    deal_start(*qx_move)
    gvec_ref[...] = jnp.zeros_like(gvec_ref)
    block = s.sums[0:8, part(member // 4, 128)]
    gvec_ref[0:8, :] = pltpu.roll(block, (128 - (member % 4) * 32) % 128, 1)
    block = s.sums[8:16, part(member % 2, 128)]
    chosen = lax.broadcasted_iota(jnp.int32, block.shape, 0) == member // 2
    gvec_ref[8:9, :] = jnp.sum(jnp.where(chosen, block, 0.0), 0, keepdims=True)
    deal_wait(*fx_move)
    for slot in range(members):
        for quarter in range(quarters):
            start = quarter * width + slot * piece
            gfc_ref[:, start : start + piece] = s.fc_y[
                slot, :, quarter * piece : quarter * piece + piece
            ].astype(F32)
    deal_wait(*qx_move)
    for slot in range(members):
        for third in range(3):
            start = third * width + slot * 128
            columns = slice(third * 128, third * 128 + 128)
            gqkv_ref[:, start : start + 128] = s.qkv_y[slot, :, columns].astype(
                F32
            ) + s.qkv_y[members + slot, :, columns].astype(F32)

    settle(s.sums_in, s.low_sent.at[0])
    settle(s.sums_all.at[pl.ds(0, members - 1)], s.low_sent.at[1])
    settle(peer_rows(s.w_qkv, wq_hbm), s.w_sent.at[0])
    for index in range(3):
        big_piece(index).wait_send()
    vec_copy.wait_send()
    for move in (o_move, g_move, kv_back, q_back):
        swap_drain(*move)
    for move in (att_move, qg_move, fx_move):
        deal_drain(*move)
    settle(s.qkv_x.at[pl.ds(0, 2 * members - 1)], s.deal_sent.at[3])
    for where, sent, got in (
        (cot_at, s.cot_sent, s.cot_got),
        (n1_at, s.n1_sent, s.n1_got),
        (n2_at, s.n2_sent, s.n2_got),
        (bg_at, s.bg_sent, s.bg_got),
    ):
        gather_drain(where, sent, got)
    for move in (sum_proj, sum_fc, sum_out):
        spread_drain(move)
    settle(sum_qkv[0](0, 2), s.sum_sent.at[3])


def hand_over(*refs):
    for source, target in zip(refs[:6], refs[7:13]):
        target[...] = source[...]
    for index, low in enumerate(refs[13:]):
        low[...] = refs[6][index : index + 1, : low.shape[1]]


def fused_layer(
    block_input,
    w_qkv,
    w_out,
    w_fc,
    w_proj,
    ln1_gain,
    ln1_bias,
    ln2_gain,
    ln2_bias,
    bias_q,
    bias_v,
    bias_out,
    bias_fc,
    bias_proj,
    cotangent,
):
    width = block_input.shape[4]
    rows = 2 * block_input.shape[3]
    ff = w_fc.shape[1]
    groups = lax.axis_size("ctx")
    shards = 2 * groups
    small = (ln1_gain, ln1_bias, ln2_gain, ln2_bias, bias_q, bias_v, bias_out, bias_proj, bias_fc)
    line = lax.broadcasted_iota(jnp.int32, (16, width // 2), 0)
    vectors, at = jnp.zeros(line.shape, BF16), 0
    for vector in small:
        for start in range(0, vector.shape[0], width // 2):
            piece = lax.broadcast_in_dim(vector[start : start + width // 2], line.shape, (1,))
            vectors = jnp.where(line == at, piece, vectors)
            at += 1
    shapes = layer_shapes(rows, width, ff, groups)
    names = tuple(shapes) + tuple(SEMAPHORES)
    scratch = [pltpu.VMEM(shape, kind) for shape, kind in shapes.values()]
    scratch += [pltpu.SemaphoreType.DMA((count,)) for count in SEMAPHORES.values()]
    in_vmem = pl.BlockSpec(memory_space=pltpu.VMEM)
    in_hbm = pl.BlockSpec(memory_space=pl.ANY)
    outs = pl.pallas_call(
        partial(layer_kernel, names),
        out_shape=(
            jax.ShapeDtypeStruct((rows, width), BF16),
            jax.ShapeDtypeStruct((rows, width), F32),
            jax.ShapeDtypeStruct((width // shards, 3 * width), F32),
            jax.ShapeDtypeStruct((width // shards, width), F32),
            jax.ShapeDtypeStruct((width // shards, ff), F32),
            jax.ShapeDtypeStruct((ff // shards, width), F32),
            jax.ShapeDtypeStruct((16, 128), F32),
        ),
        in_specs=[in_vmem] * 3 + [in_hbm] * 4,
        out_specs=(in_vmem,) * 7,
        scratch_shapes=scratch,
        compiler_params=pltpu.CompilerParams(
            collective_id=0, has_side_effects=True, vmem_limit_bytes=VMEM_BYTES
        ),
        cost_estimate=pl.CostEstimate(
            flops=14 * 10**9, bytes_accessed=30 * 10**6, transcendentals=5 * 10**6
        ),
    )(
        block_input.reshape(rows, width),
        cotangent.reshape(rows, width),
        vectors,
        w_qkv,
        w_out,
        w_fc,
        w_proj,
    )
    piece = width // shards
    wide = ff // shards
    results = pl.pallas_call(
        hand_over,
        out_shape=tuple(jax.ShapeDtypeStruct(out.shape, out.dtype) for out in outs[:6])
        + (jax.ShapeDtypeStruct((1, piece), F32),) * 8
        + (jax.ShapeDtypeStruct((1, wide), F32),),
        in_specs=[in_vmem] * 7,
        out_specs=(in_vmem,) * 15,
    )(*outs)
    block_output, input_grad, grad_qkv, grad_out, grad_fc, grad_proj = results[:6]
    lows = [result.reshape(-1) for result in results[6:]]
    return (
        block_output.reshape(block_input.shape),
        input_grad.reshape(block_input.shape),
        grad_qkv,
        grad_out,
        grad_fc,
        grad_proj,
        *lows[:7],
        lows[8],
        lows[7],
    )


def on_device(*arrays):
    width, ff = arrays[0].shape[4], arrays[3].shape[1]
    fits = (
        lax.axis_size("ctx") == HEADS
        and lax.axis_size("fsdp") == 2
        and arrays[0].shape[:4] == (1, 1, 2, 64)
        and (width, ff) == (1024, 4096)
    )
    return fused_layer(*arrays) if fits else general_layer(*arrays)


def solution(mesh):
    placed = (
        P("fsdp", "ctx", None, None, None),
        P("fsdp", None),
        P("fsdp", None),
        P("fsdp", None),
        P("fsdp", None),
        P("fsdp"),
        P("fsdp"),
        P("fsdp"),
        P("fsdp"),
        P("fsdp"),
        P("fsdp"),
        P("fsdp"),
        P("fsdp"),
        P("fsdp"),
        P("fsdp", "ctx", None, None, None),
    )
    return jax.shard_map(
        on_device,
        mesh=mesh,
        in_specs=placed,
        out_specs=(
            P("fsdp", "ctx", None, None, None),
            P("fsdp", "ctx", None, None, None),
            P(("ctx", "fsdp"), None),
            P(("ctx", "fsdp"), None),
            P(("ctx", "fsdp"), None),
            P(("ctx", "fsdp"), None),
            P(("ctx", "fsdp")),
            P(("ctx", "fsdp")),
            P(("ctx", "fsdp")),
            P(("ctx", "fsdp")),
            P(("ctx", "fsdp")),
            P(("ctx", "fsdp")),
            P(("ctx", "fsdp")),
            P(("ctx", "fsdp")),
            P(("ctx", "fsdp")),
        ),
        check_vma=False,
    )
```

```python
from functools import partial
from types import SimpleNamespace

import jax
import jax.numpy as jnp
from jax import lax
from jax.experimental import pallas as pl
from jax.experimental.pallas import tpu as pltpu
from jax.sharding import PartitionSpec as P

HEADS = 16
VMEM_BYTES = 127 * 2**19


def norm_parts(values):
    average = jnp.mean(values, -1, keepdims=True)
    centered = values - average
    variance = jnp.mean(centered * centered, -1, keepdims=True)
    inverse = lax.rsqrt(variance + 1e-05)
    return (centered * inverse, inverse)


def norm_grads(upstream, normalized, inverse, gain):
    scaled = upstream * gain
    inner_part = (
        scaled
        - jnp.mean(scaled, -1, keepdims=True)
        - normalized * jnp.mean(scaled * normalized, -1, keepdims=True)
    )
    return (inverse * inner_part, jnp.sum(upstream * normalized, 0), jnp.sum(upstream, 0))


def rows_product(left, right):
    return lax.dot_general(
        left, right, (((0,), (0,)), ((), ())), preferred_element_type=jnp.float32
    )


def right_transposed(left, weight):
    return lax.dot_general(
        left, weight, (((1,), (1,)), ((), ())), preferred_element_type=jnp.float32
    )


def split_heads(matrix):
    return matrix.reshape(matrix.shape[0], HEADS, -1)


def head_scores(queries, keys, allowed, scaling):
    scores = (
        jnp.einsum(
            "qhd,khd->hqk",
            split_heads(queries),
            split_heads(keys),
            preferred_element_type=jnp.float32,
        )
        * scaling
    )
    return jnp.where(allowed[None], scores, -1e30)


def general_layer(
    block_input,
    w_qkv,
    w_out,
    w_fc,
    w_proj,
    ln1_gain,
    ln1_bias,
    ln2_gain,
    ln2_bias,
    bias_q,
    bias_v,
    bias_out,
    bias_fc,
    bias_proj,
    cotangent,
):
    seq_count = block_input.shape[0]
    blk_rows = block_input.shape[3]
    width = block_input.shape[4]
    seq_rows = 2 * blk_rows
    row_count = seq_count * seq_rows
    groups = lax.axis_size("ctx")
    member = lax.axis_index("ctx")
    head_size = width // HEADS
    scaling = head_size ** (-0.5)
    full_rows = groups * seq_rows
    gathered = (
        lax.all_gather(w_qkv, "fsdp", axis=0, tiled=True),
        lax.all_gather(w_out, "fsdp", axis=0, tiled=True),
        lax.all_gather(w_fc, "fsdp", axis=0, tiled=True),
        lax.all_gather(w_proj, "fsdp", axis=0, tiled=True),
        lax.all_gather(ln1_gain, "fsdp", axis=0, tiled=True),
        lax.all_gather(ln1_bias, "fsdp", axis=0, tiled=True),
        lax.all_gather(ln2_gain, "fsdp", axis=0, tiled=True),
        lax.all_gather(ln2_bias, "fsdp", axis=0, tiled=True),
        lax.all_gather(bias_q, "fsdp", axis=0, tiled=True),
        lax.all_gather(bias_v, "fsdp", axis=0, tiled=True),
        lax.all_gather(bias_out, "fsdp", axis=0, tiled=True),
        lax.all_gather(bias_fc, "fsdp", axis=0, tiled=True),
        lax.all_gather(bias_proj, "fsdp", axis=0, tiled=True),
    )
    weight_qkv, weight_out, weight_fc, weight_proj = (
        gathered[0],
        gathered[1],
        gathered[2],
        gathered[3],
    )
    vectors = [piece.astype(jnp.float32) for piece in gathered[4:]]
    (
        gain_one,
        shift_one,
        gain_two,
        shift_two,
        query_bias,
        value_bias,
        out_bias,
        fc_bias,
        proj_bias,
    ) = vectors
    local_index = jnp.arange(seq_rows)
    own_block = jnp.where(local_index // blk_rows == 0, member, 2 * groups - 1 - member)
    own_pos = own_block * blk_rows + local_index % blk_rows
    every_index = jnp.arange(full_rows)
    every_owner = every_index // seq_rows
    every_block = jnp.where(
        every_index // blk_rows % 2 == 0, every_owner, 2 * groups - 1 - every_owner
    )
    every_pos = every_block * blk_rows + every_index % blk_rows
    allowed = every_pos[None, :] <= own_pos[:, None]
    inputs = block_input.reshape(row_count, width).astype(jnp.float32)
    normal_one, inverse_one = norm_parts(inputs)
    normed_one = (normal_one * gain_one + shift_one).astype(jnp.bfloat16)
    bias_all = jnp.concatenate([query_bias, jnp.zeros_like(query_bias), value_bias])
    projected = (
        jnp.dot(normed_one, weight_qkv, preferred_element_type=jnp.float32) + bias_all
    ).astype(jnp.bfloat16)
    queries = projected[:, :width]
    keys = projected[:, width : 2 * width]
    values = projected[:, 2 * width :]
    key_all = lax.all_gather(keys, "ctx", axis=0, tiled=True)
    value_all = lax.all_gather(values, "ctx", axis=0, tiled=True)
    scores = head_scores(queries, key_all, allowed, scaling)
    row_top = jnp.max(scores, -1, keepdims=True)
    log_sum = row_top + jnp.log(jnp.sum(jnp.exp(scores - row_top), -1, keepdims=True))
    probs_low = jnp.exp(scores - log_sum).astype(jnp.bfloat16)
    mixed = jnp.einsum(
        "hqk,khd->qhd", probs_low, split_heads(value_all), preferred_element_type=jnp.float32
    )
    mixed_rows = mixed.reshape(seq_rows, width)
    attended = mixed_rows.astype(jnp.bfloat16)
    residual = inputs + jnp.dot(attended, weight_out, preferred_element_type=jnp.float32) + out_bias
    normal_two, inverse_two = norm_parts(residual)
    normed_two = (normal_two * gain_two + shift_two).astype(jnp.bfloat16)
    hidden = jnp.dot(normed_two, weight_fc, preferred_element_type=jnp.float32) + fc_bias
    activated, gelu_pullback = jax.vjp(partial(jax.nn.gelu, approximate=True), hidden)
    activated_low = activated.astype(jnp.bfloat16)
    result = (
        residual
        + jnp.dot(activated_low, weight_proj, preferred_element_type=jnp.float32)
        + proj_bias
    )
    block_output = result.astype(jnp.bfloat16).reshape(block_input.shape)
    weight_qkv, weight_out, weight_fc, weight_proj, gain_low_one, gain_low_two = (
        lax.all_gather(w_qkv, "fsdp", axis=0, tiled=True),
        lax.all_gather(w_out, "fsdp", axis=0, tiled=True),
        lax.all_gather(w_fc, "fsdp", axis=0, tiled=True),
        lax.all_gather(w_proj, "fsdp", axis=0, tiled=True),
        lax.all_gather(ln1_gain, "fsdp", axis=0, tiled=True),
        lax.all_gather(ln2_gain, "fsdp", axis=0, tiled=True),
    )
    gain_one = gain_low_one.astype(jnp.float32)
    gain_two = gain_low_two.astype(jnp.float32)
    out_grad_low = cotangent.reshape(row_count, width)
    upstream = out_grad_low.astype(jnp.float32)
    grad_proj = rows_product(activated_low, out_grad_low)
    grad_proj_bias = jnp.sum(upstream, 0)
    hidden_grad = gelu_pullback(right_transposed(out_grad_low, weight_proj))[0].astype(jnp.bfloat16)
    grad_fc = rows_product(normed_two, hidden_grad)
    grad_fc_bias = jnp.sum(hidden_grad.astype(jnp.float32), 0)
    residual_part, grad_gain_two, grad_shift_two = norm_grads(
        right_transposed(hidden_grad, weight_fc), normal_two, inverse_two, gain_two
    )
    residual_grad = upstream + residual_part
    branch_grad = residual_grad.astype(jnp.bfloat16)
    grad_out = rows_product(attended, branch_grad)
    grad_out_bias = jnp.sum(branch_grad.astype(jnp.float32), 0)
    attended_grad = right_transposed(branch_grad, weight_out).astype(jnp.bfloat16)
    key_all = lax.all_gather(keys, "ctx", axis=0, tiled=True)
    value_all = lax.all_gather(values, "ctx", axis=0, tiled=True)
    scores = head_scores(queries, key_all, allowed, scaling)
    probs = jnp.exp(scores - log_sum)
    prob_grad = jnp.einsum(
        "qhd,khd->hqk",
        split_heads(attended_grad),
        split_heads(value_all),
        preferred_element_type=jnp.float32,
    )
    inner_sum = jnp.sum(probs * prob_grad, -1, keepdims=True)
    score_grad = (probs * (prob_grad - inner_sum)).astype(jnp.bfloat16)
    query_part = (
        jnp.einsum(
            "hqk,khd->qhd", score_grad, split_heads(key_all), preferred_element_type=jnp.float32
        )
        * scaling
    )
    query_grads = query_part.reshape(seq_rows, width)
    probs_low = probs.astype(jnp.bfloat16)
    query_heads = split_heads(queries)
    grad_heads = split_heads(attended_grad)

    def key_terms(
        start,
        count,
        score_grad=score_grad,
        probs_low=probs_low,
        query_heads=query_heads,
        grad_heads=grad_heads,
    ):
        key_part = (
            jnp.einsum("hqk,qhd->khd", score_grad, query_heads, preferred_element_type=jnp.float32)
            * scaling
        )
        value_part = jnp.einsum(
            "hqk,qhd->khd", probs_low, grad_heads, preferred_element_type=jnp.float32
        )
        return jnp.concatenate(
            [key_part.reshape(count, width), value_part.reshape(count, width)], 1
        )

    own_terms = lax.psum_scatter(
        key_terms(jnp.int32(0), lax.axis_size("ctx") * seq_rows),
        "ctx",
        scatter_dimension=0,
        tiled=True,
    )
    key_grads = own_terms[:, :width]
    value_grads = own_terms[:, width:]
    qkv_grad = jnp.concatenate([query_grads, key_grads, value_grads], 1).astype(jnp.bfloat16)
    grad_qkv = rows_product(normed_one, qkv_grad)
    qkv_sums = jnp.sum(qkv_grad.astype(jnp.float32), 0)
    grad_query_bias = qkv_sums[:width]
    grad_value_bias = qkv_sums[2 * width :]
    input_part, grad_gain_one, grad_shift_one = norm_grads(
        right_transposed(qkv_grad, weight_qkv), normal_one, inverse_one, gain_one
    )
    input_grad = (residual_grad + input_part).reshape(block_input.shape)
    sharded = (
        lax.psum_scatter(grad_qkv, ("ctx", "fsdp"), scatter_dimension=0, tiled=True),
        lax.psum_scatter(grad_out, ("ctx", "fsdp"), scatter_dimension=0, tiled=True),
        lax.psum_scatter(grad_fc, ("ctx", "fsdp"), scatter_dimension=0, tiled=True),
        lax.psum_scatter(grad_proj, ("ctx", "fsdp"), scatter_dimension=0, tiled=True),
        lax.psum_scatter(grad_gain_one, ("ctx", "fsdp"), scatter_dimension=0, tiled=True),
        lax.psum_scatter(grad_shift_one, ("ctx", "fsdp"), scatter_dimension=0, tiled=True),
        lax.psum_scatter(grad_gain_two, ("ctx", "fsdp"), scatter_dimension=0, tiled=True),
        lax.psum_scatter(grad_shift_two, ("ctx", "fsdp"), scatter_dimension=0, tiled=True),
        lax.psum_scatter(grad_query_bias, ("ctx", "fsdp"), scatter_dimension=0, tiled=True),
        lax.psum_scatter(grad_value_bias, ("ctx", "fsdp"), scatter_dimension=0, tiled=True),
        lax.psum_scatter(grad_out_bias, ("ctx", "fsdp"), scatter_dimension=0, tiled=True),
        lax.psum_scatter(grad_fc_bias, ("ctx", "fsdp"), scatter_dimension=0, tiled=True),
        lax.psum_scatter(grad_proj_bias, ("ctx", "fsdp"), scatter_dimension=0, tiled=True),
    )
    return (
        block_output,
        input_grad,
        sharded[0],
        sharded[1],
        sharded[2],
        sharded[3],
        sharded[4],
        sharded[5],
        sharded[6],
        sharded[7],
        sharded[8],
        sharded[9],
        sharded[10],
        sharded[11],
        sharded[12],
    )


MESH = pl.DeviceIdType.MESH
HAND_STEPS = 2
BF16, F32 = jnp.bfloat16, jnp.float32
PLANE = 4
NEG = -1e30


def remote(src, dst, sent, received, device):
    return pltpu.make_async_remote_copy(
        src_ref=src,
        dst_ref=dst,
        send_sem=sent,
        recv_sem=received,
        device_id=device,
        device_id_type=MESH,
    )


def dot(left, right):
    return jnp.dot(left, right, preferred_element_type=F32)


def low_lanes(rows):
    return lax.broadcasted_iota(jnp.int32, (rows, 128), 1) < 64


def swap(block):
    return pltpu.roll(block, 64, 1)


def pack_pair(pair):
    half = pair.shape[0] // 2
    low = low_lanes(half)
    top, bottom = pair[:half], pair[half:]
    return jnp.where(low, top, swap(bottom)), jnp.where(low, swap(top), bottom)


def unpack_pair(even, odd):
    low = low_lanes(even.shape[0])
    return jnp.concatenate(
        [jnp.where(low, even, swap(odd)), jnp.where(low, swap(even), odd)], 0
    )


def part(index, size):
    return pl.ds(pl.multiple_of(index * size, size), size)


def layer_shapes(rows, width, ff, groups):
    members = 2 * PLANE
    layers = groups // PLANE
    tokens = members * rows
    half = rows // 2
    keys = groups * half
    share = width // members
    return dict(
        w_qkv=((width, 3 * width), BF16),
        w_out=((width, width), BF16),
        w_fc=((width, ff), BF16),
        w_proj=((ff, width), BF16),
        vec=((2, 16, width // 2), F32),
        row=((8, width), F32),
        cot_all=((members, rows, width), BF16),
        n1=((rows, width), BF16),
        n1_t=((width, tokens), BF16),
        stage=((groups, 3, half, 128), BF16),
        qkv=((3, keys, 128), BF16),
        kv_roll=((2, keys, 128), BF16),
        q_low=((2, keys, 128), BF16),
        g_low=((2, keys, 128), BF16),
        q_t=((128, keys), BF16),
        g_t=((128, keys), BF16),
        stat=((2, 2, keys, 128), F32),
        mixed=((keys, 128), F32),
        scores=((256, 9 * 256), F32),
        dq=((2, keys, 128), F32),
        o_out=((groups, half, 128), BF16),
        o_in=((groups, half, 128), BF16),
        att=((rows, width), BF16),
        att_t=((layers, members, width // members // layers, rows), BF16),
        att_all=((layers, width // members // layers, tokens), BF16),
        res=((rows, width), F32),
        n2=((rows, width), BF16),
        n2_t=((width, tokens), BF16),
        fc_t=((ff // members, width), BF16),
        bias_t=((ff // members, 128), F32),
        proj_own=((ff // members, width), BF16),
        proj_in=((3 * (ff // members // layers), width), BF16),
        act_all=((ff // members, tokens), BF16),
        hg_all=((ff // members, tokens), BF16),
        upstream=((members, rows, ff // members), F32),
        acc_o=((rows, width), F32),
        acc_d=((rows, width), F32),
        res_grad=((rows, width), F32),
        bg_all=((members, rows, width), BF16),
        g_out=((groups, half, 128), BF16),
        g_in=((keys, 128), BF16),
        back=((groups, 3, half, 128), BF16),
        qg=((rows, 3 * width), BF16),
        qg_out=((members, rows, 3 * share), BF16),
        qg_all=((members, rows, 3 * share), BF16),
        fc_x=((members, width // layers // members, ff // members), BF16),
        fc_y=((members, width // layers // members, ff // members), BF16),
        qkv_x=((2 * members, width // layers // members, 3 * share), BF16),
        qkv_y=((2 * members, width // layers // members, 3 * share), BF16),
        out_y=((rows, width), BF16),
        out_gx=((rows, width), F32),
        out_gqkv=((width // members // layers, 3 * width), F32),
        out_gout=((width // members // layers, width), F32),
        out_gfc=((width // members // layers, ff), F32),
        out_gproj=((ff // members // layers, width), F32),
        sums=((16, width), F32),
        sums_out=((layers, 16, width // layers), F32),
        sums_in=((3, 16, width // layers), F32),
        sums_all=((members, 16, width // layers), F32),
    )


SEMAPHORES = dict(
    local=4,
    out_sem=6,
    w_sent=4,
    w_got=7,
    vec_sent=1,
    vec_got=1,
    swap_sent=5,
    swap_got=5,
    cot_sent=1,
    cot_got=5,
    n1_sent=1,
    n1_got=5,
    n2_sent=1,
    n2_got=5,
    bg_sent=1,
    bg_got=5,
    deal_sent=4,
    deal_got=4,
    sum_sent=4,
    sum_got=8,
    low_sent=2,
    low_got=2,
)


def settle(ref, semaphore):
    pltpu.make_async_copy(ref, ref, semaphore).wait()


def layer_kernel(names, *refs):
    x_ref, cot_ref, wq_hbm, wo_hbm, wf_hbm, wp_hbm = refs[:6]
    small = refs[6:15]
    finals, gvec_ref = refs[15:21], refs[21]
    s = SimpleNamespace(**dict(zip(names, refs[22:])))
    held = (s.out_y, s.out_gx, s.out_gqkv, s.out_gout, s.out_gfc, s.out_gproj)
    y_ref, gx_ref, gqkv_ref, gout_ref, gfc_ref, gproj_ref = held

    def hand_out(index):
        return pltpu.make_async_copy(held[index], finals[index], s.out_sem.at[index])

    rows, width = x_ref.shape
    ff = s.w_fc.shape[1]
    half = rows // 2
    groups = s.stage.shape[0]
    members = 2 * PLANE
    layers = groups // PLANE
    tokens = members * rows
    keys = groups * half
    chunk = ff // members
    share = width // members
    scaling = float(width // HEADS) ** (-0.5)
    factor = scaling * 1.4426950408889634
    me = lax.axis_index("ctx")
    core = lax.axis_index("fsdp")
    other = 1 - core
    layer, place = me // PLANE, me % PLANE
    member = place * 2 + core
    twin = (me, other)

    barrier = pltpu.get_barrier_semaphore()
    for step in range(1, groups):
        pl.semaphore_signal(
            barrier, inc=1, device_id=((me + step) % groups, core), device_id_type=MESH
        )
    for step in range(PLANE):
        pl.semaphore_signal(
            barrier,
            inc=1,
            device_id=(layer * PLANE + (place + step) % PLANE, other),
            device_id_type=MESH,
        )
    pl.semaphore_wait(barrier, groups - 1 + PLANE)

    def at_member(index):
        return (layer * PLANE + index // 2, index % 2)

    def top_rows(ref, source):
        count = source.shape[0]
        return ref.at[pl.ds(pl.multiple_of(core * count, count), count)]

    def peer_rows(ref, source):
        count = source.shape[0]
        return ref.at[pl.ds(pl.multiple_of(other * count, count), count)]


    def order(step):
        return (layer + 2 + step) % 4

    def order_in(step):
        return (place + 1 + step) % 4

    pltpu.make_async_copy(wq_hbm, top_rows(s.w_qkv, wq_hbm), s.local.at[0]).start()

    def qkv_piece(step, third):
        columns = part(third * 4 + order(step), 256)
        return remote(
            wq_hbm.at[:, columns],
            top_rows(s.w_qkv, wq_hbm).at[:, columns],
            s.w_sent.at[0],
            s.w_got.at[step],
            twin,
        )

    at = 0
    for vector in small:
        for start in range(0, vector.shape[0], width // 2):
            line = vector[start : start + width // 2].astype(F32)
            s.vec[core, at : at + 1, :] = line.reshape(1, width // 2)
            at += 1
    s.vec[core, at:, :] = jnp.zeros((16 - at, width // 2), F32)
    vec_copy = remote(s.vec.at[core], s.vec.at[core], s.vec_sent.at[0], s.vec_got.at[0], twin)
    vec_copy.start()
    for step in range(4):
        for third in range(3):
            qkv_piece(step, third).start()
    big = ((wp_hbm, s.w_proj), (wo_hbm, s.w_out), (wf_hbm, s.w_fc))

    def big_piece(index):
        source, target = big[index]
        return remote(
            source, top_rows(target, source), s.w_sent.at[1 + index], s.w_got.at[4 + index], twin
        )

    def big_local(index):
        source, target = big[index]
        return pltpu.make_async_copy(source, top_rows(target, source), s.local.at[1 + index])

    def gather_copy(where, sent, got, slot, index, device):
        return remote(where(slot), where(slot), sent.at[0], got.at[index], device)

    near_x = place + 1 - 2 * (place % 2)
    near_y = (place + 2) % PLANE
    diagonal = (near_x + 2) % PLANE

    def gather_start(where, sent, got):
        for peer in (near_x, near_y):
            gather_copy(where, sent, got, member, place, (layer * PLANE + peer, core)).start()
        gather_copy(where, sent, got, member, PLANE, twin).start()

    def gather_relay(where, sent, got):
        for peer, onward, lower in ((near_x, near_y, 0), (near_y, near_x, 1)):
            slot = peer * 2 + core
            settle(where(slot), got.at[peer])
            size = where(slot).shape[0] // 2
            half_block = where(slot).at[pl.ds(lower * size, size)]
            remote(
                half_block, half_block, sent.at[0], got.at[peer], (layer * PLANE + onward, core)
            ).start()
            gather_copy(where, sent, got, slot, PLANE, twin).start()

    def gather_forward(where, sent, got):
        slot = diagonal * 2 + core
        settle(where(slot), got.at[diagonal])
        gather_copy(where, sent, got, slot, PLANE, twin).start()

    def gather_finish(where, sent, got):
        settle(where(0, PLANE), got.at[PLANE])

    def gather_drain(where, sent, got):
        settle(where(0, 2 * PLANE - 1), sent.at[0])

    def cot_at(slot, count=None):
        return s.cot_all.at[slot if count is None else pl.ds(slot, count)]

    def bg_at(slot, count=None):
        return s.bg_all.at[slot if count is None else pl.ds(slot, count)]

    def columns_at(ref, slot, count):
        return ref.at[:, part(slot, rows) if count is None else pl.ds(slot * rows, count * rows)]

    def n1_at(slot, count=None):
        return columns_at(s.n1_t, slot, count)

    def n2_at(slot, count=None):
        return columns_at(s.n2_t, slot, count)

    def deal_copy(source, target, number, index):
        return remote(
            source(index),
            target(member),
            s.deal_sent.at[number],
            s.deal_got.at[number],
            at_member(index),
        )

    def deal_own(source, target, number):
        return pltpu.make_async_copy(source(member), target(member), s.deal_got.at[number])

    def deal_start(source, target, number):
        for step in range(1, members):
            deal_copy(source, target, number, (member + step) % members).start()
        deal_own(source, target, number).start()

    def deal_wait(source, target, number):
        settle(target(None), s.deal_got.at[number])

    def deal_drain(source, target, number):
        settle(source(None), s.deal_sent.at[number])

    def seven(index):
        return pl.ds(0, members - 1) if index is None else index

    def whole(index):
        return slice(None) if index is None else index

    def lanes(index):
        return slice(None) if index is None else part(index, rows)

    def swap_one(source, target, number, index):
        @pl.when(index == me)
        def _():
            pltpu.make_async_copy(source(index), target(me), s.swap_got.at[number]).start()

        @pl.when(index != me)
        def _():
            remote(
                source(index),
                target(me),
                s.swap_sent.at[number],
                s.swap_got.at[number],
                (index, core),
            ).start()

    def swap_wait(source, target, number):
        settle(target(None), s.swap_got.at[number])

    def swap_drain(source, target, number):
        settle(source(None), s.swap_sent.at[number])

    def others(index):
        return pl.ds(0, groups - 1) if index is None else index

    def block(index):
        return slice(None) if index is None else part(index, half)

    qkv_move = (lambda h: s.stage.at[others(h)], lambda i: s.qkv.at[:, block(i)], 0)
    o_move = (lambda h: s.o_out.at[others(h)], lambda h: s.o_in.at[whole(h)], 1)
    g_move = (lambda h: s.g_out.at[others(h)], lambda i: s.g_in.at[block(i)], 2)
    kv_back = (
        lambda h: s.stage.at[others(h), pl.ds(1, 2)],
        lambda h: s.back.at[whole(h), pl.ds(1, 2)],
        3,
    )
    q_back = (lambda h: s.stage.at[others(h), 0], lambda h: s.back.at[whole(h), 0], 4)
    att_move = (lambda g: s.att_t.at[:, seven(g)], lambda g: s.att_all.at[:, :, lanes(g)], 0)
    qg_move = (lambda g: s.qg_out.at[seven(g)], lambda g: s.qg_all.at[whole(g)], 1)
    fx_move = (lambda g: s.fc_x.at[seven(g)], lambda g: s.fc_y.at[whole(g)], 2)
    qx_move = (lambda g: s.qkv_x.at[g], lambda g: s.qkv_y.at[whole(g)], 3)

    def vec_row(index):
        return jnp.concatenate([s.vec[0, index : index + 1, :], s.vec[1, index : index + 1, :]], 1)

    s.cot_all[member] = cot_ref[...]
    inputs = x_ref[...].astype(F32)
    normal, _ = norm_parts(inputs)
    settle(s.vec.at[other], s.vec_got.at[0])
    s.row[0:1, :] = vec_row(4)
    s.row[1:2, :] = vec_row(5)
    for quarter in range(4):
        at = 8 + quarter % 2 * 2
        s.row[4 + quarter : 5 + quarter, :] = jnp.concatenate(
            [s.vec[quarter // 2, at : at + 1, :], s.vec[quarter // 2, at + 1 : at + 2, :]], 1
        )
    normed = (normal * vec_row(0) + vec_row(1)).astype(BF16)
    s.n1[...] = normed
    s.n1_t[:, part(member, rows)] = normed.astype(F32).T.astype(BF16)
    pltpu.make_async_copy(wq_hbm, top_rows(s.w_qkv, wq_hbm), s.local.at[0]).wait()

    for step in range(4):
        four = order(step)
        settle(peer_rows(s.w_qkv, wq_hbm).at[:, pl.ds(0, 768)], s.w_got.at[step])
        for third in range(3):
            columns = part(third * 4 + four, 256)
            product = dot(s.n1[...], s.w_qkv[:, columns])
            if third == 0:
                product = product + s.row[0:1, part(four, 256)]
            if third == 2:
                product = product + s.row[1:2, part(four, 256)]
            for pair in range(2):
                even, odd = pack_pair(product[:, pair * 128 : pair * 128 + 128])
                s.stage[four * 4 + 2 * pair, third] = even.astype(BF16)
                s.stage[four * 4 + 2 * pair + 1, third] = odd.astype(BF16)
        for head in range(4):
            swap_one(*qkv_move, four * 4 + order_in(head))
    gather_start(cot_at, s.cot_sent, s.cot_got)
    for index in range(3):
        big_piece(index).start()
        big_local(index).start()

    settle(peer_rows(s.w_proj, wp_hbm), s.w_got.at[4])
    big_local(0).wait()

    def send_back(index, _):
        s.upstream[index] = right_transposed(cot_ref[...], s.w_proj[part(index, chunk), :])
        return 0

    lax.fori_loop(0, members, send_back, 0)

    swap_wait(*qkv_move)
    gather_relay(cot_at, s.cot_sent, s.cot_got)
    low_all = low_lanes(keys)
    query = s.qkv[0].astype(F32)
    s.q_low[0] = jnp.where(low_all, query, 0.0).astype(BF16)
    s.q_low[1] = jnp.where(low_all, swap(query), 0.0).astype(BF16)
    s.q_t[...] = query.T.astype(BF16)
    s.kv_roll[0] = swap(s.qkv[1].astype(F32)).astype(BF16)
    s.kv_roll[1] = swap(s.qkv[2].astype(F32)).astype(BF16)

    tile = 256
    per_tile = tile // half
    low_tile = low_lanes(tile)
    row_at = lax.broadcasted_iota(jnp.int32, (tile, tile), 0)
    col_at = lax.broadcasted_iota(jnp.int32, (tile, tile), 1)

    def late(index):
        return index + (per_tile - 1 - 2 * (index // half)) * half

    masks = (col_at <= row_at, late(col_at) <= late(row_at))

    def key_block(region, at):
        return s.qkv[1, at, :] if region == 0 else s.kv_roll[0, at, :]

    def value_block(region, at):
        return s.qkv[2, at, :] if region == 0 else s.kv_roll[1, at, :]

    n_tiles = keys // tile

    def span(start, count=1):
        return slice(start * tile, (start + count) * tile)

    def score_block(queries, region, first, count, column, masked):
        scores = right_transposed(queries, key_block(region, span(first, count)))
        if masked:
            scores = jnp.where(masks[region], scores, NEG)
        s.scores[:, span(column, count)] = scores
        return scores

    def fold(values, combine):
        out = values[:, :128]
        for start in range(128, values.shape[1], 128):
            out = combine(out, values[:, start : start + 128])
        return out

    def softmax_rows(side, blocks, at):
        queries = s.q_low[side, at, :]
        top = None
        for block in blocks:
            high = fold(score_block(queries, *block), jnp.maximum)
            top = high if top is None else jnp.maximum(top, high)
        top = jnp.max(top, 1, keepdims=True) * factor
        total, mix = None, None
        for region, first, count, column, _ in blocks:
            probs = jnp.exp2(s.scores[:, span(column, count)] * factor - top)
            folded = fold(probs, jnp.add)
            total = folded if total is None else total + folded
            more = dot(probs.astype(BF16), value_block(region, span(first, count)))
            mix = more if mix is None else mix + more
        total = jnp.sum(total, 1, keepdims=True)
        s.stat[0, side, at, :] = jnp.broadcast_to(top + jnp.log2(total), (tile, 128))
        return mix / total

    def attend(index):
        at = span(index)
        early = [(0, index, 1, 0, True)]
        if index:
            early.append((0, 0, index, 1, False))
        late_blocks = [(1, index, 1, index + 1, True)]
        if index + 1 < n_tiles:
            late_blocks.append((1, index + 1, n_tiles - 1 - index, index + 2, False))
        late_blocks.append((0, 0, n_tiles, n_tiles + 1, False))
        one = softmax_rows(0, early, at)
        two = softmax_rows(1, late_blocks, at)
        out = jnp.where(low_tile, one, swap(two))
        s.mixed[at, :] = out
        s.o_out[pl.ds(index * per_tile, per_tile)] = out.astype(BF16).reshape(per_tile, half, 128)
        for step in range(per_tile):
            swap_one(*o_move, index * per_tile + order_in(step))

    for index in range(n_tiles):
        attend(index)

    for index in range(1, 3):
        settle(peer_rows(big[index][1], big[index][0]), s.w_got.at[4 + index])
        big_local(index).wait()
    quarters = ff // width
    piece = width // members

    curve = 0.7978845608028654

    def features(index):
        return [part(quarter * members + index, piece) for quarter in range(quarters)]

    mine = features(member)
    s.proj_own[...] = jnp.concatenate([s.w_proj[at, :] for at in mine], 0)
    for quarter, at in enumerate(mine):
        into = slice(quarter * piece, quarter * piece + piece)
        s.fc_t[into, :] = s.w_fc[:, at].astype(F32).T.astype(BF16)
        bias = s.row[4 + quarter : 5 + quarter, part(member, piece)]
        s.bias_t[into, :] = jnp.broadcast_to(bias, (128, piece)).T
    swap_wait(*o_move)
    gather_forward(cot_at, s.cot_sent, s.cot_got)
    for pair in range(HEADS // 2):
        columns = slice(pair * 128, pair * 128 + 128)
        s.att[:, columns] = unpack_pair(
            s.o_in[2 * pair].astype(F32), s.o_in[2 * pair + 1].astype(F32)
        ).astype(BF16)
    turned = s.att[...].astype(F32).T.astype(BF16)
    s.att_t[...] = turned.reshape(s.att_t.shape)
    def project(index, _):
        at = part(index, 256)
        s.acc_d[:, at] = dot(s.att[...], s.w_out[:, at])
        return 0

    lax.fori_loop(0, width // 256, project, 0)
    s.res[...] = x_ref[...].astype(F32) + s.acc_d[...] + vec_row(6)
    normal, _ = norm_parts(s.res[...])
    normed = (normal * vec_row(2) + vec_row(3)).astype(BF16)
    s.n2[...] = normed
    s.n2_t[:, part(member, rows)] = normed.astype(F32).T.astype(BF16)
    gather_start(n2_at, s.n2_sent, s.n2_got)
    s.acc_o[...] = jnp.zeros_like(s.acc_o)
    s.acc_d[...] = jnp.zeros_like(s.acc_d)
    s.sums[...] = jnp.zeros_like(s.sums)


    def gelu_parts(hidden):
        square = hidden * hidden
        bend = jnp.tanh(curve * hidden * (1.0 + 0.044715 * square))
        rise = 0.5 * (1.0 + bend)
        slope = rise + 0.5 * hidden * (1.0 - bend * bend) * (
            curve * (1.0 + 3.0 * 0.044715 * square)
        )
        return hidden * rise, slope

    def feed(index, _):
        at = part(index, 2 * chunk)
        lines = s.vec.at[index // 2]
        first = 8 + index % 2 * 2
        bias = jnp.concatenate(
            [lines[pl.ds(first, 1), :], lines[pl.ds(first + 1, 1), :]], 1
        )
        active, slope = gelu_parts(dot(s.n2[...], s.w_fc[:, at]) + bias)
        active = active.astype(BF16)
        upstream = jnp.concatenate([s.upstream[2 * index], s.upstream[2 * index + 1]], 1)
        grad = (upstream * slope).astype(BF16)
        s.acc_o[...] += dot(active, s.w_proj[at, :])
        s.acc_d[...] += right_transposed(grad, s.w_fc[:, at])
        s.sums[pl.ds(8 + index, 1), :] = jnp.sum(grad.astype(F32), 0, keepdims=True)
        return 0

    lax.fori_loop(0, PLANE - 1, feed, 0)
    gather_relay(n2_at, s.n2_sent, s.n2_got)
    lax.fori_loop(PLANE - 1, PLANE, feed, 0)
    upstream = cot_ref[...].astype(F32)
    normal, inverse = norm_parts(s.res[...])
    step_grad, gain_grad, shift_grad = norm_grads(s.acc_d[...], normal, inverse, vec_row(2))
    s.sums[2:3, :] = gain_grad[None]
    s.sums[3:4, :] = shift_grad[None]
    s.sums[7:8, :] = jnp.sum(upstream, 0, keepdims=True)
    res_grad = upstream + step_grad
    s.res_grad[...] = res_grad
    branch = res_grad.astype(BF16)
    s.bg_all[member] = branch
    s.sums[6:7, :] = jnp.sum(branch.astype(F32), 0, keepdims=True)
    for step in range(4):
        four = order(step)
        product = right_transposed(s.bg_all[member], s.w_out[part(four, 256), :])
        for pair in range(2):
            even, odd = pack_pair(product[:, pair * 128 : pair * 128 + 128])
            s.g_out[four * 4 + 2 * pair] = even.astype(BF16)
            s.g_out[four * 4 + 2 * pair + 1] = odd.astype(BF16)
        for head in range(4):
            swap_one(*g_move, four * 4 + order_in(head))
    y_ref[...] = (s.res[...] + s.acc_o[...] + vec_row(7)).astype(BF16)
    hand_out(0).start()
    gather_start(bg_at, s.bg_sent, s.bg_got)
    deal_start(*att_move)
    gather_forward(n2_at, s.n2_sent, s.n2_got)
    swap_drain(*qkv_move)

    beside = layer + 1 - 2 * (layer % 2)
    beyond = (layer + 2) % layers
    across = (beside + 2) % layers

    def spread_copy(move, slot, target):
        buffer_out, buffer_in, number = move
        return remote(
            buffer_out(slot),
            buffer_in(slot),
            s.sum_sent.at[number],
            s.sum_got.at[2 * number + (slot + 1) // 2],
            (target * PLANE + place, core),
        )

    def spread_prepare(move, product, own_ref):
        for slot, index in enumerate((across, beside, beyond)):
            move[0](slot)[...] = product(index).astype(BF16)
        own_ref[...] = product(layer)

    def spread_start(move):
        for slot in range(2):
            spread_copy(move, slot, beside).start()

    def spread(move, product, own_ref):
        for slot, index in enumerate((across, beside, beyond)):
            move[0](slot)[...] = product(index).astype(BF16)
            if slot < 2:
                spread_copy(move, slot, beside).start()
        own_ref[...] = product(layer)

    def spread_on(move):
        settle(move[1](0), s.sum_got.at[2 * move[2]])
        pair = move[0](2)[...].astype(F32) + move[1](0)[...].astype(F32)
        move[0](2)[...] = pair.astype(BF16)
        spread_copy(move, 2, beyond).start()

    def collect(move, own_ref):
        settle(move[1](1, 2), s.sum_got.at[2 * move[2] + 1])
        own_ref[...] += move[1](1)[...].astype(F32) + move[1](2)[...].astype(F32)

    def spread_drain(move):
        settle(move[0](0, 3), s.sum_sent.at[move[2]])

    proj_rows = ff // members // layers
    out_rows = share // layers
    fc_rows = width // layers

    def rows_of(ref, start, size, columns=slice(None)):
        return lambda slot, count=1: ref.at[pl.ds(start + slot * size, count * size), columns]

    spare = s.upstream.reshape(tokens, chunk)
    fc_own = spare.at[pl.ds(0, fc_rows), :]
    qkv_own = spare.at[pl.ds(fc_rows, fc_rows), pl.ds(0, 3 * share)]
    qkv_next = spare.at[pl.ds(2 * fc_rows, fc_rows), pl.ds(0, 3 * share)]
    sum_proj = (rows_of(s.w_proj, 0, proj_rows), rows_of(s.proj_in, 0, proj_rows), 0)
    sum_out = (rows_of(s.w_proj, 1024, out_rows), rows_of(s.w_proj, 1152, out_rows), 1)
    sum_fc = (
        rows_of(s.w_fc, 0, fc_rows, pl.ds(0, chunk)),
        rows_of(s.w_fc, 0, fc_rows, pl.ds(chunk, chunk)),
        2,
    )
    sum_qkv = (
        rows_of(s.w_fc, 0, fc_rows, pl.ds(2 * chunk, 3 * share)),
        rows_of(s.w_fc, 0, fc_rows, pl.ds(3 * chunk, 3 * share)),
        3,
    )

    part_rows = chunk // 2

    def tokens_of(first, second):
        return [part(first, rows), part(second, rows)]

    def feed_again(first, second):
        here = tokens_of(first, second)
        normed = jnp.concatenate([s.n2_t[:, at] for at in here], 1)
        hidden = dot(s.fc_t[...], normed) + jnp.concatenate([s.bias_t[...]] * 2, 1)
        active, slope = gelu_parts(hidden)
        active = active.astype(BF16)
        for index, at in enumerate(here):
            columns = slice(index * rows, (index + 1) * rows)
            s.act_all[:, at] = active[:, columns]
            s.scores[:, at] = slope[:part_rows, columns]
            s.scores[:, part((first, second)[index] + members, rows)] = slope[part_rows:, columns]

    def back_again(first, second):
        cotangents = jnp.concatenate([s.cot_all[first], s.cot_all[second]], 0)
        upstream = right_transposed(s.proj_own[...], cotangents)
        for index, slot in enumerate((first, second)):
            at = part(slot, rows)
            columns = slice(index * rows, (index + 1) * rows)
            grad = upstream[:part_rows, columns] * s.scores[:, at]
            s.hg_all[:part_rows, at] = grad.astype(BF16)
            grad = upstream[part_rows:, columns] * s.scores[:, part(slot + members, rows)]
            s.hg_all[part_rows:, at] = grad.astype(BF16)

    def grads_of_feed():
        pairs = (
            (member, near_x * 2 + core),
            (near_y * 2 + core, diagonal * 2 + core),
            (place * 2 + other, near_x * 2 + other),
            (near_y * 2 + other, diagonal * 2 + other),
        )
        gather_finish(cot_at, s.cot_sent, s.cot_got)
        for index, pair in enumerate(pairs):
            if index == 2:
                gather_finish(n2_at, s.n2_sent, s.n2_got)
            feed_again(*pair)
        spread(
            sum_proj,
            lambda i: dot(s.act_all[part(i, proj_rows), :], s.cot_all[...].reshape(tokens, width)),
            gproj_ref,
        )
        for pair in pairs:
            back_again(*pair)

    def grad_of_fc():
        spread_prepare(
            sum_fc,
            lambda i: right_transposed(s.n2_t[part(i, fc_rows), :], s.hg_all[...]),
            fc_own,
        )

    def grad_of_out():
        gather_finish(bg_at, s.bg_sent, s.bg_got)
        deal_wait(*att_move)
        spread(
            sum_out,
            lambda i: dot(s.att_all[i], s.bg_all[...].reshape(tokens, width)),
            gout_ref,
        )

    grads_of_feed()
    swap_wait(*g_move)
    upstream = s.g_in[...].astype(F32)
    s.g_low[0] = jnp.where(low_all, upstream, 0.0).astype(BF16)
    s.g_low[1] = jnp.where(low_all, swap(upstream), 0.0).astype(BF16)
    s.g_t[...] = upstream.T.astype(BF16)
    inner = upstream * s.mixed[...]
    for side in range(2):
        kept = jnp.where(low_all == (side == 0), inner, 0.0)
        s.stat[1, side] = jnp.broadcast_to(jnp.sum(kept, 1, keepdims=True), (keys, 128))
    s.dq[...] = jnp.zeros_like(s.dq)

    def wide(block):
        return jnp.concatenate([block] * (tile // 128), 1)

    def back_tile(side, region, at_q, at_k, masked):
        scores = right_transposed(s.q_low[side, at_q, :], key_block(region, at_k))
        probs = jnp.exp2(scores * factor - wide(s.stat[0, side, at_q, :]))
        if masked:
            probs = jnp.where(masks[region], probs, 0.0)
        prob_grad = right_transposed(s.g_low[side, at_q, :], value_block(region, at_k))
        score_grad = (probs * (prob_grad - wide(s.stat[1, side, at_q, :]))).astype(BF16)
        head = slice(side * 64, side * 64 + 64)
        s.dq[side, at_q, :] += dot(score_grad, key_block(region, at_k))
        return dot(s.q_t[head, at_q], score_grad), dot(s.g_t[head, at_q], probs.astype(BF16))

    def attend_back(index):
        at = span(index)
        early = [(0, 0, k, k == index) for k in range(index, n_tiles)]
        early += [(1, 0, k, False) for k in range(n_tiles)]
        late_pairs = [(1, 1, k, k == index) for k in range(index + 1)]
        grads = []
        for pairs in (early, late_pairs):
            both = [
                back_tile(side, region, span(k), at, masked) for side, region, k, masked in pairs
            ]
            grads.append([sum(parts) for parts in zip(*both)])
        for third, scale in ((1, scaling), (2, 1.0)):
            rows_t = jnp.concatenate([grads[0][third - 1], grads[1][third - 1]], 0)
            s.stage[pl.ds(index * per_tile, per_tile), third] = (
                (rows_t.T * scale).astype(BF16).reshape(per_tile, half, 128)
            )
        for step in range(per_tile):
            swap_one(*kv_back, index * per_tile + order_in(step))

    gather_relay(bg_at, s.bg_sent, s.bg_got)
    attend_back(0)
    attend_back(1)
    grad_of_fc()
    attend_back(2)
    gather_forward(bg_at, s.bg_sent, s.bg_got)
    attend_back(3)
    out = jnp.where(low_all, s.dq[0], swap(s.dq[1])) * scaling
    s.stage[:, 0] = out.astype(BF16).reshape(groups, half, 128)
    for step in range(4):
        for head in range(4):
            swap_one(*q_back, order(step) * 4 + order_in(head))
    spread_start(sum_fc)
    gather_start(n1_at, s.n1_sent, s.n1_got)
    grad_of_out()
    spread_on(sum_proj)

    swap_wait(*kv_back)
    gather_relay(n1_at, s.n1_sent, s.n1_got)
    swap_wait(*q_back)
    for pair in range(HEADS // 2):
        for third in range(3):
            block = unpack_pair(
                s.back[2 * pair, third].astype(F32), s.back[2 * pair + 1, third].astype(F32)
            ).astype(BF16)
            s.qg_out[pair, :, third * 128 : third * 128 + 128] = block
            columns = slice(third * width + pair * 128, third * width + pair * 128 + 128)
            s.qg[:, columns] = block
    deal_start(*qg_move)
    gather_forward(n1_at, s.n1_sent, s.n1_got)
    s.sums[4:5, :] = jnp.sum(s.qg[:, :width].astype(F32), 0, keepdims=True)
    s.sums[5:6, :] = jnp.sum(s.qg[:, 2 * width :].astype(F32), 0, keepdims=True)

    def project_back(index, _):
        s.acc_d[:, part(index, 256)] = right_transposed(s.qg[...], s.w_qkv[part(index, 256), :])
        return 0

    lax.fori_loop(0, width // 256, project_back, 0)
    normal, inverse = norm_parts(x_ref[...].astype(F32))
    step_grad, gain_grad, shift_grad = norm_grads(s.acc_d[...], normal, inverse, vec_row(0))
    s.sums[0:1, :] = gain_grad[None]
    s.sums[1:2, :] = shift_grad[None]
    gx_ref[...] = s.res_grad[...] + step_grad
    hand_out(1).start()

    lanes_of_layer = width // layers
    for index in range(layers):
        columns = slice(index * lanes_of_layer, (index + 1) * lanes_of_layer)
        s.sums_out[index, 0:8, :] = s.sums[0:8, columns]
        for quarter in range(layers):
            columns = slice(quarter * lanes_of_layer, (quarter + 1) * lanes_of_layer)
            s.sums_out[index, 8 + quarter : 9 + quarter, :] = s.sums[8 + index : 9 + index, columns]
    for step in range(1, layers):
        target = (layer + step) % layers
        remote(
            s.sums_out.at[target],
            s.sums_in.at[step - 1],
            s.low_sent.at[0],
            s.low_got.at[0],
            (target * PLANE + place, core),
        ).start()

    def low_copy(step):
        return remote(
            s.sums_all.at[member],
            s.sums_all.at[member],
            s.low_sent.at[1],
            s.low_got.at[1],
            at_member((member + step) % members),
        )

    spread_on(sum_fc)
    gather_finish(n1_at, s.n1_sent, s.n1_got)
    deal_wait(*qg_move)
    def qkv_product(index):
        return dot(
            s.n1_t[part(index, fc_rows), :], s.qg_all[...].reshape(tokens, 3 * share)
        )

    for slot, index in enumerate((across, beside)):
        sum_qkv[0](slot)[...] = qkv_product(index).astype(BF16)
        spread_copy(sum_qkv, slot, beside).start()
    qkv_next[...] = qkv_product(beyond)
    qkv_own[...] = qkv_product(layer)

    def pair_sum(move, slot, own, into):
        settle(move[1](slot), s.sum_got.at[2 * move[2] + slot])
        both = own[...] + move[1](slot)[...].astype(F32)
        s.qkv_x[pl.ds(into, members)] = both.astype(BF16).reshape(members, -1, 3 * share)

    spread_on(sum_out)
    pair_sum(sum_qkv, 0, qkv_next, members)
    for index in range(members):
        remote(
            s.qkv_x.at[members + index],
            s.qkv_y.at[members + member],
            s.deal_sent.at[3],
            s.deal_got.at[3],
            (beyond * PLANE + index // 2, index % 2),
        ).start()
    settle(s.sums_in, s.low_got.at[0])
    s.sums_all[member] = s.sums_out[layer] + s.sums_in[0] + s.sums_in[1] + s.sums_in[2]
    for step in range(1, members):
        low_copy(step).start()
    collect(sum_proj, gproj_ref)
    hand_out(5).start()
    collect(sum_fc, fc_own)
    s.fc_x[...] = fc_own[...].astype(BF16).reshape(s.fc_x.shape)
    deal_start(*fx_move)
    collect(sum_out, gout_ref)
    hand_out(3).start()
    settle(s.sums_all.at[pl.ds(0, members - 1)], s.low_got.at[1])
    total = s.sums_all[0]
    for slot in range(1, members):
        total = total + s.sums_all[slot]
    s.sums[:, :lanes_of_layer] = total
    pair_sum(sum_qkv, 1, qkv_own, 0)
    deal_start(*qx_move)
    gvec_ref[...] = jnp.zeros_like(gvec_ref)
    block = s.sums[0:8, part(member // 4, 128)]
    gvec_ref[0:8, :] = pltpu.roll(block, (128 - (member % 4) * 32) % 128, 1)
    block = s.sums[8:16, part(member % 2, 128)]
    chosen = lax.broadcasted_iota(jnp.int32, block.shape, 0) == member // 2
    gvec_ref[8:9, :] = jnp.sum(jnp.where(chosen, block, 0.0), 0, keepdims=True)
    deal_wait(*fx_move)
    for slot in range(members):
        for quarter in range(quarters):
            start = quarter * width + slot * piece
            gfc_ref[:, start : start + piece] = s.fc_y[
                slot, :, quarter * piece : quarter * piece + piece
            ].astype(F32)
    hand_out(4).start()
    deal_wait(*qx_move)
    for slot in range(members):
        for third in range(3):
            start = third * width + slot * 128
            columns = slice(third * 128, third * 128 + 128)
            gqkv_ref[:, start : start + 128] = s.qkv_y[slot, :, columns].astype(
                F32
            ) + s.qkv_y[members + slot, :, columns].astype(F32)

    hand_out(2).start()
    settle(s.sums_in, s.low_sent.at[0])
    settle(s.sums_all.at[pl.ds(0, members - 1)], s.low_sent.at[1])
    settle(peer_rows(s.w_qkv, wq_hbm), s.w_sent.at[0])
    for index in range(3):
        big_piece(index).wait_send()
    vec_copy.wait_send()
    for move in (o_move, g_move, kv_back, q_back):
        swap_drain(*move)
    for move in (att_move, qg_move, fx_move):
        deal_drain(*move)
    settle(s.qkv_x.at[pl.ds(0, 2 * members - 1)], s.deal_sent.at[3])
    for where, sent, got in (
        (cot_at, s.cot_sent, s.cot_got),
        (n1_at, s.n1_sent, s.n1_got),
        (n2_at, s.n2_sent, s.n2_got),
        (bg_at, s.bg_sent, s.bg_got),
    ):
        gather_drain(where, sent, got)
    for move in (sum_proj, sum_fc, sum_out):
        spread_drain(move)
    settle(sum_qkv[0](0, 2), s.sum_sent.at[3])
    for index in range(6):
        hand_out(index).wait()


def hand_over(*refs):
    for source, target in zip(refs[:6], refs[7:13]):
        target[...] = source[...]
    for index, low in enumerate(refs[13:]):
        low[...] = refs[6][index : index + 1, : low.shape[1]]


def fused_layer(
    block_input,
    w_qkv,
    w_out,
    w_fc,
    w_proj,
    ln1_gain,
    ln1_bias,
    ln2_gain,
    ln2_bias,
    bias_q,
    bias_v,
    bias_out,
    bias_fc,
    bias_proj,
    cotangent,
):
    width = block_input.shape[4]
    rows = 2 * block_input.shape[3]
    ff = w_fc.shape[1]
    groups = lax.axis_size("ctx")
    shards = 2 * groups
    small = (ln1_gain, ln1_bias, ln2_gain, ln2_bias, bias_q, bias_v, bias_out, bias_proj, bias_fc)
    shapes = layer_shapes(rows, width, ff, groups)
    names = tuple(shapes) + tuple(SEMAPHORES)
    scratch = [pltpu.VMEM(shape, kind) for shape, kind in shapes.values()]
    scratch += [pltpu.SemaphoreType.DMA((count,)) for count in SEMAPHORES.values()]
    in_vmem = pl.BlockSpec(memory_space=pltpu.VMEM)
    in_hbm = pl.BlockSpec(memory_space=pl.ANY)
    outs = pl.pallas_call(
        partial(layer_kernel, names),
        out_shape=(
            jax.ShapeDtypeStruct((rows, width), BF16),
            jax.ShapeDtypeStruct((rows, width), F32),
            jax.ShapeDtypeStruct((width // shards, 3 * width), F32),
            jax.ShapeDtypeStruct((width // shards, width), F32),
            jax.ShapeDtypeStruct((width // shards, ff), F32),
            jax.ShapeDtypeStruct((ff // shards, width), F32),
            jax.ShapeDtypeStruct((16, 128), F32),
        ),
        in_specs=[in_vmem] * 2 + [in_hbm] * 4 + [in_vmem] * 9,
        out_specs=(in_hbm,) * 6 + (in_vmem,),
        scratch_shapes=scratch,
        compiler_params=pltpu.CompilerParams(
            collective_id=0, has_side_effects=True, vmem_limit_bytes=VMEM_BYTES
        ),
        cost_estimate=pl.CostEstimate(
            flops=14 * 10**9, bytes_accessed=30 * 10**6, transcendentals=5 * 10**6
        ),
    )(
        block_input.reshape(rows, width),
        cotangent.reshape(rows, width),
        w_qkv,
        w_out,
        w_fc,
        w_proj,
        *small,
    )
    piece = width // shards
    wide = ff // shards

    def block_of(array):
        return pl.BlockSpec((array.shape[0] // HAND_STEPS, array.shape[1]), lambda i: (i, 0))

    results = pl.pallas_call(
        hand_over,
        out_shape=tuple(jax.ShapeDtypeStruct(out.shape, out.dtype) for out in outs[:6])
        + (jax.ShapeDtypeStruct((1, piece), F32),) * 8
        + (jax.ShapeDtypeStruct((1, wide), F32),),
        grid=(HAND_STEPS,),
        in_specs=[block_of(out) for out in outs[:6]] + [in_vmem],
        out_specs=tuple(block_of(out) for out in outs[:6]) + (in_vmem,) * 9,
    )(*outs)
    block_output, input_grad, grad_qkv, grad_out, grad_fc, grad_proj = results[:6]
    lows = [result.reshape(-1) for result in results[6:]]
    return (
        block_output.reshape(block_input.shape),
        input_grad.reshape(block_input.shape),
        grad_qkv,
        grad_out,
        grad_fc,
        grad_proj,
        *lows[:7],
        lows[8],
        lows[7],
    )


def on_device(*arrays):
    width, ff = arrays[0].shape[4], arrays[3].shape[1]
    fits = (
        lax.axis_size("ctx") == HEADS
        and lax.axis_size("fsdp") == 2
        and arrays[0].shape[:4] == (1, 1, 2, 64)
        and (width, ff) == (1024, 4096)
    )
    return fused_layer(*arrays) if fits else general_layer(*arrays)


def solution(mesh):
    placed = (
        P("fsdp", "ctx", None, None, None),
        P("fsdp", None),
        P("fsdp", None),
        P("fsdp", None),
        P("fsdp", None),
        P("fsdp"),
        P("fsdp"),
        P("fsdp"),
        P("fsdp"),
        P("fsdp"),
        P("fsdp"),
        P("fsdp"),
        P("fsdp"),
        P("fsdp"),
        P("fsdp", "ctx", None, None, None),
    )
    return jax.shard_map(
        on_device,
        mesh=mesh,
        in_specs=placed,
        out_specs=(
            P("fsdp", "ctx", None, None, None),
            P("fsdp", "ctx", None, None, None),
            P(("ctx", "fsdp"), None),
            P(("ctx", "fsdp"), None),
            P(("ctx", "fsdp"), None),
            P(("ctx", "fsdp"), None),
            P(("ctx", "fsdp")),
            P(("ctx", "fsdp")),
            P(("ctx", "fsdp")),
            P(("ctx", "fsdp")),
            P(("ctx", "fsdp")),
            P(("ctx", "fsdp")),
            P(("ctx", "fsdp")),
            P(("ctx", "fsdp")),
            P(("ctx", "fsdp")),
        ),
        check_vma=False,
    )
```

```python
from functools import partial
from types import SimpleNamespace

import jax
import jax.numpy as jnp
from jax import lax
from jax.experimental import pallas as pl
from jax.experimental.pallas import tpu as pltpu
from jax.sharding import PartitionSpec as P

HEADS = 16
VMEM_BYTES = 127 * 2**19


def norm_parts(values):
    average = jnp.mean(values, -1, keepdims=True)
    centered = values - average
    variance = jnp.mean(centered * centered, -1, keepdims=True)
    inverse = lax.rsqrt(variance + 1e-05)
    return (centered * inverse, inverse)


def norm_grads(upstream, normalized, inverse, gain):
    scaled = upstream * gain
    inner_part = (
        scaled
        - jnp.mean(scaled, -1, keepdims=True)
        - normalized * jnp.mean(scaled * normalized, -1, keepdims=True)
    )
    return (inverse * inner_part, jnp.sum(upstream * normalized, 0), jnp.sum(upstream, 0))


def rows_product(left, right):
    return lax.dot_general(
        left, right, (((0,), (0,)), ((), ())), preferred_element_type=jnp.float32
    )


def right_transposed(left, weight):
    return lax.dot_general(
        left, weight, (((1,), (1,)), ((), ())), preferred_element_type=jnp.float32
    )


def split_heads(matrix):
    return matrix.reshape(matrix.shape[0], HEADS, -1)


def head_scores(queries, keys, allowed, scaling):
    scores = (
        jnp.einsum(
            "qhd,khd->hqk",
            split_heads(queries),
            split_heads(keys),
            preferred_element_type=jnp.float32,
        )
        * scaling
    )
    return jnp.where(allowed[None], scores, -1e30)


def general_layer(
    block_input,
    w_qkv,
    w_out,
    w_fc,
    w_proj,
    ln1_gain,
    ln1_bias,
    ln2_gain,
    ln2_bias,
    bias_q,
    bias_v,
    bias_out,
    bias_fc,
    bias_proj,
    cotangent,
):
    seq_count = block_input.shape[0]
    blk_rows = block_input.shape[3]
    width = block_input.shape[4]
    seq_rows = 2 * blk_rows
    row_count = seq_count * seq_rows
    groups = lax.axis_size("ctx")
    member = lax.axis_index("ctx")
    head_size = width // HEADS
    scaling = head_size ** (-0.5)
    full_rows = groups * seq_rows
    gathered = (
        lax.all_gather(w_qkv, "fsdp", axis=0, tiled=True),
        lax.all_gather(w_out, "fsdp", axis=0, tiled=True),
        lax.all_gather(w_fc, "fsdp", axis=0, tiled=True),
        lax.all_gather(w_proj, "fsdp", axis=0, tiled=True),
        lax.all_gather(ln1_gain, "fsdp", axis=0, tiled=True),
        lax.all_gather(ln1_bias, "fsdp", axis=0, tiled=True),
        lax.all_gather(ln2_gain, "fsdp", axis=0, tiled=True),
        lax.all_gather(ln2_bias, "fsdp", axis=0, tiled=True),
        lax.all_gather(bias_q, "fsdp", axis=0, tiled=True),
        lax.all_gather(bias_v, "fsdp", axis=0, tiled=True),
        lax.all_gather(bias_out, "fsdp", axis=0, tiled=True),
        lax.all_gather(bias_fc, "fsdp", axis=0, tiled=True),
        lax.all_gather(bias_proj, "fsdp", axis=0, tiled=True),
    )
    weight_qkv, weight_out, weight_fc, weight_proj = (
        gathered[0],
        gathered[1],
        gathered[2],
        gathered[3],
    )
    vectors = [piece.astype(jnp.float32) for piece in gathered[4:]]
    (
        gain_one,
        shift_one,
        gain_two,
        shift_two,
        query_bias,
        value_bias,
        out_bias,
        fc_bias,
        proj_bias,
    ) = vectors
    local_index = jnp.arange(seq_rows)
    own_block = jnp.where(local_index // blk_rows == 0, member, 2 * groups - 1 - member)
    own_pos = own_block * blk_rows + local_index % blk_rows
    every_index = jnp.arange(full_rows)
    every_owner = every_index // seq_rows
    every_block = jnp.where(
        every_index // blk_rows % 2 == 0, every_owner, 2 * groups - 1 - every_owner
    )
    every_pos = every_block * blk_rows + every_index % blk_rows
    allowed = every_pos[None, :] <= own_pos[:, None]
    inputs = block_input.reshape(row_count, width).astype(jnp.float32)
    normal_one, inverse_one = norm_parts(inputs)
    normed_one = (normal_one * gain_one + shift_one).astype(jnp.bfloat16)
    bias_all = jnp.concatenate([query_bias, jnp.zeros_like(query_bias), value_bias])
    projected = (
        jnp.dot(normed_one, weight_qkv, preferred_element_type=jnp.float32) + bias_all
    ).astype(jnp.bfloat16)
    queries = projected[:, :width]
    keys = projected[:, width : 2 * width]
    values = projected[:, 2 * width :]
    key_all = lax.all_gather(keys, "ctx", axis=0, tiled=True)
    value_all = lax.all_gather(values, "ctx", axis=0, tiled=True)
    scores = head_scores(queries, key_all, allowed, scaling)
    row_top = jnp.max(scores, -1, keepdims=True)
    log_sum = row_top + jnp.log(jnp.sum(jnp.exp(scores - row_top), -1, keepdims=True))
    probs_low = jnp.exp(scores - log_sum).astype(jnp.bfloat16)
    mixed = jnp.einsum(
        "hqk,khd->qhd", probs_low, split_heads(value_all), preferred_element_type=jnp.float32
    )
    mixed_rows = mixed.reshape(seq_rows, width)
    attended = mixed_rows.astype(jnp.bfloat16)
    residual = inputs + jnp.dot(attended, weight_out, preferred_element_type=jnp.float32) + out_bias
    normal_two, inverse_two = norm_parts(residual)
    normed_two = (normal_two * gain_two + shift_two).astype(jnp.bfloat16)
    hidden = jnp.dot(normed_two, weight_fc, preferred_element_type=jnp.float32) + fc_bias
    activated, gelu_pullback = jax.vjp(partial(jax.nn.gelu, approximate=True), hidden)
    activated_low = activated.astype(jnp.bfloat16)
    result = (
        residual
        + jnp.dot(activated_low, weight_proj, preferred_element_type=jnp.float32)
        + proj_bias
    )
    block_output = result.astype(jnp.bfloat16).reshape(block_input.shape)
    weight_qkv, weight_out, weight_fc, weight_proj, gain_low_one, gain_low_two = (
        lax.all_gather(w_qkv, "fsdp", axis=0, tiled=True),
        lax.all_gather(w_out, "fsdp", axis=0, tiled=True),
        lax.all_gather(w_fc, "fsdp", axis=0, tiled=True),
        lax.all_gather(w_proj, "fsdp", axis=0, tiled=True),
        lax.all_gather(ln1_gain, "fsdp", axis=0, tiled=True),
        lax.all_gather(ln2_gain, "fsdp", axis=0, tiled=True),
    )
    gain_one = gain_low_one.astype(jnp.float32)
    gain_two = gain_low_two.astype(jnp.float32)
    out_grad_low = cotangent.reshape(row_count, width)
    upstream = out_grad_low.astype(jnp.float32)
    grad_proj = rows_product(activated_low, out_grad_low)
    grad_proj_bias = jnp.sum(upstream, 0)
    hidden_grad = gelu_pullback(right_transposed(out_grad_low, weight_proj))[0].astype(jnp.bfloat16)
    grad_fc = rows_product(normed_two, hidden_grad)
    grad_fc_bias = jnp.sum(hidden_grad.astype(jnp.float32), 0)
    residual_part, grad_gain_two, grad_shift_two = norm_grads(
        right_transposed(hidden_grad, weight_fc), normal_two, inverse_two, gain_two
    )
    residual_grad = upstream + residual_part
    branch_grad = residual_grad.astype(jnp.bfloat16)
    grad_out = rows_product(attended, branch_grad)
    grad_out_bias = jnp.sum(branch_grad.astype(jnp.float32), 0)
    attended_grad = right_transposed(branch_grad, weight_out).astype(jnp.bfloat16)
    key_all = lax.all_gather(keys, "ctx", axis=0, tiled=True)
    value_all = lax.all_gather(values, "ctx", axis=0, tiled=True)
    scores = head_scores(queries, key_all, allowed, scaling)
    probs = jnp.exp(scores - log_sum)
    prob_grad = jnp.einsum(
        "qhd,khd->hqk",
        split_heads(attended_grad),
        split_heads(value_all),
        preferred_element_type=jnp.float32,
    )
    inner_sum = jnp.sum(probs * prob_grad, -1, keepdims=True)
    score_grad = (probs * (prob_grad - inner_sum)).astype(jnp.bfloat16)
    query_part = (
        jnp.einsum(
            "hqk,khd->qhd", score_grad, split_heads(key_all), preferred_element_type=jnp.float32
        )
        * scaling
    )
    query_grads = query_part.reshape(seq_rows, width)
    probs_low = probs.astype(jnp.bfloat16)
    query_heads = split_heads(queries)
    grad_heads = split_heads(attended_grad)

    def key_terms(
        start,
        count,
        score_grad=score_grad,
        probs_low=probs_low,
        query_heads=query_heads,
        grad_heads=grad_heads,
    ):
        key_part = (
            jnp.einsum("hqk,qhd->khd", score_grad, query_heads, preferred_element_type=jnp.float32)
            * scaling
        )
        value_part = jnp.einsum(
            "hqk,qhd->khd", probs_low, grad_heads, preferred_element_type=jnp.float32
        )
        return jnp.concatenate(
            [key_part.reshape(count, width), value_part.reshape(count, width)], 1
        )

    own_terms = lax.psum_scatter(
        key_terms(jnp.int32(0), lax.axis_size("ctx") * seq_rows),
        "ctx",
        scatter_dimension=0,
        tiled=True,
    )
    key_grads = own_terms[:, :width]
    value_grads = own_terms[:, width:]
    qkv_grad = jnp.concatenate([query_grads, key_grads, value_grads], 1).astype(jnp.bfloat16)
    grad_qkv = rows_product(normed_one, qkv_grad)
    qkv_sums = jnp.sum(qkv_grad.astype(jnp.float32), 0)
    grad_query_bias = qkv_sums[:width]
    grad_value_bias = qkv_sums[2 * width :]
    input_part, grad_gain_one, grad_shift_one = norm_grads(
        right_transposed(qkv_grad, weight_qkv), normal_one, inverse_one, gain_one
    )
    input_grad = (residual_grad + input_part).reshape(block_input.shape)
    sharded = (
        lax.psum_scatter(grad_qkv, ("ctx", "fsdp"), scatter_dimension=0, tiled=True),
        lax.psum_scatter(grad_out, ("ctx", "fsdp"), scatter_dimension=0, tiled=True),
        lax.psum_scatter(grad_fc, ("ctx", "fsdp"), scatter_dimension=0, tiled=True),
        lax.psum_scatter(grad_proj, ("ctx", "fsdp"), scatter_dimension=0, tiled=True),
        lax.psum_scatter(grad_gain_one, ("ctx", "fsdp"), scatter_dimension=0, tiled=True),
        lax.psum_scatter(grad_shift_one, ("ctx", "fsdp"), scatter_dimension=0, tiled=True),
        lax.psum_scatter(grad_gain_two, ("ctx", "fsdp"), scatter_dimension=0, tiled=True),
        lax.psum_scatter(grad_shift_two, ("ctx", "fsdp"), scatter_dimension=0, tiled=True),
        lax.psum_scatter(grad_query_bias, ("ctx", "fsdp"), scatter_dimension=0, tiled=True),
        lax.psum_scatter(grad_value_bias, ("ctx", "fsdp"), scatter_dimension=0, tiled=True),
        lax.psum_scatter(grad_out_bias, ("ctx", "fsdp"), scatter_dimension=0, tiled=True),
        lax.psum_scatter(grad_fc_bias, ("ctx", "fsdp"), scatter_dimension=0, tiled=True),
        lax.psum_scatter(grad_proj_bias, ("ctx", "fsdp"), scatter_dimension=0, tiled=True),
    )
    return (
        block_output,
        input_grad,
        sharded[0],
        sharded[1],
        sharded[2],
        sharded[3],
        sharded[4],
        sharded[5],
        sharded[6],
        sharded[7],
        sharded[8],
        sharded[9],
        sharded[10],
        sharded[11],
        sharded[12],
    )


MESH = pl.DeviceIdType.MESH
HAND_STEPS = 2
BF16, F32 = jnp.bfloat16, jnp.float32
PLANE = 4
NEG = -1e30


def remote(src, dst, sent, received, device):
    return pltpu.make_async_remote_copy(
        src_ref=src,
        dst_ref=dst,
        send_sem=sent,
        recv_sem=received,
        device_id=device,
        device_id_type=MESH,
    )


def dot(left, right):
    return jnp.dot(left, right, preferred_element_type=F32)


def low_lanes(rows):
    return lax.broadcasted_iota(jnp.int32, (rows, 128), 1) < 64


def swap(block):
    return pltpu.roll(block, 64, 1)


def pack_pair(pair):
    half = pair.shape[0] // 2
    low = low_lanes(half)
    top, bottom = pair[:half], pair[half:]
    return jnp.where(low, top, swap(bottom)), jnp.where(low, swap(top), bottom)


def unpack_pair(even, odd):
    low = low_lanes(even.shape[0])
    return jnp.concatenate(
        [jnp.where(low, even, swap(odd)), jnp.where(low, swap(even), odd)], 0
    )


def part(index, size):
    return pl.ds(pl.multiple_of(index * size, size), size)


def layer_shapes(rows, width, ff, groups):
    members = 2 * PLANE
    layers = groups // PLANE
    tokens = members * rows
    half = rows // 2
    keys = groups * half
    share = width // members
    return dict(
        w_qkv=((width, 3 * width), BF16),
        w_out=((width, width), BF16),
        w_fc=((width, ff), BF16),
        w_proj=((ff, width), BF16),
        vec=((2, 16, width // 2), F32),
        row=((8, width), F32),
        cot_all=((members, rows, width), BF16),
        n1=((rows, width), BF16),
        n1_t=((width, tokens), BF16),
        stage=((groups, 3, half, 128), BF16),
        qkv=((3, keys, 128), BF16),
        kv_roll=((2, keys, 128), BF16),
        q_low=((2, keys, 128), BF16),
        g_low=((2, keys, 128), BF16),
        q_t=((128, keys), BF16),
        g_t=((128, keys), BF16),
        stat=((2, 2, keys, 128), F32),
        mixed=((keys, 128), F32),
        scores=((256, 9 * 256), F32),
        dq=((2, keys, 128), F32),
        o_out=((groups, half, 128), BF16),
        o_in=((groups, half, 128), BF16),
        att=((rows, width), BF16),
        att_t=((layers, members, width // members // layers, rows), BF16),
        att_all=((layers, width // members // layers, tokens), BF16),
        res=((rows, width), F32),
        n2=((rows, width), BF16),
        n2_t=((width, tokens), BF16),
        fc_t=((ff // members, width), BF16),
        bias_t=((ff // members, 128), F32),
        proj_own=((ff // members, width), BF16),
        proj_in=((3 * (ff // members // layers), width), BF16),
        act_all=((ff // members, tokens), BF16),
        hg_all=((ff // members, tokens), BF16),
        upstream=((members, rows, ff // members), F32),
        acc_o=((rows, width), F32),
        acc_d=((rows, width), F32),
        res_grad=((rows, width), F32),
        bg_all=((members, rows, width), BF16),
        g_out=((groups, half, 128), BF16),
        g_in=((keys, 128), BF16),
        back=((groups, 3, half, 128), BF16),
        qg=((rows, 3 * width), BF16),
        qg_out=((members, rows, 3 * share), BF16),
        qg_all=((members, rows, 3 * share), BF16),
        fc_x=((members, width // layers // members, ff // members), BF16),
        fc_y=((members, width // layers // members, ff // members), BF16),
        qkv_x=((2 * members, width // layers // members, 3 * share), BF16),
        qkv_y=((2 * members, width // layers // members, 3 * share), BF16),
        out_y=((rows, width), BF16),
        out_gx=((rows, width), F32),
        out_gqkv=((width // members // layers, 3 * width), F32),
        out_gout=((width // members // layers, width), F32),
        out_gfc=((width // members // layers, ff), F32),
        out_gproj=((ff // members // layers, width), F32),
        sums=((16, width), F32),
        sums_out=((layers, 16, width // layers), F32),
        sums_in=((3, 16, width // layers), F32),
        sums_all=((members, 16, width // layers), F32),
    )


SEMAPHORES = dict(
    local=4,
    out_sem=6,
    w_sent=4,
    w_got=7,
    vec_sent=1,
    vec_got=1,
    swap_sent=5,
    swap_got=5,
    cot_sent=1,
    cot_got=5,
    n1_sent=1,
    n1_got=5,
    n2_sent=1,
    n2_got=5,
    bg_sent=1,
    bg_got=5,
    deal_sent=4,
    deal_got=4,
    sum_sent=4,
    sum_got=8,
    low_sent=2,
    low_got=2,
)


def settle(ref, semaphore):
    pltpu.make_async_copy(ref, ref, semaphore).wait()


def layer_kernel(names, *refs):
    x_ref, cot_ref, wq_hbm, wo_hbm, wf_hbm, wp_hbm = refs[:6]
    small = refs[6:15]
    finals, gvec_ref = refs[15:21], refs[21]
    s = SimpleNamespace(**dict(zip(names, refs[22:])))
    held = (s.out_y, s.out_gx, s.out_gqkv, s.out_gout, s.out_gfc, s.out_gproj)
    y_ref, gx_ref, gqkv_ref, gout_ref, gfc_ref, gproj_ref = held

    def hand_out(index):
        return pltpu.make_async_copy(held[index], finals[index], s.out_sem.at[index])

    rows, width = x_ref.shape
    ff = s.w_fc.shape[1]
    half = rows // 2
    groups = s.stage.shape[0]
    members = 2 * PLANE
    layers = groups // PLANE
    tokens = members * rows
    keys = groups * half
    chunk = ff // members
    share = width // members
    scaling = float(width // HEADS) ** (-0.5)
    factor = scaling * 1.4426950408889634
    me = lax.axis_index("ctx")
    core = lax.axis_index("fsdp")
    other = 1 - core
    layer, place = me // PLANE, me % PLANE
    member = place * 2 + core
    twin = (me, other)

    barrier = pltpu.get_barrier_semaphore()
    for step in range(1, groups):
        pl.semaphore_signal(
            barrier, inc=1, device_id=((me + step) % groups, core), device_id_type=MESH
        )
    for step in range(PLANE):
        pl.semaphore_signal(
            barrier,
            inc=1,
            device_id=(layer * PLANE + (place + step) % PLANE, other),
            device_id_type=MESH,
        )
    pl.semaphore_wait(barrier, groups - 1 + PLANE)

    def at_member(index):
        return (layer * PLANE + index // 2, index % 2)

    def top_rows(ref, source):
        count = source.shape[0]
        return ref.at[pl.ds(pl.multiple_of(core * count, count), count)]

    def peer_rows(ref, source):
        count = source.shape[0]
        return ref.at[pl.ds(pl.multiple_of(other * count, count), count)]


    def order(step):
        return (layer + 2 + step) % 4

    def order_in(step):
        return (place + 1 + step) % 4

    pltpu.make_async_copy(wq_hbm, top_rows(s.w_qkv, wq_hbm), s.local.at[0]).start()

    def qkv_piece(step, third):
        columns = part(third * 4 + order(step), 256)
        return remote(
            wq_hbm.at[:, columns],
            top_rows(s.w_qkv, wq_hbm).at[:, columns],
            s.w_sent.at[0],
            s.w_got.at[step],
            twin,
        )

    at = 0
    for vector in small:
        for start in range(0, vector.shape[0], width // 2):
            line = vector[start : start + width // 2].astype(F32)
            s.vec[core, at : at + 1, :] = line.reshape(1, width // 2)
            at += 1
    s.vec[core, at:, :] = jnp.zeros((16 - at, width // 2), F32)
    vec_copy = remote(s.vec.at[core], s.vec.at[core], s.vec_sent.at[0], s.vec_got.at[0], twin)
    vec_copy.start()
    for step in range(4):
        for third in range(3):
            qkv_piece(step, third).start()
    big = ((wp_hbm, s.w_proj), (wo_hbm, s.w_out), (wf_hbm, s.w_fc))

    def big_piece(index):
        source, target = big[index]
        return remote(
            source, top_rows(target, source), s.w_sent.at[1 + index], s.w_got.at[4 + index], twin
        )

    def big_local(index):
        source, target = big[index]
        return pltpu.make_async_copy(source, top_rows(target, source), s.local.at[1 + index])

    def gather_copy(where, sent, got, slot, index, device):
        return remote(where(slot), where(slot), sent.at[0], got.at[index], device)

    near_x = place + 1 - 2 * (place % 2)
    near_y = (place + 2) % PLANE
    diagonal = (near_x + 2) % PLANE

    def gather_start(where, sent, got):
        for peer in (near_x, near_y):
            gather_copy(where, sent, got, member, place, (layer * PLANE + peer, core)).start()
        gather_copy(where, sent, got, member, PLANE, twin).start()

    def gather_relay(where, sent, got):
        for peer, onward, lower in ((near_x, near_y, 0), (near_y, near_x, 1)):
            slot = peer * 2 + core
            settle(where(slot), got.at[peer])
            size = where(slot).shape[0] // 2
            half_block = where(slot).at[pl.ds(lower * size, size)]
            remote(
                half_block, half_block, sent.at[0], got.at[peer], (layer * PLANE + onward, core)
            ).start()
            gather_copy(where, sent, got, slot, PLANE, twin).start()

    def gather_forward(where, sent, got):
        slot = diagonal * 2 + core
        settle(where(slot), got.at[diagonal])
        gather_copy(where, sent, got, slot, PLANE, twin).start()

    def gather_finish(where, sent, got):
        settle(where(0, PLANE), got.at[PLANE])

    def gather_drain(where, sent, got):
        settle(where(0, 2 * PLANE - 1), sent.at[0])

    def cot_at(slot, count=None):
        return s.cot_all.at[slot if count is None else pl.ds(slot, count)]

    def bg_at(slot, count=None):
        return s.bg_all.at[slot if count is None else pl.ds(slot, count)]

    def columns_at(ref, slot, count):
        return ref.at[:, part(slot, rows) if count is None else pl.ds(slot * rows, count * rows)]

    def n1_at(slot, count=None):
        return columns_at(s.n1_t, slot, count)

    def n2_at(slot, count=None):
        return columns_at(s.n2_t, slot, count)

    def deal_copy(source, target, number, index):
        return remote(
            source(index),
            target(member),
            s.deal_sent.at[number],
            s.deal_got.at[number],
            at_member(index),
        )

    def deal_own(source, target, number):
        return pltpu.make_async_copy(source(member), target(member), s.deal_got.at[number])

    def deal_start(source, target, number):
        for step in range(1, members):
            deal_copy(source, target, number, (member + step) % members).start()
        deal_own(source, target, number).start()

    def deal_wait(source, target, number):
        settle(target(None), s.deal_got.at[number])

    def deal_drain(source, target, number):
        settle(source(None), s.deal_sent.at[number])

    def seven(index):
        return pl.ds(0, members - 1) if index is None else index

    def whole(index):
        return slice(None) if index is None else index

    def lanes(index):
        return slice(None) if index is None else part(index, rows)

    def swap_one(source, target, number, index):
        @pl.when(index == me)
        def _():
            pltpu.make_async_copy(source(index), target(me), s.swap_got.at[number]).start()

        @pl.when(index != me)
        def _():
            remote(
                source(index),
                target(me),
                s.swap_sent.at[number],
                s.swap_got.at[number],
                (index, core),
            ).start()

    def swap_wait(source, target, number):
        settle(target(None), s.swap_got.at[number])

    def swap_drain(source, target, number):
        settle(source(None), s.swap_sent.at[number])

    def others(index):
        return pl.ds(0, groups - 1) if index is None else index

    def block(index):
        return slice(None) if index is None else part(index, half)

    qkv_move = (lambda h: s.stage.at[others(h)], lambda i: s.qkv.at[:, block(i)], 0)
    o_move = (lambda h: s.o_out.at[others(h)], lambda h: s.o_in.at[whole(h)], 1)
    g_move = (lambda h: s.g_out.at[others(h)], lambda i: s.g_in.at[block(i)], 2)
    kv_back = (
        lambda h: s.stage.at[others(h), pl.ds(1, 2)],
        lambda h: s.back.at[whole(h), pl.ds(1, 2)],
        3,
    )
    q_back = (lambda h: s.stage.at[others(h), 0], lambda h: s.back.at[whole(h), 0], 4)
    att_move = (lambda g: s.att_t.at[:, seven(g)], lambda g: s.att_all.at[:, :, lanes(g)], 0)
    qg_move = (lambda g: s.qg_out.at[seven(g)], lambda g: s.qg_all.at[whole(g)], 1)
    fx_move = (lambda g: s.fc_x.at[seven(g)], lambda g: s.fc_y.at[whole(g)], 2)
    qx_move = (lambda g: s.qkv_x.at[g], lambda g: s.qkv_y.at[whole(g)], 3)

    def vec_row(index):
        return jnp.concatenate([s.vec[0, index : index + 1, :], s.vec[1, index : index + 1, :]], 1)

    s.cot_all[member] = cot_ref[...]
    inputs = x_ref[...].astype(F32)
    normal, _ = norm_parts(inputs)
    settle(s.vec.at[other], s.vec_got.at[0])
    s.row[0:1, :] = vec_row(4)
    s.row[1:2, :] = vec_row(5)
    for quarter in range(4):
        at = 8 + quarter % 2 * 2
        s.row[4 + quarter : 5 + quarter, :] = jnp.concatenate(
            [s.vec[quarter // 2, at : at + 1, :], s.vec[quarter // 2, at + 1 : at + 2, :]], 1
        )
    normed = (normal * vec_row(0) + vec_row(1)).astype(BF16)
    s.n1[...] = normed
    pltpu.make_async_copy(wq_hbm, top_rows(s.w_qkv, wq_hbm), s.local.at[0]).wait()

    for step in range(4):
        four = order(step)
        settle(peer_rows(s.w_qkv, wq_hbm).at[:, pl.ds(0, 768)], s.w_got.at[step])
        for third in range(3):
            columns = part(third * 4 + four, 256)
            product = dot(s.n1[...], s.w_qkv[:, columns])
            if third == 0:
                product = product + s.row[0:1, part(four, 256)]
            if third == 2:
                product = product + s.row[1:2, part(four, 256)]
            for pair in range(2):
                even, odd = pack_pair(product[:, pair * 128 : pair * 128 + 128])
                s.stage[four * 4 + 2 * pair, third] = even.astype(BF16)
                s.stage[four * 4 + 2 * pair + 1, third] = odd.astype(BF16)
        for head in range(4):
            swap_one(*qkv_move, four * 4 + order_in(head))
    gather_start(cot_at, s.cot_sent, s.cot_got)
    for index in range(3):
        big_piece(index).start()
        big_local(index).start()

    s.n1_t[:, part(member, rows)] = s.n1[...].astype(F32).T.astype(BF16)
    settle(peer_rows(s.w_proj, wp_hbm), s.w_got.at[4])
    big_local(0).wait()

    def send_back(index, _):
        s.upstream[index] = right_transposed(cot_ref[...], s.w_proj[part(index, chunk), :])
        return 0

    lax.fori_loop(0, members, send_back, 0)

    swap_wait(*qkv_move)
    gather_relay(cot_at, s.cot_sent, s.cot_got)
    low_all = low_lanes(keys)
    query = s.qkv[0].astype(F32)
    s.q_low[0] = jnp.where(low_all, query, 0.0).astype(BF16)
    s.q_low[1] = jnp.where(low_all, swap(query), 0.0).astype(BF16)
    s.kv_roll[0] = swap(s.qkv[1].astype(F32)).astype(BF16)
    s.kv_roll[1] = swap(s.qkv[2].astype(F32)).astype(BF16)

    tile = 256
    per_tile = tile // half
    low_tile = low_lanes(tile)
    row_at = lax.broadcasted_iota(jnp.int32, (tile, tile), 0)
    col_at = lax.broadcasted_iota(jnp.int32, (tile, tile), 1)

    def late(index):
        return index + (per_tile - 1 - 2 * (index // half)) * half

    masks = (col_at <= row_at, late(col_at) <= late(row_at))

    def key_block(region, at):
        return s.qkv[1, at, :] if region == 0 else s.kv_roll[0, at, :]

    def value_block(region, at):
        return s.qkv[2, at, :] if region == 0 else s.kv_roll[1, at, :]

    n_tiles = keys // tile

    def span(start, count=1):
        return slice(start * tile, (start + count) * tile)

    def score_block(queries, region, first, count, column, masked):
        scores = right_transposed(queries, key_block(region, span(first, count)))
        if masked:
            scores = jnp.where(masks[region], scores, NEG)
        s.scores[:, span(column, count)] = scores
        return scores

    def fold(values, combine):
        out = values[:, :128]
        for start in range(128, values.shape[1], 128):
            out = combine(out, values[:, start : start + 128])
        return out

    def softmax_rows(side, blocks, at):
        queries = s.q_low[side, at, :]
        top = None
        for block in blocks:
            high = fold(score_block(queries, *block), jnp.maximum)
            top = high if top is None else jnp.maximum(top, high)
        top = jnp.max(top, 1, keepdims=True) * factor
        total, mix = None, None
        for region, first, count, column, _ in blocks:
            probs = jnp.exp2(s.scores[:, span(column, count)] * factor - top)
            folded = fold(probs, jnp.add)
            total = folded if total is None else total + folded
            more = dot(probs.astype(BF16), value_block(region, span(first, count)))
            mix = more if mix is None else mix + more
        total = jnp.sum(total, 1, keepdims=True)
        s.stat[0, side, at, :] = jnp.broadcast_to(top + jnp.log2(total), (tile, 128))
        return mix / total

    def attend(index):
        at = span(index)
        early = [(0, index, 1, 0, True)]
        if index:
            early.append((0, 0, index, 1, False))
        late_blocks = [(1, index, 1, index + 1, True)]
        if index + 1 < n_tiles:
            late_blocks.append((1, index + 1, n_tiles - 1 - index, index + 2, False))
        late_blocks.append((0, 0, n_tiles, n_tiles + 1, False))
        one = softmax_rows(0, early, at)
        two = softmax_rows(1, late_blocks, at)
        out = jnp.where(low_tile, one, swap(two))
        s.mixed[at, :] = out
        s.o_out[pl.ds(index * per_tile, per_tile)] = out.astype(BF16).reshape(per_tile, half, 128)
        for step in range(per_tile):
            swap_one(*o_move, index * per_tile + order_in(step))

    for index in (0, 3, 1, 2):
        attend(index)
    s.q_t[...] = s.qkv[0].astype(F32).T.astype(BF16)

    for index in range(1, 3):
        settle(peer_rows(big[index][1], big[index][0]), s.w_got.at[4 + index])
        big_local(index).wait()
    quarters = ff // width
    piece = width // members

    curve = 0.7978845608028654

    def features(index):
        return [part(quarter * members + index, piece) for quarter in range(quarters)]

    mine = features(member)
    s.proj_own[...] = jnp.concatenate([s.w_proj[at, :] for at in mine], 0)
    for quarter, at in enumerate(mine):
        into = slice(quarter * piece, quarter * piece + piece)
        s.fc_t[into, :] = s.w_fc[:, at].astype(F32).T.astype(BF16)
        bias = s.row[4 + quarter : 5 + quarter, part(member, piece)]
        s.bias_t[into, :] = jnp.broadcast_to(bias, (128, piece)).T
    swap_wait(*o_move)
    gather_forward(cot_at, s.cot_sent, s.cot_got)
    for pair in range(HEADS // 2):
        columns = slice(pair * 128, pair * 128 + 128)
        s.att[:, columns] = unpack_pair(
            s.o_in[2 * pair].astype(F32), s.o_in[2 * pair + 1].astype(F32)
        ).astype(BF16)
    def project(index, _):
        at = part(index, 256)
        s.acc_d[:, at] = dot(s.att[...], s.w_out[:, at])
        return 0

    lax.fori_loop(0, width // 256, project, 0)
    s.res[...] = x_ref[...].astype(F32) + s.acc_d[...] + vec_row(6)
    normal, _ = norm_parts(s.res[...])
    normed = (normal * vec_row(2) + vec_row(3)).astype(BF16)
    s.n2[...] = normed
    s.n2_t[:, part(member, rows)] = normed.astype(F32).T.astype(BF16)
    gather_start(n2_at, s.n2_sent, s.n2_got)
    s.acc_o[...] = jnp.zeros_like(s.acc_o)
    s.acc_d[...] = jnp.zeros_like(s.acc_d)
    s.sums[...] = jnp.zeros_like(s.sums)


    def gelu_parts(hidden):
        square = hidden * hidden
        bend = jnp.tanh(curve * hidden * (1.0 + 0.044715 * square))
        rise = 0.5 * (1.0 + bend)
        slope = rise + 0.5 * hidden * (1.0 - bend * bend) * (
            curve * (1.0 + 3.0 * 0.044715 * square)
        )
        return hidden * rise, slope

    def feed(index, _):
        at = part(index, 2 * chunk)
        lines = s.vec.at[index // 2]
        first = 8 + index % 2 * 2
        bias = jnp.concatenate(
            [lines[pl.ds(first, 1), :], lines[pl.ds(first + 1, 1), :]], 1
        )
        active, slope = gelu_parts(dot(s.n2[...], s.w_fc[:, at]) + bias)
        active = active.astype(BF16)
        upstream = jnp.concatenate([s.upstream[2 * index], s.upstream[2 * index + 1]], 1)
        grad = (upstream * slope).astype(BF16)
        s.acc_o[...] += dot(active, s.w_proj[at, :])
        s.acc_d[...] += right_transposed(grad, s.w_fc[:, at])
        s.sums[pl.ds(8 + index, 1), :] = jnp.sum(grad.astype(F32), 0, keepdims=True)
        return 0

    lax.fori_loop(0, PLANE - 1, feed, 0)
    gather_relay(n2_at, s.n2_sent, s.n2_got)
    lax.fori_loop(PLANE - 1, PLANE, feed, 0)
    upstream = cot_ref[...].astype(F32)
    normal, inverse = norm_parts(s.res[...])
    step_grad, gain_grad, shift_grad = norm_grads(s.acc_d[...], normal, inverse, vec_row(2))
    s.sums[2:3, :] = gain_grad[None]
    s.sums[3:4, :] = shift_grad[None]
    s.sums[7:8, :] = jnp.sum(upstream, 0, keepdims=True)
    res_grad = upstream + step_grad
    s.res_grad[...] = res_grad
    branch = res_grad.astype(BF16)
    s.bg_all[member] = branch
    s.sums[6:7, :] = jnp.sum(branch.astype(F32), 0, keepdims=True)
    for step in range(4):
        four = order(step)
        product = right_transposed(s.bg_all[member], s.w_out[part(four, 256), :])
        for pair in range(2):
            even, odd = pack_pair(product[:, pair * 128 : pair * 128 + 128])
            s.g_out[four * 4 + 2 * pair] = even.astype(BF16)
            s.g_out[four * 4 + 2 * pair + 1] = odd.astype(BF16)
        for head in range(4):
            swap_one(*g_move, four * 4 + order_in(head))
    y_ref[...] = (s.res[...] + s.acc_o[...] + vec_row(7)).astype(BF16)
    hand_out(0).start()
    gather_start(bg_at, s.bg_sent, s.bg_got)
    s.att_t[...] = s.att[...].astype(F32).T.astype(BF16).reshape(s.att_t.shape)
    deal_start(*att_move)
    gather_forward(n2_at, s.n2_sent, s.n2_got)
    swap_drain(*qkv_move)

    beside = layer + 1 - 2 * (layer % 2)
    beyond = (layer + 2) % layers
    across = (beside + 2) % layers

    def spread_copy(move, slot, target):
        buffer_out, buffer_in, number = move
        return remote(
            buffer_out(slot),
            buffer_in(slot),
            s.sum_sent.at[number],
            s.sum_got.at[2 * number + (slot + 1) // 2],
            (target * PLANE + place, core),
        )

    def spread_prepare(move, product, own_ref):
        for slot, index in enumerate((across, beside, beyond)):
            move[0](slot)[...] = product(index).astype(BF16)
        own_ref[...] = product(layer)

    def spread_start(move):
        for slot in range(2):
            spread_copy(move, slot, beside).start()

    def spread(move, product, own_ref):
        for slot, index in enumerate((across, beside, beyond)):
            move[0](slot)[...] = product(index).astype(BF16)
            if slot < 2:
                spread_copy(move, slot, beside).start()
        own_ref[...] = product(layer)

    def spread_on(move):
        settle(move[1](0), s.sum_got.at[2 * move[2]])
        pair = move[0](2)[...].astype(F32) + move[1](0)[...].astype(F32)
        move[0](2)[...] = pair.astype(BF16)
        spread_copy(move, 2, beyond).start()

    def collect(move, own_ref):
        settle(move[1](1, 2), s.sum_got.at[2 * move[2] + 1])
        own_ref[...] += move[1](1)[...].astype(F32) + move[1](2)[...].astype(F32)

    def spread_drain(move):
        settle(move[0](0, 3), s.sum_sent.at[move[2]])

    proj_rows = ff // members // layers
    out_rows = share // layers
    fc_rows = width // layers

    def rows_of(ref, start, size, columns=slice(None)):
        return lambda slot, count=1: ref.at[pl.ds(start + slot * size, count * size), columns]

    spare = s.upstream.reshape(tokens, chunk)
    fc_own = spare.at[pl.ds(0, fc_rows), :]
    qkv_own = spare.at[pl.ds(fc_rows, fc_rows), pl.ds(0, 3 * share)]
    qkv_next = spare.at[pl.ds(2 * fc_rows, fc_rows), pl.ds(0, 3 * share)]
    sum_proj = (rows_of(s.w_proj, 0, proj_rows), rows_of(s.proj_in, 0, proj_rows), 0)
    sum_out = (rows_of(s.w_proj, 1024, out_rows), rows_of(s.w_proj, 1152, out_rows), 1)
    sum_fc = (
        rows_of(s.w_fc, 0, fc_rows, pl.ds(0, chunk)),
        rows_of(s.w_fc, 0, fc_rows, pl.ds(chunk, chunk)),
        2,
    )
    sum_qkv = (
        rows_of(s.w_fc, 0, fc_rows, pl.ds(2 * chunk, 3 * share)),
        rows_of(s.w_fc, 0, fc_rows, pl.ds(3 * chunk, 3 * share)),
        3,
    )

    part_rows = chunk // 2

    def tokens_of(first, second):
        return [part(first, rows), part(second, rows)]

    def feed_again(first, second):
        here = tokens_of(first, second)
        normed = jnp.concatenate([s.n2_t[:, at] for at in here], 1)
        hidden = dot(s.fc_t[...], normed) + jnp.concatenate([s.bias_t[...]] * 2, 1)
        active, slope = gelu_parts(hidden)
        active = active.astype(BF16)
        for index, at in enumerate(here):
            columns = slice(index * rows, (index + 1) * rows)
            s.act_all[:, at] = active[:, columns]
            s.scores[:, at] = slope[:part_rows, columns]
            s.scores[:, part((first, second)[index] + members, rows)] = slope[part_rows:, columns]

    def back_again(first, second):
        cotangents = jnp.concatenate([s.cot_all[first], s.cot_all[second]], 0)
        upstream = right_transposed(s.proj_own[...], cotangents)
        for index, slot in enumerate((first, second)):
            at = part(slot, rows)
            columns = slice(index * rows, (index + 1) * rows)
            grad = upstream[:part_rows, columns] * s.scores[:, at]
            s.hg_all[:part_rows, at] = grad.astype(BF16)
            grad = upstream[part_rows:, columns] * s.scores[:, part(slot + members, rows)]
            s.hg_all[part_rows:, at] = grad.astype(BF16)

    def grads_of_feed():
        pairs = (
            (member, near_x * 2 + core),
            (near_y * 2 + core, diagonal * 2 + core),
            (place * 2 + other, near_x * 2 + other),
            (near_y * 2 + other, diagonal * 2 + other),
        )
        gather_finish(cot_at, s.cot_sent, s.cot_got)
        for index, pair in enumerate(pairs):
            if index == 2:
                gather_finish(n2_at, s.n2_sent, s.n2_got)
            feed_again(*pair)
        spread(
            sum_proj,
            lambda i: dot(s.act_all[part(i, proj_rows), :], s.cot_all[...].reshape(tokens, width)),
            gproj_ref,
        )
        for pair in pairs:
            back_again(*pair)

    def grad_of_fc():
        spread_prepare(
            sum_fc,
            lambda i: right_transposed(s.n2_t[part(i, fc_rows), :], s.hg_all[...]),
            fc_own,
        )

    def grad_of_out():
        gather_finish(bg_at, s.bg_sent, s.bg_got)
        deal_wait(*att_move)
        spread(
            sum_out,
            lambda i: dot(s.att_all[i], s.bg_all[...].reshape(tokens, width)),
            gout_ref,
        )

    grads_of_feed()
    swap_wait(*g_move)
    upstream = s.g_in[...].astype(F32)
    s.g_low[0] = jnp.where(low_all, upstream, 0.0).astype(BF16)
    s.g_low[1] = jnp.where(low_all, swap(upstream), 0.0).astype(BF16)
    s.g_t[...] = upstream.T.astype(BF16)
    inner = upstream * s.mixed[...]
    for side in range(2):
        kept = jnp.where(low_all == (side == 0), inner, 0.0)
        s.stat[1, side] = jnp.broadcast_to(jnp.sum(kept, 1, keepdims=True), (keys, 128))
    s.dq[...] = jnp.zeros_like(s.dq)

    def wide(block):
        return jnp.concatenate([block] * (tile // 128), 1)

    def back_tile(side, region, at_q, at_k, masked):
        scores = right_transposed(s.q_low[side, at_q, :], key_block(region, at_k))
        probs = jnp.exp2(scores * factor - wide(s.stat[0, side, at_q, :]))
        if masked:
            probs = jnp.where(masks[region], probs, 0.0)
        prob_grad = right_transposed(s.g_low[side, at_q, :], value_block(region, at_k))
        score_grad = (probs * (prob_grad - wide(s.stat[1, side, at_q, :]))).astype(BF16)
        head = slice(side * 64, side * 64 + 64)
        s.dq[side, at_q, :] += dot(score_grad, key_block(region, at_k))
        return dot(s.q_t[head, at_q], score_grad), dot(s.g_t[head, at_q], probs.astype(BF16))

    def attend_back(index):
        at = span(index)
        early = [(0, 0, k, k == index) for k in range(index, n_tiles)]
        early += [(1, 0, k, False) for k in range(n_tiles)]
        late_pairs = [(1, 1, k, k == index) for k in range(index + 1)]
        grads = []
        for pairs in (early, late_pairs):
            both = [
                back_tile(side, region, span(k), at, masked) for side, region, k, masked in pairs
            ]
            grads.append([sum(parts) for parts in zip(*both)])
        for third, scale in ((1, scaling), (2, 1.0)):
            rows_t = jnp.concatenate([grads[0][third - 1], grads[1][third - 1]], 0)
            s.stage[pl.ds(index * per_tile, per_tile), third] = (
                (rows_t.T * scale).astype(BF16).reshape(per_tile, half, 128)
            )
        for step in range(per_tile):
            swap_one(*kv_back, index * per_tile + order_in(step))

    gather_relay(bg_at, s.bg_sent, s.bg_got)
    attend_back(0)
    attend_back(3)
    grad_of_fc()
    attend_back(2)
    gather_forward(bg_at, s.bg_sent, s.bg_got)
    attend_back(1)
    out = jnp.where(low_all, s.dq[0], swap(s.dq[1])) * scaling
    s.stage[:, 0] = out.astype(BF16).reshape(groups, half, 128)
    for step in range(4):
        for head in range(4):
            swap_one(*q_back, order(step) * 4 + order_in(head))
    spread_start(sum_fc)
    gather_start(n1_at, s.n1_sent, s.n1_got)
    grad_of_out()
    spread_on(sum_proj)

    swap_wait(*kv_back)
    gather_relay(n1_at, s.n1_sent, s.n1_got)
    swap_wait(*q_back)
    for pair in range(HEADS // 2):
        for third in range(3):
            block = unpack_pair(
                s.back[2 * pair, third].astype(F32), s.back[2 * pair + 1, third].astype(F32)
            ).astype(BF16)
            s.qg_out[pair, :, third * 128 : third * 128 + 128] = block
            columns = slice(third * width + pair * 128, third * width + pair * 128 + 128)
            s.qg[:, columns] = block
    deal_start(*qg_move)
    gather_forward(n1_at, s.n1_sent, s.n1_got)
    s.sums[4:5, :] = jnp.sum(s.qg[:, :width].astype(F32), 0, keepdims=True)
    s.sums[5:6, :] = jnp.sum(s.qg[:, 2 * width :].astype(F32), 0, keepdims=True)

    def project_back(index, _):
        s.acc_d[:, part(index, 256)] = right_transposed(s.qg[...], s.w_qkv[part(index, 256), :])
        return 0

    lax.fori_loop(0, width // 256, project_back, 0)
    normal, inverse = norm_parts(x_ref[...].astype(F32))
    step_grad, gain_grad, shift_grad = norm_grads(s.acc_d[...], normal, inverse, vec_row(0))
    s.sums[0:1, :] = gain_grad[None]
    s.sums[1:2, :] = shift_grad[None]
    gx_ref[...] = s.res_grad[...] + step_grad
    hand_out(1).start()

    lanes_of_layer = width // layers
    for index in range(layers):
        columns = slice(index * lanes_of_layer, (index + 1) * lanes_of_layer)
        s.sums_out[index, 0:8, :] = s.sums[0:8, columns]
        for quarter in range(layers):
            columns = slice(quarter * lanes_of_layer, (quarter + 1) * lanes_of_layer)
            s.sums_out[index, 8 + quarter : 9 + quarter, :] = s.sums[8 + index : 9 + index, columns]
    for step in range(1, layers):
        target = (layer + step) % layers
        remote(
            s.sums_out.at[target],
            s.sums_in.at[step - 1],
            s.low_sent.at[0],
            s.low_got.at[0],
            (target * PLANE + place, core),
        ).start()

    def low_copy(step):
        return remote(
            s.sums_all.at[member],
            s.sums_all.at[member],
            s.low_sent.at[1],
            s.low_got.at[1],
            at_member((member + step) % members),
        )

    spread_on(sum_fc)
    gather_finish(n1_at, s.n1_sent, s.n1_got)
    deal_wait(*qg_move)
    def qkv_product(index):
        return dot(
            s.n1_t[part(index, fc_rows), :], s.qg_all[...].reshape(tokens, 3 * share)
        )

    for slot, index in enumerate((across, beside)):
        sum_qkv[0](slot)[...] = qkv_product(index).astype(BF16)
        spread_copy(sum_qkv, slot, beside).start()
    qkv_next[...] = qkv_product(beyond)
    qkv_own[...] = qkv_product(layer)

    def pair_sum(move, slot, own, into):
        settle(move[1](slot), s.sum_got.at[2 * move[2] + slot])
        both = own[...] + move[1](slot)[...].astype(F32)
        s.qkv_x[pl.ds(into, members)] = both.astype(BF16).reshape(members, -1, 3 * share)

    spread_on(sum_out)
    pair_sum(sum_qkv, 0, qkv_next, members)
    for index in range(members):
        remote(
            s.qkv_x.at[members + index],
            s.qkv_y.at[members + member],
            s.deal_sent.at[3],
            s.deal_got.at[3],
            (beyond * PLANE + index // 2, index % 2),
        ).start()
    settle(s.sums_in, s.low_got.at[0])
    s.sums_all[member] = s.sums_out[layer] + s.sums_in[0] + s.sums_in[1] + s.sums_in[2]
    for step in range(1, members):
        low_copy(step).start()
    collect(sum_proj, gproj_ref)
    hand_out(5).start()
    collect(sum_fc, fc_own)
    s.fc_x[...] = fc_own[...].astype(BF16).reshape(s.fc_x.shape)
    deal_start(*fx_move)
    collect(sum_out, gout_ref)
    hand_out(3).start()
    settle(s.sums_all.at[pl.ds(0, members - 1)], s.low_got.at[1])
    total = s.sums_all[0]
    for slot in range(1, members):
        total = total + s.sums_all[slot]
    s.sums[:, :lanes_of_layer] = total
    pair_sum(sum_qkv, 1, qkv_own, 0)
    deal_start(*qx_move)
    gvec_ref[...] = jnp.zeros_like(gvec_ref)
    block = s.sums[0:8, part(member // 4, 128)]
    gvec_ref[0:8, :] = pltpu.roll(block, (128 - (member % 4) * 32) % 128, 1)
    block = s.sums[8:16, part(member % 2, 128)]
    chosen = lax.broadcasted_iota(jnp.int32, block.shape, 0) == member // 2
    gvec_ref[8:9, :] = jnp.sum(jnp.where(chosen, block, 0.0), 0, keepdims=True)
    deal_wait(*fx_move)
    for slot in range(members):
        for quarter in range(quarters):
            start = quarter * width + slot * piece
            gfc_ref[:, start : start + piece] = s.fc_y[
                slot, :, quarter * piece : quarter * piece + piece
            ].astype(F32)
    hand_out(4).start()
    deal_wait(*qx_move)
    for slot in range(members):
        for third in range(3):
            start = third * width + slot * 128
            columns = slice(third * 128, third * 128 + 128)
            gqkv_ref[:, start : start + 128] = s.qkv_y[slot, :, columns].astype(
                F32
            ) + s.qkv_y[members + slot, :, columns].astype(F32)

    hand_out(2).start()
    settle(s.sums_in, s.low_sent.at[0])
    settle(s.sums_all.at[pl.ds(0, members - 1)], s.low_sent.at[1])
    settle(peer_rows(s.w_qkv, wq_hbm), s.w_sent.at[0])
    for index in range(3):
        big_piece(index).wait_send()
    vec_copy.wait_send()
    for move in (o_move, g_move, kv_back, q_back):
        swap_drain(*move)
    for move in (att_move, qg_move, fx_move):
        deal_drain(*move)
    settle(s.qkv_x.at[pl.ds(0, 2 * members - 1)], s.deal_sent.at[3])
    for where, sent, got in (
        (cot_at, s.cot_sent, s.cot_got),
        (n1_at, s.n1_sent, s.n1_got),
        (n2_at, s.n2_sent, s.n2_got),
        (bg_at, s.bg_sent, s.bg_got),
    ):
        gather_drain(where, sent, got)
    for move in (sum_proj, sum_fc, sum_out):
        spread_drain(move)
    settle(sum_qkv[0](0, 2), s.sum_sent.at[3])
    for index in range(6):
        hand_out(index).wait()


def hand_over(*refs):
    for source, target in zip(refs[:6], refs[7:13]):
        target[...] = source[...]
    for index, low in enumerate(refs[13:]):
        low[...] = refs[6][index : index + 1, : low.shape[1]]


def fused_layer(
    block_input,
    w_qkv,
    w_out,
    w_fc,
    w_proj,
    ln1_gain,
    ln1_bias,
    ln2_gain,
    ln2_bias,
    bias_q,
    bias_v,
    bias_out,
    bias_fc,
    bias_proj,
    cotangent,
):
    width = block_input.shape[4]
    rows = 2 * block_input.shape[3]
    ff = w_fc.shape[1]
    groups = lax.axis_size("ctx")
    shards = 2 * groups
    small = (ln1_gain, ln1_bias, ln2_gain, ln2_bias, bias_q, bias_v, bias_out, bias_proj, bias_fc)
    shapes = layer_shapes(rows, width, ff, groups)
    names = tuple(shapes) + tuple(SEMAPHORES)
    scratch = [pltpu.VMEM(shape, kind) for shape, kind in shapes.values()]
    scratch += [pltpu.SemaphoreType.DMA((count,)) for count in SEMAPHORES.values()]
    in_vmem = pl.BlockSpec(memory_space=pltpu.VMEM)
    in_hbm = pl.BlockSpec(memory_space=pl.ANY)
    outs = pl.pallas_call(
        partial(layer_kernel, names),
        out_shape=(
            jax.ShapeDtypeStruct((rows, width), BF16),
            jax.ShapeDtypeStruct((rows, width), F32),
            jax.ShapeDtypeStruct((width // shards, 3 * width), F32),
            jax.ShapeDtypeStruct((width // shards, width), F32),
            jax.ShapeDtypeStruct((width // shards, ff), F32),
            jax.ShapeDtypeStruct((ff // shards, width), F32),
            jax.ShapeDtypeStruct((16, 128), F32),
        ),
        in_specs=[in_vmem] * 2 + [in_hbm] * 4 + [in_vmem] * 9,
        out_specs=(in_hbm,) * 6 + (in_vmem,),
        scratch_shapes=scratch,
        compiler_params=pltpu.CompilerParams(
            collective_id=0, has_side_effects=True, vmem_limit_bytes=VMEM_BYTES
        ),
        cost_estimate=pl.CostEstimate(
            flops=14 * 10**9, bytes_accessed=30 * 10**6, transcendentals=5 * 10**6
        ),
    )(
        block_input.reshape(rows, width),
        cotangent.reshape(rows, width),
        w_qkv,
        w_out,
        w_fc,
        w_proj,
        *small,
    )
    piece = width // shards
    wide = ff // shards

    def block_of(array):
        return pl.BlockSpec((array.shape[0] // HAND_STEPS, array.shape[1]), lambda i: (i, 0))

    results = pl.pallas_call(
        hand_over,
        out_shape=tuple(jax.ShapeDtypeStruct(out.shape, out.dtype) for out in outs[:6])
        + (jax.ShapeDtypeStruct((1, piece), F32),) * 8
        + (jax.ShapeDtypeStruct((1, wide), F32),),
        grid=(HAND_STEPS,),
        in_specs=[block_of(out) for out in outs[:6]] + [in_vmem],
        out_specs=tuple(block_of(out) for out in outs[:6]) + (in_vmem,) * 9,
    )(*outs)
    block_output, input_grad, grad_qkv, grad_out, grad_fc, grad_proj = results[:6]
    lows = [result.reshape(-1) for result in results[6:]]
    return (
        block_output.reshape(block_input.shape),
        input_grad.reshape(block_input.shape),
        grad_qkv,
        grad_out,
        grad_fc,
        grad_proj,
        *lows[:7],
        lows[8],
        lows[7],
    )


def on_device(*arrays):
    width, ff = arrays[0].shape[4], arrays[3].shape[1]
    fits = (
        lax.axis_size("ctx") == HEADS
        and lax.axis_size("fsdp") == 2
        and arrays[0].shape[:4] == (1, 1, 2, 64)
        and (width, ff) == (1024, 4096)
    )
    return fused_layer(*arrays) if fits else general_layer(*arrays)


def solution(mesh):
    placed = (
        P("fsdp", "ctx", None, None, None),
        P("fsdp", None),
        P("fsdp", None),
        P("fsdp", None),
        P("fsdp", None),
        P("fsdp"),
        P("fsdp"),
        P("fsdp"),
        P("fsdp"),
        P("fsdp"),
        P("fsdp"),
        P("fsdp"),
        P("fsdp"),
        P("fsdp"),
        P("fsdp", "ctx", None, None, None),
    )
    return jax.shard_map(
        on_device,
        mesh=mesh,
        in_specs=placed,
        out_specs=(
            P("fsdp", "ctx", None, None, None),
            P("fsdp", "ctx", None, None, None),
            P(("ctx", "fsdp"), None),
            P(("ctx", "fsdp"), None),
            P(("ctx", "fsdp"), None),
            P(("ctx", "fsdp"), None),
            P(("ctx", "fsdp")),
            P(("ctx", "fsdp")),
            P(("ctx", "fsdp")),
            P(("ctx", "fsdp")),
            P(("ctx", "fsdp")),
            P(("ctx", "fsdp")),
            P(("ctx", "fsdp")),
            P(("ctx", "fsdp")),
            P(("ctx", "fsdp")),
        ),
        check_vma=False,
    )
```

```python
from functools import partial
from types import SimpleNamespace

import jax
import jax.numpy as jnp
from jax import lax
from jax.experimental import pallas as pl
from jax.experimental.pallas import tpu as pltpu
from jax.sharding import PartitionSpec as P

HEADS = 16
VMEM_BYTES = 127 * 2**19


def norm_parts(values):
    average = jnp.mean(values, -1, keepdims=True)
    centered = values - average
    variance = jnp.mean(centered * centered, -1, keepdims=True)
    inverse = lax.rsqrt(variance + 1e-05)
    return (centered * inverse, inverse)


def norm_grads(upstream, normalized, inverse, gain):
    scaled = upstream * gain
    inner_part = (
        scaled
        - jnp.mean(scaled, -1, keepdims=True)
        - normalized * jnp.mean(scaled * normalized, -1, keepdims=True)
    )
    return (inverse * inner_part, jnp.sum(upstream * normalized, 0), jnp.sum(upstream, 0))


def rows_product(left, right):
    return lax.dot_general(
        left, right, (((0,), (0,)), ((), ())), preferred_element_type=jnp.float32
    )


def right_transposed(left, weight):
    return lax.dot_general(
        left, weight, (((1,), (1,)), ((), ())), preferred_element_type=jnp.float32
    )


def split_heads(matrix):
    return matrix.reshape(matrix.shape[0], HEADS, -1)


def head_scores(queries, keys, allowed, scaling):
    scores = (
        jnp.einsum(
            "qhd,khd->hqk",
            split_heads(queries),
            split_heads(keys),
            preferred_element_type=jnp.float32,
        )
        * scaling
    )
    return jnp.where(allowed[None], scores, -1e30)


def general_layer(
    block_input,
    w_qkv,
    w_out,
    w_fc,
    w_proj,
    ln1_gain,
    ln1_bias,
    ln2_gain,
    ln2_bias,
    bias_q,
    bias_v,
    bias_out,
    bias_fc,
    bias_proj,
    cotangent,
):
    seq_count = block_input.shape[0]
    blk_rows = block_input.shape[3]
    width = block_input.shape[4]
    seq_rows = 2 * blk_rows
    row_count = seq_count * seq_rows
    groups = lax.axis_size("ctx")
    member = lax.axis_index("ctx")
    head_size = width // HEADS
    scaling = head_size ** (-0.5)
    full_rows = groups * seq_rows
    gathered = (
        lax.all_gather(w_qkv, "fsdp", axis=0, tiled=True),
        lax.all_gather(w_out, "fsdp", axis=0, tiled=True),
        lax.all_gather(w_fc, "fsdp", axis=0, tiled=True),
        lax.all_gather(w_proj, "fsdp", axis=0, tiled=True),
        lax.all_gather(ln1_gain, "fsdp", axis=0, tiled=True),
        lax.all_gather(ln1_bias, "fsdp", axis=0, tiled=True),
        lax.all_gather(ln2_gain, "fsdp", axis=0, tiled=True),
        lax.all_gather(ln2_bias, "fsdp", axis=0, tiled=True),
        lax.all_gather(bias_q, "fsdp", axis=0, tiled=True),
        lax.all_gather(bias_v, "fsdp", axis=0, tiled=True),
        lax.all_gather(bias_out, "fsdp", axis=0, tiled=True),
        lax.all_gather(bias_fc, "fsdp", axis=0, tiled=True),
        lax.all_gather(bias_proj, "fsdp", axis=0, tiled=True),
    )
    weight_qkv, weight_out, weight_fc, weight_proj = (
        gathered[0],
        gathered[1],
        gathered[2],
        gathered[3],
    )
    vectors = [piece.astype(jnp.float32) for piece in gathered[4:]]
    (
        gain_one,
        shift_one,
        gain_two,
        shift_two,
        query_bias,
        value_bias,
        out_bias,
        fc_bias,
        proj_bias,
    ) = vectors
    local_index = jnp.arange(seq_rows)
    own_block = jnp.where(local_index // blk_rows == 0, member, 2 * groups - 1 - member)
    own_pos = own_block * blk_rows + local_index % blk_rows
    every_index = jnp.arange(full_rows)
    every_owner = every_index // seq_rows
    every_block = jnp.where(
        every_index // blk_rows % 2 == 0, every_owner, 2 * groups - 1 - every_owner
    )
    every_pos = every_block * blk_rows + every_index % blk_rows
    allowed = every_pos[None, :] <= own_pos[:, None]
    inputs = block_input.reshape(row_count, width).astype(jnp.float32)
    normal_one, inverse_one = norm_parts(inputs)
    normed_one = (normal_one * gain_one + shift_one).astype(jnp.bfloat16)
    bias_all = jnp.concatenate([query_bias, jnp.zeros_like(query_bias), value_bias])
    projected = (
        jnp.dot(normed_one, weight_qkv, preferred_element_type=jnp.float32) + bias_all
    ).astype(jnp.bfloat16)
    queries = projected[:, :width]
    keys = projected[:, width : 2 * width]
    values = projected[:, 2 * width :]
    key_all = lax.all_gather(keys, "ctx", axis=0, tiled=True)
    value_all = lax.all_gather(values, "ctx", axis=0, tiled=True)
    scores = head_scores(queries, key_all, allowed, scaling)
    row_top = jnp.max(scores, -1, keepdims=True)
    log_sum = row_top + jnp.log(jnp.sum(jnp.exp(scores - row_top), -1, keepdims=True))
    probs_low = jnp.exp(scores - log_sum).astype(jnp.bfloat16)
    mixed = jnp.einsum(
        "hqk,khd->qhd", probs_low, split_heads(value_all), preferred_element_type=jnp.float32
    )
    mixed_rows = mixed.reshape(seq_rows, width)
    attended = mixed_rows.astype(jnp.bfloat16)
    residual = inputs + jnp.dot(attended, weight_out, preferred_element_type=jnp.float32) + out_bias
    normal_two, inverse_two = norm_parts(residual)
    normed_two = (normal_two * gain_two + shift_two).astype(jnp.bfloat16)
    hidden = jnp.dot(normed_two, weight_fc, preferred_element_type=jnp.float32) + fc_bias
    activated, gelu_pullback = jax.vjp(partial(jax.nn.gelu, approximate=True), hidden)
    activated_low = activated.astype(jnp.bfloat16)
    result = (
        residual
        + jnp.dot(activated_low, weight_proj, preferred_element_type=jnp.float32)
        + proj_bias
    )
    block_output = result.astype(jnp.bfloat16).reshape(block_input.shape)
    weight_qkv, weight_out, weight_fc, weight_proj, gain_low_one, gain_low_two = (
        lax.all_gather(w_qkv, "fsdp", axis=0, tiled=True),
        lax.all_gather(w_out, "fsdp", axis=0, tiled=True),
        lax.all_gather(w_fc, "fsdp", axis=0, tiled=True),
        lax.all_gather(w_proj, "fsdp", axis=0, tiled=True),
        lax.all_gather(ln1_gain, "fsdp", axis=0, tiled=True),
        lax.all_gather(ln2_gain, "fsdp", axis=0, tiled=True),
    )
    gain_one = gain_low_one.astype(jnp.float32)
    gain_two = gain_low_two.astype(jnp.float32)
    out_grad_low = cotangent.reshape(row_count, width)
    upstream = out_grad_low.astype(jnp.float32)
    grad_proj = rows_product(activated_low, out_grad_low)
    grad_proj_bias = jnp.sum(upstream, 0)
    hidden_grad = gelu_pullback(right_transposed(out_grad_low, weight_proj))[0].astype(jnp.bfloat16)
    grad_fc = rows_product(normed_two, hidden_grad)
    grad_fc_bias = jnp.sum(hidden_grad.astype(jnp.float32), 0)
    residual_part, grad_gain_two, grad_shift_two = norm_grads(
        right_transposed(hidden_grad, weight_fc), normal_two, inverse_two, gain_two
    )
    residual_grad = upstream + residual_part
    branch_grad = residual_grad.astype(jnp.bfloat16)
    grad_out = rows_product(attended, branch_grad)
    grad_out_bias = jnp.sum(branch_grad.astype(jnp.float32), 0)
    attended_grad = right_transposed(branch_grad, weight_out).astype(jnp.bfloat16)
    key_all = lax.all_gather(keys, "ctx", axis=0, tiled=True)
    value_all = lax.all_gather(values, "ctx", axis=0, tiled=True)
    scores = head_scores(queries, key_all, allowed, scaling)
    probs = jnp.exp(scores - log_sum)
    prob_grad = jnp.einsum(
        "qhd,khd->hqk",
        split_heads(attended_grad),
        split_heads(value_all),
        preferred_element_type=jnp.float32,
    )
    inner_sum = jnp.sum(probs * prob_grad, -1, keepdims=True)
    score_grad = (probs * (prob_grad - inner_sum)).astype(jnp.bfloat16)
    query_part = (
        jnp.einsum(
            "hqk,khd->qhd", score_grad, split_heads(key_all), preferred_element_type=jnp.float32
        )
        * scaling
    )
    query_grads = query_part.reshape(seq_rows, width)
    probs_low = probs.astype(jnp.bfloat16)
    query_heads = split_heads(queries)
    grad_heads = split_heads(attended_grad)

    def key_terms(
        start,
        count,
        score_grad=score_grad,
        probs_low=probs_low,
        query_heads=query_heads,
        grad_heads=grad_heads,
    ):
        key_part = (
            jnp.einsum("hqk,qhd->khd", score_grad, query_heads, preferred_element_type=jnp.float32)
            * scaling
        )
        value_part = jnp.einsum(
            "hqk,qhd->khd", probs_low, grad_heads, preferred_element_type=jnp.float32
        )
        return jnp.concatenate(
            [key_part.reshape(count, width), value_part.reshape(count, width)], 1
        )

    own_terms = lax.psum_scatter(
        key_terms(jnp.int32(0), lax.axis_size("ctx") * seq_rows),
        "ctx",
        scatter_dimension=0,
        tiled=True,
    )
    key_grads = own_terms[:, :width]
    value_grads = own_terms[:, width:]
    qkv_grad = jnp.concatenate([query_grads, key_grads, value_grads], 1).astype(jnp.bfloat16)
    grad_qkv = rows_product(normed_one, qkv_grad)
    qkv_sums = jnp.sum(qkv_grad.astype(jnp.float32), 0)
    grad_query_bias = qkv_sums[:width]
    grad_value_bias = qkv_sums[2 * width :]
    input_part, grad_gain_one, grad_shift_one = norm_grads(
        right_transposed(qkv_grad, weight_qkv), normal_one, inverse_one, gain_one
    )
    input_grad = (residual_grad + input_part).reshape(block_input.shape)
    sharded = (
        lax.psum_scatter(grad_qkv, ("ctx", "fsdp"), scatter_dimension=0, tiled=True),
        lax.psum_scatter(grad_out, ("ctx", "fsdp"), scatter_dimension=0, tiled=True),
        lax.psum_scatter(grad_fc, ("ctx", "fsdp"), scatter_dimension=0, tiled=True),
        lax.psum_scatter(grad_proj, ("ctx", "fsdp"), scatter_dimension=0, tiled=True),
        lax.psum_scatter(grad_gain_one, ("ctx", "fsdp"), scatter_dimension=0, tiled=True),
        lax.psum_scatter(grad_shift_one, ("ctx", "fsdp"), scatter_dimension=0, tiled=True),
        lax.psum_scatter(grad_gain_two, ("ctx", "fsdp"), scatter_dimension=0, tiled=True),
        lax.psum_scatter(grad_shift_two, ("ctx", "fsdp"), scatter_dimension=0, tiled=True),
        lax.psum_scatter(grad_query_bias, ("ctx", "fsdp"), scatter_dimension=0, tiled=True),
        lax.psum_scatter(grad_value_bias, ("ctx", "fsdp"), scatter_dimension=0, tiled=True),
        lax.psum_scatter(grad_out_bias, ("ctx", "fsdp"), scatter_dimension=0, tiled=True),
        lax.psum_scatter(grad_fc_bias, ("ctx", "fsdp"), scatter_dimension=0, tiled=True),
        lax.psum_scatter(grad_proj_bias, ("ctx", "fsdp"), scatter_dimension=0, tiled=True),
    )
    return (
        block_output,
        input_grad,
        sharded[0],
        sharded[1],
        sharded[2],
        sharded[3],
        sharded[4],
        sharded[5],
        sharded[6],
        sharded[7],
        sharded[8],
        sharded[9],
        sharded[10],
        sharded[11],
        sharded[12],
    )


MESH = pl.DeviceIdType.MESH
HAND_STEPS = 2
BF16, F32 = jnp.bfloat16, jnp.float32
PLANE = 4
NEG = -1e30


def remote(src, dst, sent, received, device):
    return pltpu.make_async_remote_copy(
        src_ref=src,
        dst_ref=dst,
        send_sem=sent,
        recv_sem=received,
        device_id=device,
        device_id_type=MESH,
    )


def dot(left, right):
    return jnp.dot(left, right, preferred_element_type=F32)


def low_lanes(rows):
    return lax.broadcasted_iota(jnp.int32, (rows, 128), 1) < 64


def swap(block):
    return pltpu.roll(block, 64, 1)


def pack_pair(pair):
    half = pair.shape[0] // 2
    low = low_lanes(half)
    top, bottom = pair[:half], pair[half:]
    return jnp.where(low, top, swap(bottom)), jnp.where(low, swap(top), bottom)


def unpack_pair(even, odd):
    low = low_lanes(even.shape[0])
    return jnp.concatenate(
        [jnp.where(low, even, swap(odd)), jnp.where(low, swap(even), odd)], 0
    )


def part(index, size):
    return pl.ds(pl.multiple_of(index * size, size), size)


def layer_shapes(rows, width, ff, groups):
    members = 2 * PLANE
    layers = groups // PLANE
    tokens = members * rows
    half = rows // 2
    keys = groups * half
    share = width // members
    return dict(
        w_qkv=((width, 3 * width), BF16),
        w_out=((width, width), BF16),
        w_fc=((width, ff), BF16),
        w_proj=((ff, width), BF16),
        vec=((2, 16, width // 2), F32),
        row=((8, width), F32),
        cot_all=((members, rows, width), BF16),
        n1=((rows, width), BF16),
        n1_t=((width, tokens), BF16),
        stage=((groups, 3, half, 128), BF16),
        qkv=((3, keys, 128), BF16),
        kv_roll=((2, keys, 128), BF16),
        q_low=((2, keys, 128), BF16),
        g_low=((2, keys, 128), BF16),
        q_t=((128, keys), BF16),
        g_t=((128, keys), BF16),
        stat=((2, 2, keys, 128), F32),
        mixed=((keys, 128), F32),
        scores=((256, 9 * 256), F32),
        dq=((2, keys, 128), F32),
        o_out=((groups, half, 128), BF16),
        o_in=((groups, half, 128), BF16),
        att=((rows, width), BF16),
        att_t=((layers, members, width // members // layers, rows), BF16),
        att_all=((layers, width // members // layers, tokens), BF16),
        res=((rows, width), F32),
        n2=((rows, width), BF16),
        n2_t=((width, tokens), BF16),
        fc_t=((ff // members, width), BF16),
        bias_t=((ff // members, 128), F32),
        proj_own=((ff // members, width), BF16),
        proj_in=((3 * (ff // members // layers), width), BF16),
        act_all=((ff // members, tokens), BF16),
        hg_all=((ff // members, tokens), BF16),
        upstream=((members, rows, ff // members), F32),
        acc_o=((rows, width), F32),
        acc_d=((rows, width), F32),
        res_grad=((rows, width), F32),
        bg_all=((members, rows, width), BF16),
        g_out=((groups, half, 128), BF16),
        g_in=((keys, 128), BF16),
        back=((groups, 3, half, 128), BF16),
        qg=((rows, 3 * width), BF16),
        qg_out=((members, rows, 3 * share), BF16),
        qg_all=((members, rows, 3 * share), BF16),
        fc_x=((members, width // layers // members, ff // members), BF16),
        fc_y=((members, width // layers // members, ff // members), BF16),
        qkv_x=((2 * members, width // layers // members, 3 * share), BF16),
        qkv_y=((2 * members, width // layers // members, 3 * share), BF16),
        out_y=((rows, width), BF16),
        out_gx=((rows, width), F32),
        out_gqkv=((width // members // layers, 3 * width), F32),
        out_gout=((width // members // layers, width), F32),
        out_gfc=((width // members // layers, ff), F32),
        out_gproj=((ff // members // layers, width), F32),
        sums=((16, width), F32),
        sums_out=((layers, 16, width // layers), F32),
        sums_in=((3, 16, width // layers), F32),
        sums_all=((members, 16, width // layers), F32),
    )


SEMAPHORES = dict(
    local=4,
    out_sem=6,
    w_sent=4,
    w_got=7,
    vec_sent=1,
    vec_got=1,
    swap_sent=5,
    swap_got=5,
    cot_sent=1,
    cot_got=5,
    n1_sent=1,
    n1_got=5,
    n2_sent=1,
    n2_got=5,
    bg_sent=1,
    bg_got=5,
    deal_sent=4,
    deal_got=4,
    sum_sent=4,
    sum_got=8,
    low_sent=2,
    low_got=2,
)


def settle(ref, semaphore):
    pltpu.make_async_copy(ref, ref, semaphore).wait()


def layer_kernel(names, *refs):
    x_ref, cot_ref, wq_hbm, wo_hbm, wf_hbm, wp_hbm = refs[:6]
    small = refs[6:15]
    finals, gvec_ref = refs[15:21], refs[21]
    s = SimpleNamespace(**dict(zip(names, refs[22:])))
    held = (s.out_y, s.out_gx, s.out_gqkv, s.out_gout, s.out_gfc, s.out_gproj)
    y_ref, gx_ref, gqkv_ref, gout_ref, gfc_ref, gproj_ref = held

    def hand_out(index):
        return pltpu.make_async_copy(held[index], finals[index], s.out_sem.at[index])

    rows, width = x_ref.shape
    ff = s.w_fc.shape[1]
    half = rows // 2
    groups = s.stage.shape[0]
    members = 2 * PLANE
    layers = groups // PLANE
    tokens = members * rows
    keys = groups * half
    chunk = ff // members
    share = width // members
    scaling = float(width // HEADS) ** (-0.5)
    factor = scaling * 1.4426950408889634
    me = lax.axis_index("ctx")
    core = lax.axis_index("fsdp")
    other = 1 - core
    layer, place = me // PLANE, me % PLANE
    member = place * 2 + core
    twin = (me, other)

    barrier = pltpu.get_barrier_semaphore()
    for step in range(1, groups):
        pl.semaphore_signal(
            barrier, inc=1, device_id=((me + step) % groups, core), device_id_type=MESH
        )
    for step in range(PLANE):
        pl.semaphore_signal(
            barrier,
            inc=1,
            device_id=(layer * PLANE + (place + step) % PLANE, other),
            device_id_type=MESH,
        )
    pl.semaphore_wait(barrier, groups - 1 + PLANE)

    def at_member(index):
        return (layer * PLANE + index // 2, index % 2)

    def top_rows(ref, source):
        count = source.shape[0]
        return ref.at[pl.ds(pl.multiple_of(core * count, count), count)]

    def peer_rows(ref, source):
        count = source.shape[0]
        return ref.at[pl.ds(pl.multiple_of(other * count, count), count)]


    def order(step):
        return (layer + 2 + step) % 4

    def order_in(step):
        return (place + 1 + step) % 4

    pltpu.make_async_copy(wq_hbm, top_rows(s.w_qkv, wq_hbm), s.local.at[0]).start()

    def qkv_piece(step, third):
        columns = part(third * 4 + order(step), 256)
        return remote(
            wq_hbm.at[:, columns],
            top_rows(s.w_qkv, wq_hbm).at[:, columns],
            s.w_sent.at[0],
            s.w_got.at[step],
            twin,
        )

    at = 0
    for vector in small:
        for start in range(0, vector.shape[0], width // 2):
            line = vector[start : start + width // 2].astype(F32)
            s.vec[core, at : at + 1, :] = line.reshape(1, width // 2)
            at += 1
    s.vec[core, at:, :] = jnp.zeros((16 - at, width // 2), F32)
    vec_copy = remote(s.vec.at[core], s.vec.at[core], s.vec_sent.at[0], s.vec_got.at[0], twin)
    vec_copy.start()
    for step in range(4):
        for third in range(3):
            qkv_piece(step, third).start()
    big = ((wp_hbm, s.w_proj), (wo_hbm, s.w_out), (wf_hbm, s.w_fc))

    def big_piece(index):
        source, target = big[index]
        return remote(
            source, top_rows(target, source), s.w_sent.at[1 + index], s.w_got.at[4 + index], twin
        )

    def big_local(index):
        source, target = big[index]
        return pltpu.make_async_copy(source, top_rows(target, source), s.local.at[1 + index])

    def gather_copy(where, sent, got, slot, index, device):
        return remote(where(slot), where(slot), sent.at[0], got.at[index], device)

    near_x = place + 1 - 2 * (place % 2)
    near_y = (place + 2) % PLANE
    diagonal = (near_x + 2) % PLANE

    def gather_start(where, sent, got):
        for peer in (near_x, near_y):
            gather_copy(where, sent, got, member, place, (layer * PLANE + peer, core)).start()
        gather_copy(where, sent, got, member, PLANE, twin).start()

    def gather_relay(where, sent, got):
        for peer, onward, lower in ((near_x, near_y, 0), (near_y, near_x, 1)):
            slot = peer * 2 + core
            settle(where(slot), got.at[peer])
            size = where(slot).shape[0] // 2
            half_block = where(slot).at[pl.ds(lower * size, size)]
            remote(
                half_block, half_block, sent.at[0], got.at[peer], (layer * PLANE + onward, core)
            ).start()
            gather_copy(where, sent, got, slot, PLANE, twin).start()

    def gather_forward(where, sent, got):
        slot = diagonal * 2 + core
        settle(where(slot), got.at[diagonal])
        gather_copy(where, sent, got, slot, PLANE, twin).start()

    def gather_finish(where, sent, got):
        settle(where(0, PLANE), got.at[PLANE])

    def gather_drain(where, sent, got):
        settle(where(0, 2 * PLANE - 1), sent.at[0])

    def cot_at(slot, count=None):
        return s.cot_all.at[slot if count is None else pl.ds(slot, count)]

    def bg_at(slot, count=None):
        return s.bg_all.at[slot if count is None else pl.ds(slot, count)]

    def columns_at(ref, slot, count):
        return ref.at[:, part(slot, rows) if count is None else pl.ds(slot * rows, count * rows)]

    def n1_at(slot, count=None):
        return columns_at(s.n1_t, slot, count)

    def n2_at(slot, count=None):
        return columns_at(s.n2_t, slot, count)

    def deal_copy(source, target, number, index):
        return remote(
            source(index),
            target(member),
            s.deal_sent.at[number],
            s.deal_got.at[number],
            at_member(index),
        )

    def deal_own(source, target, number):
        return pltpu.make_async_copy(source(member), target(member), s.deal_got.at[number])

    def deal_start(source, target, number):
        for step in range(1, members):
            deal_copy(source, target, number, (member + step) % members).start()
        deal_own(source, target, number).start()

    def deal_wait(source, target, number):
        settle(target(None), s.deal_got.at[number])

    def deal_drain(source, target, number):
        settle(source(None), s.deal_sent.at[number])

    def seven(index):
        return pl.ds(0, members - 1) if index is None else index

    def whole(index):
        return slice(None) if index is None else index

    def lanes(index):
        return slice(None) if index is None else part(index, rows)

    def swap_one(source, target, number, index):
        @pl.when(index == me)
        def _():
            pltpu.make_async_copy(source(index), target(me), s.swap_got.at[number]).start()

        @pl.when(index != me)
        def _():
            remote(
                source(index),
                target(me),
                s.swap_sent.at[number],
                s.swap_got.at[number],
                (index, core),
            ).start()

    def swap_wait(source, target, number):
        settle(target(None), s.swap_got.at[number])

    def swap_drain(source, target, number):
        settle(source(None), s.swap_sent.at[number])

    def others(index):
        return pl.ds(0, groups - 1) if index is None else index

    def block(index):
        return slice(None) if index is None else part(index, half)

    qkv_move = (lambda h: s.stage.at[others(h)], lambda i: s.qkv.at[:, block(i)], 0)
    o_move = (lambda h: s.o_out.at[others(h)], lambda h: s.o_in.at[whole(h)], 1)
    g_move = (lambda h: s.g_out.at[others(h)], lambda i: s.g_in.at[block(i)], 2)
    kv_back = (
        lambda h: s.stage.at[others(h), pl.ds(1, 2)],
        lambda h: s.back.at[whole(h), pl.ds(1, 2)],
        3,
    )
    q_back = (lambda h: s.stage.at[others(h), 0], lambda h: s.back.at[whole(h), 0], 4)
    att_move = (lambda g: s.att_t.at[:, seven(g)], lambda g: s.att_all.at[:, :, lanes(g)], 0)
    qg_move = (lambda g: s.qg_out.at[seven(g)], lambda g: s.qg_all.at[whole(g)], 1)
    fx_move = (lambda g: s.fc_x.at[seven(g)], lambda g: s.fc_y.at[whole(g)], 2)
    qx_move = (lambda g: s.qkv_x.at[g], lambda g: s.qkv_y.at[whole(g)], 3)

    def vec_row(index):
        return jnp.concatenate([s.vec[0, index : index + 1, :], s.vec[1, index : index + 1, :]], 1)

    s.cot_all[member] = cot_ref[...]
    inputs = x_ref[...].astype(F32)
    normal, _ = norm_parts(inputs)
    settle(s.vec.at[other], s.vec_got.at[0])
    s.row[0:1, :] = vec_row(4)
    s.row[1:2, :] = vec_row(5)
    for quarter in range(4):
        at = 8 + quarter % 2 * 2
        s.row[4 + quarter : 5 + quarter, :] = jnp.concatenate(
            [s.vec[quarter // 2, at : at + 1, :], s.vec[quarter // 2, at + 1 : at + 2, :]], 1
        )
    normed = (normal * vec_row(0) + vec_row(1)).astype(BF16)
    s.n1[...] = normed
    pltpu.make_async_copy(wq_hbm, top_rows(s.w_qkv, wq_hbm), s.local.at[0]).wait()

    for step in range(4):
        four = order(step)
        settle(peer_rows(s.w_qkv, wq_hbm).at[:, pl.ds(0, 768)], s.w_got.at[step])
        for third in range(3):
            columns = part(third * 4 + four, 256)
            product = dot(s.n1[...], s.w_qkv[:, columns])
            if third == 0:
                product = product + s.row[0:1, part(four, 256)]
            if third == 2:
                product = product + s.row[1:2, part(four, 256)]
            for pair in range(2):
                even, odd = pack_pair(product[:, pair * 128 : pair * 128 + 128])
                s.stage[four * 4 + 2 * pair, third] = even.astype(BF16)
                s.stage[four * 4 + 2 * pair + 1, third] = odd.astype(BF16)
        for head in range(4):
            swap_one(*qkv_move, four * 4 + order_in(head))
    gather_start(cot_at, s.cot_sent, s.cot_got)
    for index in range(3):
        big_piece(index).start()
        big_local(index).start()

    s.n1_t[:, part(member, rows)] = s.n1[...].astype(F32).T.astype(BF16)
    settle(peer_rows(s.w_proj, wp_hbm), s.w_got.at[4])
    big_local(0).wait()

    def send_back(index, _):
        s.upstream[index] = right_transposed(cot_ref[...], s.w_proj[part(index, chunk), :])
        return 0

    lax.fori_loop(0, members, send_back, 0)

    swap_wait(*qkv_move)
    gather_relay(cot_at, s.cot_sent, s.cot_got)
    low_all = low_lanes(keys)
    query = s.qkv[0].astype(F32)
    s.q_low[0] = jnp.where(low_all, query, 0.0).astype(BF16)
    s.q_low[1] = jnp.where(low_all, swap(query), 0.0).astype(BF16)
    s.kv_roll[0] = swap(s.qkv[1].astype(F32)).astype(BF16)
    s.kv_roll[1] = swap(s.qkv[2].astype(F32)).astype(BF16)

    tile = 256
    per_tile = tile // half
    low_tile = low_lanes(tile)
    row_at = lax.broadcasted_iota(jnp.int32, (tile, tile), 0)
    col_at = lax.broadcasted_iota(jnp.int32, (tile, tile), 1)

    def late(index):
        return index + (per_tile - 1 - 2 * (index // half)) * half

    masks = (col_at <= row_at, late(col_at) <= late(row_at))

    def key_block(region, at):
        return s.qkv[1, at, :] if region == 0 else s.kv_roll[0, at, :]

    def value_block(region, at):
        return s.qkv[2, at, :] if region == 0 else s.kv_roll[1, at, :]

    n_tiles = keys // tile

    def span(start, count=1):
        return slice(start * tile, (start + count) * tile)

    def score_block(queries, region, first, count, column, masked):
        scores = right_transposed(queries, key_block(region, span(first, count)))
        if masked:
            scores = jnp.where(masks[region], scores, NEG)
        s.scores[:, span(column, count)] = scores
        return scores

    def fold(values, combine):
        out = values[:, :128]
        for start in range(128, values.shape[1], 128):
            out = combine(out, values[:, start : start + 128])
        return out

    def softmax_rows(side, blocks, at):
        queries = s.q_low[side, at, :]
        top = None
        for block in blocks:
            high = fold(score_block(queries, *block), jnp.maximum)
            top = high if top is None else jnp.maximum(top, high)
        top = jnp.max(top, 1, keepdims=True) * factor
        total, mix = None, None
        for region, first, count, column, _ in blocks:
            probs = jnp.exp2(s.scores[:, span(column, count)] * factor - top)
            folded = fold(probs, jnp.add)
            total = folded if total is None else total + folded
            more = dot(probs.astype(BF16), value_block(region, span(first, count)))
            mix = more if mix is None else mix + more
        total = jnp.sum(total, 1, keepdims=True)
        s.stat[0, side, at, :] = jnp.broadcast_to(top + jnp.log2(total), (tile, 128))
        return mix / total

    def attend(index):
        at = span(index)
        early = [(0, index, 1, 0, True)]
        if index:
            early.append((0, 0, index, 1, False))
        late_blocks = [(1, index, 1, index + 1, True)]
        if index + 1 < n_tiles:
            late_blocks.append((1, index + 1, n_tiles - 1 - index, index + 2, False))
        late_blocks.append((0, 0, n_tiles, n_tiles + 1, False))
        one = softmax_rows(0, early, at)
        two = softmax_rows(1, late_blocks, at)
        out = jnp.where(low_tile, one, swap(two))
        s.mixed[at, :] = out
        s.o_out[pl.ds(index * per_tile, per_tile)] = out.astype(BF16).reshape(per_tile, half, 128)
        for step in range(per_tile):
            swap_one(*o_move, index * per_tile + order_in(step))

    for index in (0, 3, 2, 1):
        attend(index)
    s.q_t[...] = s.qkv[0].astype(F32).T.astype(BF16)

    for index in range(1, 3):
        settle(peer_rows(big[index][1], big[index][0]), s.w_got.at[4 + index])
        big_local(index).wait()
    quarters = ff // width
    piece = width // members

    curve = 0.7978845608028654

    def features(index):
        return [part(quarter * members + index, piece) for quarter in range(quarters)]

    mine = features(member)
    s.proj_own[...] = jnp.concatenate([s.w_proj[at, :] for at in mine], 0)
    for quarter, at in enumerate(mine):
        into = slice(quarter * piece, quarter * piece + piece)
        s.fc_t[into, :] = s.w_fc[:, at].astype(F32).T.astype(BF16)
        bias = s.row[4 + quarter : 5 + quarter, part(member, piece)]
        s.bias_t[into, :] = jnp.broadcast_to(bias, (128, piece)).T
    swap_wait(*o_move)
    gather_forward(cot_at, s.cot_sent, s.cot_got)
    for pair in range(HEADS // 2):
        columns = slice(pair * 128, pair * 128 + 128)
        s.att[:, columns] = unpack_pair(
            s.o_in[2 * pair].astype(F32), s.o_in[2 * pair + 1].astype(F32)
        ).astype(BF16)
    def project(index, _):
        at = part(index, 256)
        s.acc_d[:, at] = dot(s.att[...], s.w_out[:, at])
        return 0

    lax.fori_loop(0, width // 256, project, 0)
    s.res[...] = x_ref[...].astype(F32) + s.acc_d[...] + vec_row(6)
    normal, _ = norm_parts(s.res[...])
    normed = (normal * vec_row(2) + vec_row(3)).astype(BF16)
    s.n2[...] = normed
    s.n2_t[:, part(member, rows)] = normed.astype(F32).T.astype(BF16)
    gather_start(n2_at, s.n2_sent, s.n2_got)
    s.acc_o[...] = jnp.zeros_like(s.acc_o)
    s.acc_d[...] = jnp.zeros_like(s.acc_d)
    s.sums[...] = jnp.zeros_like(s.sums)


    def gelu_parts(hidden):
        square = hidden * hidden
        bend = jnp.tanh(curve * hidden * (1.0 + 0.044715 * square))
        rise = 0.5 * (1.0 + bend)
        slope = rise + 0.5 * hidden * (1.0 - bend * bend) * (
            curve * (1.0 + 3.0 * 0.044715 * square)
        )
        return hidden * rise, slope

    def feed(index, _):
        at = part(index, 2 * chunk)
        lines = s.vec.at[index // 2]
        first = 8 + index % 2 * 2
        bias = jnp.concatenate(
            [lines[pl.ds(first, 1), :], lines[pl.ds(first + 1, 1), :]], 1
        )
        active, slope = gelu_parts(dot(s.n2[...], s.w_fc[:, at]) + bias)
        active = active.astype(BF16)
        upstream = jnp.concatenate([s.upstream[2 * index], s.upstream[2 * index + 1]], 1)
        grad = (upstream * slope).astype(BF16)
        s.acc_o[...] += dot(active, s.w_proj[at, :])
        s.acc_d[...] += right_transposed(grad, s.w_fc[:, at])
        s.sums[pl.ds(8 + index, 1), :] = jnp.sum(grad.astype(F32), 0, keepdims=True)
        return 0

    lax.fori_loop(0, PLANE - 1, feed, 0)
    gather_relay(n2_at, s.n2_sent, s.n2_got)
    lax.fori_loop(PLANE - 1, PLANE, feed, 0)
    upstream = cot_ref[...].astype(F32)
    normal, inverse = norm_parts(s.res[...])
    step_grad, gain_grad, shift_grad = norm_grads(s.acc_d[...], normal, inverse, vec_row(2))
    s.sums[2:3, :] = gain_grad[None]
    s.sums[3:4, :] = shift_grad[None]
    s.sums[7:8, :] = jnp.sum(upstream, 0, keepdims=True)
    res_grad = upstream + step_grad
    s.res_grad[...] = res_grad
    branch = res_grad.astype(BF16)
    s.bg_all[member] = branch
    s.sums[6:7, :] = jnp.sum(branch.astype(F32), 0, keepdims=True)
    for step in range(4):
        four = order(step)
        product = right_transposed(s.bg_all[member], s.w_out[part(four, 256), :])
        for pair in range(2):
            even, odd = pack_pair(product[:, pair * 128 : pair * 128 + 128])
            s.g_out[four * 4 + 2 * pair] = even.astype(BF16)
            s.g_out[four * 4 + 2 * pair + 1] = odd.astype(BF16)
        for head in range(4):
            swap_one(*g_move, four * 4 + order_in(head))
    y_ref[...] = (s.res[...] + s.acc_o[...] + vec_row(7)).astype(BF16)
    hand_out(0).start()
    gather_start(bg_at, s.bg_sent, s.bg_got)
    s.att_t[...] = s.att[...].astype(F32).T.astype(BF16).reshape(s.att_t.shape)
    deal_start(*att_move)
    gather_forward(n2_at, s.n2_sent, s.n2_got)
    swap_drain(*qkv_move)

    beside = layer + 1 - 2 * (layer % 2)
    beyond = (layer + 2) % layers
    across = (beside + 2) % layers

    def spread_copy(move, slot, target):
        buffer_out, buffer_in, number = move
        return remote(
            buffer_out(slot),
            buffer_in(slot),
            s.sum_sent.at[number],
            s.sum_got.at[2 * number + (slot + 1) // 2],
            (target * PLANE + place, core),
        )

    def spread_prepare(move, product, own_ref):
        for slot, index in enumerate((across, beside, beyond)):
            move[0](slot)[...] = product(index).astype(BF16)
        own_ref[...] = product(layer)

    def spread_start(move):
        for slot in range(2):
            spread_copy(move, slot, beside).start()

    def spread(move, product, own_ref):
        for slot, index in enumerate((across, beside, beyond)):
            move[0](slot)[...] = product(index).astype(BF16)
            if slot < 2:
                spread_copy(move, slot, beside).start()
        own_ref[...] = product(layer)

    def spread_on(move):
        settle(move[1](0), s.sum_got.at[2 * move[2]])
        pair = move[0](2)[...].astype(F32) + move[1](0)[...].astype(F32)
        move[0](2)[...] = pair.astype(BF16)
        spread_copy(move, 2, beyond).start()

    def collect(move, own_ref):
        settle(move[1](1, 2), s.sum_got.at[2 * move[2] + 1])
        own_ref[...] += move[1](1)[...].astype(F32) + move[1](2)[...].astype(F32)

    def spread_drain(move):
        settle(move[0](0, 3), s.sum_sent.at[move[2]])

    proj_rows = ff // members // layers
    out_rows = share // layers
    fc_rows = width // layers

    def rows_of(ref, start, size, columns=slice(None)):
        return lambda slot, count=1: ref.at[pl.ds(start + slot * size, count * size), columns]

    spare = s.upstream.reshape(tokens, chunk)
    fc_own = spare.at[pl.ds(0, fc_rows), :]
    qkv_own = spare.at[pl.ds(fc_rows, fc_rows), pl.ds(0, 3 * share)]
    qkv_next = spare.at[pl.ds(2 * fc_rows, fc_rows), pl.ds(0, 3 * share)]
    sum_proj = (rows_of(s.w_proj, 0, proj_rows), rows_of(s.proj_in, 0, proj_rows), 0)
    sum_out = (rows_of(s.w_proj, 1024, out_rows), rows_of(s.w_proj, 1152, out_rows), 1)
    sum_fc = (
        rows_of(s.w_fc, 0, fc_rows, pl.ds(0, chunk)),
        rows_of(s.w_fc, 0, fc_rows, pl.ds(chunk, chunk)),
        2,
    )
    sum_qkv = (
        rows_of(s.w_fc, 0, fc_rows, pl.ds(2 * chunk, 3 * share)),
        rows_of(s.w_fc, 0, fc_rows, pl.ds(3 * chunk, 3 * share)),
        3,
    )

    part_rows = chunk // 2

    def tokens_of(first, second):
        return [part(first, rows), part(second, rows)]

    def feed_again(first, second):
        here = tokens_of(first, second)
        normed = jnp.concatenate([s.n2_t[:, at] for at in here], 1)
        hidden = dot(s.fc_t[...], normed) + jnp.concatenate([s.bias_t[...]] * 2, 1)
        active, slope = gelu_parts(hidden)
        active = active.astype(BF16)
        for index, at in enumerate(here):
            columns = slice(index * rows, (index + 1) * rows)
            s.act_all[:, at] = active[:, columns]
            s.scores[:, at] = slope[:part_rows, columns]
            s.scores[:, part((first, second)[index] + members, rows)] = slope[part_rows:, columns]

    def back_again(first, second):
        cotangents = jnp.concatenate([s.cot_all[first], s.cot_all[second]], 0)
        upstream = right_transposed(s.proj_own[...], cotangents)
        for index, slot in enumerate((first, second)):
            at = part(slot, rows)
            columns = slice(index * rows, (index + 1) * rows)
            grad = upstream[:part_rows, columns] * s.scores[:, at]
            s.hg_all[:part_rows, at] = grad.astype(BF16)
            grad = upstream[part_rows:, columns] * s.scores[:, part(slot + members, rows)]
            s.hg_all[part_rows:, at] = grad.astype(BF16)

    def grads_of_feed():
        pairs = (
            (member, near_x * 2 + core),
            (near_y * 2 + core, diagonal * 2 + core),
            (place * 2 + other, near_x * 2 + other),
            (near_y * 2 + other, diagonal * 2 + other),
        )
        gather_finish(cot_at, s.cot_sent, s.cot_got)
        for index, pair in enumerate(pairs):
            if index == 2:
                gather_finish(n2_at, s.n2_sent, s.n2_got)
            feed_again(*pair)
        spread(
            sum_proj,
            lambda i: dot(s.act_all[part(i, proj_rows), :], s.cot_all[...].reshape(tokens, width)),
            gproj_ref,
        )
        for pair in pairs:
            back_again(*pair)

    def grad_of_fc():
        spread_prepare(
            sum_fc,
            lambda i: right_transposed(s.n2_t[part(i, fc_rows), :], s.hg_all[...]),
            fc_own,
        )

    def grad_of_out():
        gather_finish(bg_at, s.bg_sent, s.bg_got)
        deal_wait(*att_move)
        spread(
            sum_out,
            lambda i: dot(s.att_all[i], s.bg_all[...].reshape(tokens, width)),
            gout_ref,
        )

    grads_of_feed()
    swap_wait(*g_move)
    upstream = s.g_in[...].astype(F32)
    s.g_low[0] = jnp.where(low_all, upstream, 0.0).astype(BF16)
    s.g_low[1] = jnp.where(low_all, swap(upstream), 0.0).astype(BF16)
    s.g_t[...] = upstream.T.astype(BF16)
    inner = upstream * s.mixed[...]
    for side in range(2):
        kept = jnp.where(low_all == (side == 0), inner, 0.0)
        s.stat[1, side] = jnp.broadcast_to(jnp.sum(kept, 1, keepdims=True), (keys, 128))
    s.dq[...] = jnp.zeros_like(s.dq)

    def wide(block):
        return jnp.concatenate([block] * (tile // 128), 1)

    def back_tile(side, region, at_q, at_k, masked):
        scores = right_transposed(s.q_low[side, at_q, :], key_block(region, at_k))
        probs = jnp.exp2(scores * factor - wide(s.stat[0, side, at_q, :]))
        if masked:
            probs = jnp.where(masks[region], probs, 0.0)
        prob_grad = right_transposed(s.g_low[side, at_q, :], value_block(region, at_k))
        score_grad = (probs * (prob_grad - wide(s.stat[1, side, at_q, :]))).astype(BF16)
        head = slice(side * 64, side * 64 + 64)
        s.dq[side, at_q, :] += dot(score_grad, key_block(region, at_k))
        return dot(s.q_t[head, at_q], score_grad), dot(s.g_t[head, at_q], probs.astype(BF16))

    def attend_back(index):
        at = span(index)
        early = [(0, 0, k, k == index) for k in range(index, n_tiles)]
        early += [(1, 0, k, False) for k in range(n_tiles)]
        late_pairs = [(1, 1, k, k == index) for k in range(index + 1)]
        grads = []
        for pairs in (early, late_pairs):
            both = [
                back_tile(side, region, span(k), at, masked) for side, region, k, masked in pairs
            ]
            grads.append([sum(parts) for parts in zip(*both)])
        for third, scale in ((1, scaling), (2, 1.0)):
            rows_t = jnp.concatenate([grads[0][third - 1], grads[1][third - 1]], 0)
            s.stage[pl.ds(index * per_tile, per_tile), third] = (
                (rows_t.T * scale).astype(BF16).reshape(per_tile, half, 128)
            )
        for step in range(per_tile):
            swap_one(*kv_back, index * per_tile + order_in(step))

    gather_relay(bg_at, s.bg_sent, s.bg_got)
    attend_back(0)
    attend_back(3)
    grad_of_fc()
    attend_back(2)
    gather_forward(bg_at, s.bg_sent, s.bg_got)
    attend_back(1)
    out = jnp.where(low_all, s.dq[0], swap(s.dq[1])) * scaling
    s.stage[:, 0] = out.astype(BF16).reshape(groups, half, 128)
    for step in range(4):
        for head in range(4):
            swap_one(*q_back, order(step) * 4 + order_in(head))
    spread_start(sum_fc)
    gather_start(n1_at, s.n1_sent, s.n1_got)
    grad_of_out()
    spread_on(sum_proj)

    swap_wait(*kv_back)
    gather_relay(n1_at, s.n1_sent, s.n1_got)
    swap_wait(*q_back)
    for pair in range(HEADS // 2):
        for third in range(3):
            block = unpack_pair(
                s.back[2 * pair, third].astype(F32), s.back[2 * pair + 1, third].astype(F32)
            ).astype(BF16)
            s.qg_out[pair, :, third * 128 : third * 128 + 128] = block
            columns = slice(third * width + pair * 128, third * width + pair * 128 + 128)
            s.qg[:, columns] = block
    deal_start(*qg_move)
    gather_forward(n1_at, s.n1_sent, s.n1_got)
    s.sums[4:5, :] = jnp.sum(s.qg[:, :width].astype(F32), 0, keepdims=True)
    s.sums[5:6, :] = jnp.sum(s.qg[:, 2 * width :].astype(F32), 0, keepdims=True)

    def project_back(index, _):
        s.acc_d[:, part(index, 256)] = right_transposed(s.qg[...], s.w_qkv[part(index, 256), :])
        return 0

    lax.fori_loop(0, width // 256, project_back, 0)
    normal, inverse = norm_parts(x_ref[...].astype(F32))
    step_grad, gain_grad, shift_grad = norm_grads(s.acc_d[...], normal, inverse, vec_row(0))
    s.sums[0:1, :] = gain_grad[None]
    s.sums[1:2, :] = shift_grad[None]
    gx_ref[...] = s.res_grad[...] + step_grad
    hand_out(1).start()

    lanes_of_layer = width // layers
    for index in range(layers):
        columns = slice(index * lanes_of_layer, (index + 1) * lanes_of_layer)
        s.sums_out[index, 0:8, :] = s.sums[0:8, columns]
        for quarter in range(layers):
            columns = slice(quarter * lanes_of_layer, (quarter + 1) * lanes_of_layer)
            s.sums_out[index, 8 + quarter : 9 + quarter, :] = s.sums[8 + index : 9 + index, columns]
    for step in range(1, layers):
        target = (layer + step) % layers
        remote(
            s.sums_out.at[target],
            s.sums_in.at[step - 1],
            s.low_sent.at[0],
            s.low_got.at[0],
            (target * PLANE + place, core),
        ).start()

    def low_copy(step):
        return remote(
            s.sums_all.at[member],
            s.sums_all.at[member],
            s.low_sent.at[1],
            s.low_got.at[1],
            at_member((member + step) % members),
        )

    spread_on(sum_fc)
    gather_finish(n1_at, s.n1_sent, s.n1_got)
    deal_wait(*qg_move)
    def qkv_product(index):
        return dot(
            s.n1_t[part(index, fc_rows), :], s.qg_all[...].reshape(tokens, 3 * share)
        )

    for slot, index in enumerate((across, beside)):
        sum_qkv[0](slot)[...] = qkv_product(index).astype(BF16)
        spread_copy(sum_qkv, slot, beside).start()
    qkv_next[...] = qkv_product(beyond)
    qkv_own[...] = qkv_product(layer)

    def pair_sum(move, slot, own, into):
        settle(move[1](slot), s.sum_got.at[2 * move[2] + slot])
        both = own[...] + move[1](slot)[...].astype(F32)
        s.qkv_x[pl.ds(into, members)] = both.astype(BF16).reshape(members, -1, 3 * share)

    spread_on(sum_out)
    pair_sum(sum_qkv, 0, qkv_next, members)
    for index in range(members):
        remote(
            s.qkv_x.at[members + index],
            s.qkv_y.at[members + member],
            s.deal_sent.at[3],
            s.deal_got.at[3],
            (beyond * PLANE + index // 2, index % 2),
        ).start()
    settle(s.sums_in, s.low_got.at[0])
    s.sums_all[member] = s.sums_out[layer] + s.sums_in[0] + s.sums_in[1] + s.sums_in[2]
    for step in range(1, members):
        low_copy(step).start()
    collect(sum_proj, gproj_ref)
    hand_out(5).start()
    collect(sum_fc, fc_own)
    s.fc_x[...] = fc_own[...].astype(BF16).reshape(s.fc_x.shape)
    deal_start(*fx_move)
    collect(sum_out, gout_ref)
    hand_out(3).start()
    settle(s.sums_all.at[pl.ds(0, members - 1)], s.low_got.at[1])
    total = s.sums_all[0]
    for slot in range(1, members):
        total = total + s.sums_all[slot]
    s.sums[:, :lanes_of_layer] = total
    pair_sum(sum_qkv, 1, qkv_own, 0)
    deal_start(*qx_move)
    gvec_ref[...] = jnp.zeros_like(gvec_ref)
    block = s.sums[0:8, part(member // 4, 128)]
    gvec_ref[0:8, :] = pltpu.roll(block, (128 - (member % 4) * 32) % 128, 1)
    block = s.sums[8:16, part(member % 2, 128)]
    chosen = lax.broadcasted_iota(jnp.int32, block.shape, 0) == member // 2
    gvec_ref[8:9, :] = jnp.sum(jnp.where(chosen, block, 0.0), 0, keepdims=True)
    deal_wait(*fx_move)
    for slot in range(members):
        for quarter in range(quarters):
            start = quarter * width + slot * piece
            gfc_ref[:, start : start + piece] = s.fc_y[
                slot, :, quarter * piece : quarter * piece + piece
            ].astype(F32)
    hand_out(4).start()
    deal_wait(*qx_move)
    for slot in range(members):
        for third in range(3):
            start = third * width + slot * 128
            columns = slice(third * 128, third * 128 + 128)
            gqkv_ref[:, start : start + 128] = s.qkv_y[slot, :, columns].astype(
                F32
            ) + s.qkv_y[members + slot, :, columns].astype(F32)

    hand_out(2).start()
    settle(s.sums_in, s.low_sent.at[0])
    settle(s.sums_all.at[pl.ds(0, members - 1)], s.low_sent.at[1])
    settle(peer_rows(s.w_qkv, wq_hbm), s.w_sent.at[0])
    for index in range(3):
        big_piece(index).wait_send()
    vec_copy.wait_send()
    for move in (o_move, g_move, kv_back, q_back):
        swap_drain(*move)
    for move in (att_move, qg_move, fx_move):
        deal_drain(*move)
    settle(s.qkv_x.at[pl.ds(0, 2 * members - 1)], s.deal_sent.at[3])
    for where, sent, got in (
        (cot_at, s.cot_sent, s.cot_got),
        (n1_at, s.n1_sent, s.n1_got),
        (n2_at, s.n2_sent, s.n2_got),
        (bg_at, s.bg_sent, s.bg_got),
    ):
        gather_drain(where, sent, got)
    for move in (sum_proj, sum_fc, sum_out):
        spread_drain(move)
    settle(sum_qkv[0](0, 2), s.sum_sent.at[3])
    for index in range(6):
        hand_out(index).wait()


def hand_over(*refs):
    for source, target in zip(refs[:6], refs[7:13]):
        target[...] = source[...]
    for index, low in enumerate(refs[13:]):
        low[...] = refs[6][index : index + 1, : low.shape[1]]


def fused_layer(
    block_input,
    w_qkv,
    w_out,
    w_fc,
    w_proj,
    ln1_gain,
    ln1_bias,
    ln2_gain,
    ln2_bias,
    bias_q,
    bias_v,
    bias_out,
    bias_fc,
    bias_proj,
    cotangent,
):
    width = block_input.shape[4]
    rows = 2 * block_input.shape[3]
    ff = w_fc.shape[1]
    groups = lax.axis_size("ctx")
    shards = 2 * groups
    small = (ln1_gain, ln1_bias, ln2_gain, ln2_bias, bias_q, bias_v, bias_out, bias_proj, bias_fc)
    shapes = layer_shapes(rows, width, ff, groups)
    names = tuple(shapes) + tuple(SEMAPHORES)
    scratch = [pltpu.VMEM(shape, kind) for shape, kind in shapes.values()]
    scratch += [pltpu.SemaphoreType.DMA((count,)) for count in SEMAPHORES.values()]
    in_vmem = pl.BlockSpec(memory_space=pltpu.VMEM)
    in_hbm = pl.BlockSpec(memory_space=pl.ANY)
    outs = pl.pallas_call(
        partial(layer_kernel, names),
        out_shape=(
            jax.ShapeDtypeStruct((rows, width), BF16),
            jax.ShapeDtypeStruct((rows, width), F32),
            jax.ShapeDtypeStruct((width // shards, 3 * width), F32),
            jax.ShapeDtypeStruct((width // shards, width), F32),
            jax.ShapeDtypeStruct((width // shards, ff), F32),
            jax.ShapeDtypeStruct((ff // shards, width), F32),
            jax.ShapeDtypeStruct((16, 128), F32),
        ),
        in_specs=[in_vmem] * 2 + [in_hbm] * 4 + [in_vmem] * 9,
        out_specs=(in_hbm,) * 6 + (in_vmem,),
        scratch_shapes=scratch,
        compiler_params=pltpu.CompilerParams(
            collective_id=0, has_side_effects=True, vmem_limit_bytes=VMEM_BYTES
        ),
        cost_estimate=pl.CostEstimate(
            flops=14 * 10**9, bytes_accessed=30 * 10**6, transcendentals=5 * 10**6
        ),
    )(
        block_input.reshape(rows, width),
        cotangent.reshape(rows, width),
        w_qkv,
        w_out,
        w_fc,
        w_proj,
        *small,
    )
    piece = width // shards
    wide = ff // shards

    def block_of(array):
        return pl.BlockSpec((array.shape[0] // HAND_STEPS, array.shape[1]), lambda i: (i, 0))

    results = pl.pallas_call(
        hand_over,
        out_shape=tuple(jax.ShapeDtypeStruct(out.shape, out.dtype) for out in outs[:6])
        + (jax.ShapeDtypeStruct((1, piece), F32),) * 8
        + (jax.ShapeDtypeStruct((1, wide), F32),),
        grid=(HAND_STEPS,),
        in_specs=[block_of(out) for out in outs[:6]] + [in_vmem],
        out_specs=tuple(block_of(out) for out in outs[:6]) + (in_vmem,) * 9,
    )(*outs)
    block_output, input_grad, grad_qkv, grad_out, grad_fc, grad_proj = results[:6]
    lows = [result.reshape(-1) for result in results[6:]]
    return (
        block_output.reshape(block_input.shape),
        input_grad.reshape(block_input.shape),
        grad_qkv,
        grad_out,
        grad_fc,
        grad_proj,
        *lows[:7],
        lows[8],
        lows[7],
    )


def on_device(*arrays):
    width, ff = arrays[0].shape[4], arrays[3].shape[1]
    fits = (
        lax.axis_size("ctx") == HEADS
        and lax.axis_size("fsdp") == 2
        and arrays[0].shape[:4] == (1, 1, 2, 64)
        and (width, ff) == (1024, 4096)
    )
    return fused_layer(*arrays) if fits else general_layer(*arrays)


def solution(mesh):
    placed = (
        P("fsdp", "ctx", None, None, None),
        P("fsdp", None),
        P("fsdp", None),
        P("fsdp", None),
        P("fsdp", None),
        P("fsdp"),
        P("fsdp"),
        P("fsdp"),
        P("fsdp"),
        P("fsdp"),
        P("fsdp"),
        P("fsdp"),
        P("fsdp"),
        P("fsdp"),
        P("fsdp", "ctx", None, None, None),
    )
    return jax.shard_map(
        on_device,
        mesh=mesh,
        in_specs=placed,
        out_specs=(
            P("fsdp", "ctx", None, None, None),
            P("fsdp", "ctx", None, None, None),
            P(("ctx", "fsdp"), None),
            P(("ctx", "fsdp"), None),
            P(("ctx", "fsdp"), None),
            P(("ctx", "fsdp"), None),
            P(("ctx", "fsdp")),
            P(("ctx", "fsdp")),
            P(("ctx", "fsdp")),
            P(("ctx", "fsdp")),
            P(("ctx", "fsdp")),
            P(("ctx", "fsdp")),
            P(("ctx", "fsdp")),
            P(("ctx", "fsdp")),
            P(("ctx", "fsdp")),
        ),
        check_vma=False,
    )
```
